32 devices in a mesh: grp: 2 (over y), rep: 16 (over z, x, core).
Axes of the slice: x: 2, y: 2, z: 4, core: 2. Of those that a mesh axis runs over, the one named last changes fastest.
Arguments:
- tokens: bfloat16 [4096, 1280], P(('grp', 'rep')), may hold values from -6 to 6
- doc_ids: int32 [2, 2048], P('grp'), may hold values from 0 to 3, never falling along the last dimension, each value on 1 to 1152 neighbouring positions
- w_query: bfloat16 [1280, 1280], P('grp'), may hold values from -0.15625 to 0.15625
- w_key: bfloat16 [1280, 1280], P('grp'), may hold values from -0.15625 to 0.15625
- w_value: bfloat16 [1280, 1280], P('grp'), may hold values from -0.15625 to 0.15625
- w_out: bfloat16 [1280, 1280], P('grp'), may hold values from -1 to 1
- w_up: bfloat16 [1280, 5120], P('grp'), may hold values from -0.15625 to 0.15625
- w_down: bfloat16 [5120, 1280], P('grp'), may hold values from -0.078125 to 0.078125
- b_query: bfloat16 [1280], P('grp'), may hold values from -3 to 3
- b_value: bfloat16 [1280], P('grp'), may hold values from -3 to 3
- b_out: bfloat16 [1280], P('grp'), may hold values from -2 to 2
- b_up: bfloat16 [5120], P('grp'), may hold values from -3 to 3
- b_down: bfloat16 [1280], P('grp'), may hold values from -2 to 2
- attn_gain: bfloat16 [1280], P('grp'), may hold values from 0.5 to 1.5
- attn_beta: bfloat16 [1280], P('grp'), may hold values from -2 to 2
- ffn_gain: bfloat16 [1280], P('grp'), may hold values from 0.5 to 1.5
- ffn_beta: bfloat16 [1280], P('grp'), may hold values from -2 to 2
- cotangent: bfloat16 [4096, 1280], P(('grp', 'rep')), may hold values from -6 to 6
Outputs:
- output: bfloat16 [4096, 1280], P(('grp', 'rep'))
- grad_input: float32 [4096, 1280], P(('grp', 'rep'))
- grad_w_query: float32 [1280, 1280], P('grp')
- grad_w_key: float32 [1280, 1280], P('grp')
- grad_w_value: float32 [1280, 1280], P('grp')
- grad_w_out: float32 [1280, 1280], P('grp')
- grad_w_up: float32 [1280, 5120], P('grp')
- grad_w_down: float32 [5120, 1280], P('grp')
- grad_b_query: float32 [1280], P('grp')
- grad_b_value: float32 [1280], P('grp')
- grad_b_out: float32 [1280], P('grp')
- grad_b_up: float32 [5120], P('grp')
- grad_b_down: float32 [1280], P('grp')
- grad_attn_gain: float32 [1280], P('grp')
- grad_attn_beta: float32 [1280], P('grp')
- grad_ffn_gain: float32 [1280], P('grp')
- grad_ffn_beta: float32 [1280], P('grp')
The draws below stay inside these ranges and needn't reach their ends.
Inputs may be any that keep to these rules, and one draw needn't show every extreme that they name: `doc_ids`: in each row, document numbers start at 0 and never fall; every document 0 to 3 has 1 to 1152 tokens, and some document has exactly 1152.
All inputs are finite; a program needn't handle non-finite values.
Results may differ from the reference program's by a relative error of at most 0.02.
Values may be sent and summed in bfloat16 or wider, within the bound.
A program may use at most 256 MiB of HBM per device.

```python
import math
import jax
import jax.numpy as jnp
import numpy as np
from jax import lax

D = 1280
HEADS = 20
HEAD_DIM = 64
FF = 5120
ROW = 2048
TOKENS = 4096
DOC_MAX = 1152
DOCS = 4
N_GRP = 2


def steps_of(rng, shape, pieces, least, largest):
    def one(dim, shards_of):
        steps = jax.random.uniform(jax.random.fold_in(jax.random.fold_in(rng, 6), dim), (shards_of,), jnp.float32, least / len(pieces), largest / len(pieces))
        return jnp.repeat(jnp.exp(steps), shape[dim] // shards_of).reshape((-1,) + (1,) * (len(shape) - dim - 1))

    factor_of = one(*pieces[0])
    for cut in pieces[1:]:
        factor_of = factor_of * one(*cut)
    return factor_of


def profile(number_of, total, reach, slope):
    loads = [(1 << 20) // math.isqrt(standing ** slope) + 1 for standing in range(2, number_of + 1)]
    rest, counts = total - reach - (number_of - 1), [1] * (number_of - 1)
    while rest > 0:
        candidates = [i for i in range(number_of - 1) if counts[i] < reach]
        mass, budget = sum([loads[i] for i in candidates]), rest
        for i in candidates:
            extra = min(reach - counts[i], max(1, budget * loads[i] // mass), rest)
            counts[i] = counts[i] + extra
            rest = rest - extra
    return np.array([reach] + counts)


def ragged_sizes(stream_key, number_of, total, reach, slope):
    if number_of == 2:
        one = jax.random.randint(stream_key, (), max(1, total - reach), min(reach, total - 1) + 1)
        return jnp.stack([one, total - one])
    tallies = jnp.asarray(profile(number_of, total, reach, slope), jnp.int32)
    twos = (number_of - 1) // 2
    giver, sink = tallies[1:1 + 2 * twos:2], tallies[2:2 + 2 * twos:2]
    margin = jnp.minimum(giver - 1, reach - sink)
    passed = jax.random.randint(jax.random.fold_in(stream_key, 1), (twos,), 0, 1 << 20) % (margin + 1)
    tallies = tallies.at[1:1 + 2 * twos:2].set(giver - passed).at[2:2 + 2 * twos:2].set(sink + passed)
    return tallies[jax.random.permutation(jax.random.fold_in(stream_key, 2), number_of)]


def bell_draw(stream_key, dims, spread, bound, cuts=(), kind=jnp.bfloat16):
    entries = jax.random.normal(stream_key, dims, jnp.float32) * spread
    if len(cuts) > 0:
        entries = steps_of(stream_key, dims, cuts, -0.22, 0.18) * entries
    return jnp.clip(entries, min=-bound, max=bound).astype(kind)


def setup_inputs(seed: int = 0) -> dict:
    key_of = jax.random.split(jax.random.key(seed), 19)
    tokens = bell_draw(key_of[0], (TOKENS, D), 1.0, 6.0, ((0, 32),))
    doc_ids = jax.vmap(lambda own: jnp.searchsorted(jnp.cumsum(ragged_sizes(own, DOCS, ROW, DOC_MAX, 1)), jnp.arange(ROW), side="right"))(jax.random.split(key_of[1], N_GRP)).reshape((N_GRP, ROW)).astype(jnp.int32)
    w_query = bell_draw(key_of[2], (D, D), D ** -0.5, 0.15625, ((0, 2),))
    w_key = bell_draw(key_of[3], (D, D), D ** -0.5, 0.15625, ((0, 2),))
    w_value = bell_draw(key_of[4], (D, D), D ** -0.5, 0.15625, ((0, 2),))
    w_out = bell_draw(key_of[5], (D, D), (D // 32) ** -0.5, 1.0, ((0, 2),))
    w_up = bell_draw(key_of[6], (D, FF), D ** -0.5, 0.15625, ((0, 2),))
    w_down = bell_draw(key_of[7], (FF, D), FF ** -0.5, 0.078125, ((0, 2),))
    b_query = bell_draw(key_of[8], (D,), 0.5, 3.0, ((0, 2),))
    b_value = bell_draw(key_of[9], (D,), 0.5, 3.0, ((0, 2),))
    b_out = bell_draw(key_of[10], (D,), 0.3, 2.0, ((0, 2),))
    b_up = bell_draw(key_of[11], (FF,), 0.5, 3.0, ((0, 2),))
    b_down = bell_draw(key_of[12], (D,), 0.3, 2.0, ((0, 2),))
    attn_gain = jnp.clip(1.0 + 0.1 * jax.random.normal(key_of[13], (D,), jnp.float32), 0.5, 1.5).astype(jnp.bfloat16)
    attn_beta = bell_draw(key_of[14], (D,), 0.3, 2.0, ((0, 2),))
    ffn_gain = jnp.clip(1.0 + 0.1 * jax.random.normal(key_of[15], (D,), jnp.float32), 0.5, 1.5).astype(jnp.bfloat16)
    ffn_beta = bell_draw(key_of[16], (D,), 0.3, 2.0, ((0, 2),))
    cotangent = bell_draw(key_of[17], (TOKENS, D), 1.0, 6.0, ((0, 32),))
    return {"tokens": tokens, "doc_ids": doc_ids, "w_query": w_query, "w_key": w_key, "w_value": w_value, "w_out": w_out, "w_up": w_up, "w_down": w_down, "b_query": b_query, "b_value": b_value, "b_out": b_out, "b_up": b_up, "b_down": b_down, "attn_gain": attn_gain, "attn_beta": attn_beta, "ffn_gain": ffn_gain, "ffn_beta": ffn_beta, "cotangent": cotangent}


@jax.custom_vjp
def low(v):
    return lax.optimization_barrier(v.astype(jnp.bfloat16)).astype(jnp.float32)

@jax.custom_vjp
def low_back(v):
    return v

def low_keep(v):
    return (low(v), None)

def low_pass(kept, grad):
    return (grad,)

def back_keep(v):
    return (v, None)

def back_low(kept, grad):
    return (low(grad),)
low.defvjp(low_keep, low_pass)
low_back.defvjp(back_keep, back_low)
EPSILON = 1e-05
NEGATIVE = -1e+30
GELU_SCALE = 0.7978845608028654
GELU_CUBIC = 0.044715
HIGHEST = lax.Precision.HIGHEST

def product(left, right):
    return jnp.dot(left, right, precision=HIGHEST, preferred_element_type=jnp.float32)

def both_ways(tensor):
    return low_back(low(tensor))

def normalize(values):
    center = values - lax.optimization_barrier(jnp.mean(values, axis=-1, keepdims=True))
    inverse = lax.rsqrt(lax.optimization_barrier(jnp.mean(center * center, axis=-1, keepdims=True)) + EPSILON)
    return center * inverse

def gelu(inputs):
    return 0.5 * inputs * (1.0 + jnp.tanh(GELU_SCALE * (inputs + GELU_CUBIC * inputs * inputs * inputs)))

def attention(query, keys, values, row_ids):
    length = query.shape[0]
    block = min(512, length)
    scale = HEAD_DIM ** (-0.5)
    key_pad = jnp.concatenate([jnp.zeros((DOC_MAX, D), jnp.float32), keys], axis=0)
    value_pad = jnp.concatenate([jnp.zeros((DOC_MAX, D), jnp.float32), values], axis=0)
    id_pad = jnp.concatenate([jnp.full((DOC_MAX,), -1, jnp.int32), row_ids.astype(jnp.int32)])

    def one_block(start):
        query_block = lax.dynamic_slice_in_dim(query, start, block).reshape(block, HEADS, HEAD_DIM)
        key_block = lax.dynamic_slice_in_dim(key_pad, start, DOC_MAX + block).reshape(DOC_MAX + block, HEADS, HEAD_DIM)
        value_block = lax.dynamic_slice_in_dim(value_pad, start, DOC_MAX + block).reshape(DOC_MAX + block, HEADS, HEAD_DIM)
        key_ids = lax.dynamic_slice_in_dim(id_pad, start, DOC_MAX + block)
        query_ids = lax.dynamic_slice_in_dim(row_ids.astype(jnp.int32), start, block)
        key_pos = start - DOC_MAX + jnp.arange(DOC_MAX + block, dtype=jnp.int32)
        query_pos = start + jnp.arange(block, dtype=jnp.int32)
        allowed = (key_ids[None, :] == query_ids[:, None]) & (key_pos[None, :] <= query_pos[:, None])
        scores = low_back(jnp.einsum('qhd,khd->hqk', query_block, key_block, precision=HIGHEST) * scale)
        masked = jnp.where(allowed[None], scores, NEGATIVE)
        log_total = jax.nn.logsumexp(masked, axis=-1, keepdims=True)
        probs = low(jnp.exp(masked - log_total))
        return jnp.einsum('hqk,khd->qhd', probs, value_block, precision=HIGHEST).reshape(block, D)
    starts = jnp.arange(length // block, dtype=jnp.int32) * block
    return lax.map(jax.checkpoint(one_block), starts).reshape(length, D)

def layer(row_input, params, row_ids):
    w_query, w_key, w_value, w_out, w_up, w_down, b_query, b_value, b_out, b_up, b_down, attn_gain, attn_beta, ffn_gain, ffn_beta = params
    ln_one = low(normalize(row_input) * attn_gain + attn_beta)
    query = both_ways(product(ln_one, w_query) + b_query)
    keys = both_ways(product(ln_one, w_key))
    values = both_ways(product(ln_one, w_value) + b_value)
    attn_low = both_ways(attention(query, keys, values, row_ids))
    hidden = row_input + low_back(product(attn_low, w_out) + b_out)
    ln_two = low(normalize(hidden) * ffn_gain + ffn_beta)
    pre_act = low_back(product(ln_two, w_up) + b_up)
    act_low = low(gelu(pre_act))
    return hidden + low_back(product(act_low, w_down) + b_down)

def reference(tokens, doc_ids, w_query, w_key, w_value, w_out, w_up, w_down, b_query, b_value, b_out, b_up, b_down, attn_gain, attn_beta, ffn_gain, ffn_beta, cotangent):
    params = tuple((item.astype(jnp.float32) for item in (w_query, w_key, w_value, w_out, w_up, w_down, b_query, b_value, b_out, b_up, b_down, attn_gain, attn_beta, ffn_gain, ffn_beta)))
    input_rows = tokens.astype(jnp.float32).reshape(N_GRP, ROW, D)
    back_rows = cotangent.astype(jnp.float32).reshape(N_GRP, ROW, D)

    def row_step(total, inputs):
        row_input, row_back, row_ids = inputs

        def forward(input_value, param_values):
            return layer(input_value, param_values, row_ids)
        row_result, pullback = jax.vjp(forward, row_input, params)
        row_grad, grad_params = pullback(row_back)
        return (jax.tree.map(jnp.add, total, grad_params), (row_result, row_grad))
    zeros = tuple((jnp.zeros_like(item) for item in params))
    total, (results, grad_rows) = lax.scan(row_step, zeros, (input_rows, back_rows, doc_ids))
    output = results.reshape(TOKENS, D).astype(jnp.bfloat16)
    grad_input = grad_rows.reshape(TOKENS, D)
    return (output, grad_input, total[0], total[1], total[2], total[3], total[4], total[5], total[6], total[7], total[8], total[9], total[10], total[11], total[12], total[13], total[14])
```

```python
import jax
import jax.numpy as jnp
from jax import lax
from jax.experimental import pallas as pl
from jax.experimental.pallas import tpu as pltpu
from jax.sharding import PartitionSpec as P

HEADS = 20
HEAD_DIM = 64
PAIRS = 4


EPSILON = 1e-05
NEGATIVE = -1e30
GELU_SCALE = 0.7978845608028654
GELU_CUBIC = 0.044715


def from_behind(array, axis, by):
    length = lax.axis_size(axis)
    pairs = [(i, i + by) for i in range(length) if 0 <= i + by < length]
    return lax.ppermute(array, axis, pairs)


def passed_along(block, axis, distance):
    devices = range(lax.axis_size(axis))
    route = [((i - distance) % len(devices), i) for i in devices]
    return lax.ppermute(block, axis, route)


def norm_rows(values):
    center = values - jnp.mean(values, axis=-1, keepdims=True)
    inverse = lax.rsqrt(jnp.mean(center * center, axis=-1, keepdims=True) + EPSILON)
    return (center * inverse, inverse)


def norm_grad(grad_norm, normed, inverse, gain):
    scaled = grad_norm * gain
    return inverse * (
        scaled
        - jnp.mean(scaled, axis=-1, keepdims=True)
        - normed * jnp.mean(scaled * normed, axis=-1, keepdims=True)
    )


def gelu_pair(inputs):
    inner = jnp.tanh(GELU_SCALE * (inputs + GELU_CUBIC * inputs * inputs * inputs))
    value = 0.5 * inputs * (1.0 + inner)
    slope = 0.5 * (1.0 + inner) + 0.5 * inputs * (1.0 - inner * inner) * GELU_SCALE * (
        1.0 + 3.0 * GELU_CUBIC * inputs * inputs
    )
    return (value, slope)


def matmul(left, right):
    return jnp.dot(left, right, preferred_element_type=jnp.float32)


def matmul_tn(left, right):
    return lax.dot_general(
        left, right, (((0,), (0,)), ((), ())), preferred_element_type=jnp.float32
    )


def matmul_nt(left, right):
    return lax.dot_general(
        left, right, (((1,), (1,)), ((), ())), preferred_element_type=jnp.float32
    )


def shards(
    tokens,
    doc_ids,
    w_query,
    w_key,
    w_value,
    w_out,
    w_up,
    w_down,
    b_query,
    b_value,
    b_out,
    b_up,
    b_down,
    attn_gain,
    attn_beta,
    ffn_gain,
    ffn_beta,
    cotangent,
):
    tok_dev = tokens.shape[0]
    width = tokens.shape[1]
    scale = HEAD_DIM ** (-0.5)
    (
        full_query,
        full_key,
        full_value,
        full_out,
        full_up,
        full_down,
        bias_query,
        bias_value,
        bias_out,
        bias_up,
        bias_down,
        gain_attn,
        beta_attn,
        gain_ffn,
        beta_ffn,
    ) = (
        lax.all_gather(w_query, "grp", axis=0, tiled=True),
        lax.all_gather(w_key, "grp", axis=0, tiled=True),
        lax.all_gather(w_value, "grp", axis=0, tiled=True),
        lax.all_gather(w_out, "grp", axis=0, tiled=True),
        lax.all_gather(w_up, "grp", axis=0, tiled=True),
        lax.all_gather(w_down, "grp", axis=0, tiled=True),
        lax.all_gather(b_query, "grp", axis=0, tiled=True),
        lax.all_gather(b_value, "grp", axis=0, tiled=True),
        lax.all_gather(b_out, "grp", axis=0, tiled=True),
        lax.all_gather(b_up, "grp", axis=0, tiled=True),
        lax.all_gather(b_down, "grp", axis=0, tiled=True),
        lax.all_gather(attn_gain, "grp", axis=0, tiled=True),
        lax.all_gather(attn_beta, "grp", axis=0, tiled=True),
        lax.all_gather(ffn_gain, "grp", axis=0, tiled=True),
        lax.all_gather(ffn_beta, "grp", axis=0, tiled=True),
    )
    rep_index = lax.axis_index("rep")
    pad_front = (2 * PAIRS + 1) * tok_dev
    row_ids = doc_ids[0]
    padded_ids = jnp.concatenate([jnp.full((pad_front,), -1, jnp.int32), row_ids])
    query_pos = rep_index * tok_dev + jnp.arange(tok_dev, dtype=jnp.int32)
    query_doc = lax.dynamic_slice_in_dim(row_ids, rep_index * tok_dev, tok_dev)

    def block_mask(block_index):
        first = (rep_index - 2 * block_index - 1) * tok_dev
        key_pos = first + jnp.arange(2 * tok_dev, dtype=jnp.int32)
        key_doc = lax.dynamic_slice_in_dim(padded_ids, first + pad_front, 2 * tok_dev)
        return (key_doc[None, :] == query_doc[:, None]) & (key_pos[None, :] <= query_pos[:, None])

    xfull = tokens.astype(jnp.float32)
    normed_one, inverse_one = norm_rows(xfull)
    ln_one = (normed_one * gain_attn.astype(jnp.float32) + beta_attn.astype(jnp.float32)).astype(
        jnp.bfloat16
    )
    query = (matmul(ln_one, full_query) + bias_query.astype(jnp.float32)).astype(jnp.bfloat16)
    keys = matmul(ln_one, full_key).astype(jnp.bfloat16)
    values = (matmul(ln_one, full_value) + bias_value.astype(jnp.float32)).astype(jnp.bfloat16)
    query_heads = query.reshape(tok_dev, HEADS, HEAD_DIM)
    earlier = from_behind((keys, values), "rep", 1)
    first_block = (
        jnp.concatenate([earlier[0], keys], axis=0),
        jnp.concatenate([earlier[1], values], axis=0),
    )

    def fetch_pair(block, unused):
        moved = from_behind((block[0], block[1]), "rep", 2)
        return (moved, moved)

    unused_end, following = lax.scan(fetch_pair, first_block, None, length=PAIRS)
    key_blocks = jnp.concatenate([first_block[0][None], following[0]], axis=0)
    value_blocks = jnp.concatenate([first_block[1][None], following[1]], axis=0)
    block_numbers = jnp.arange(PAIRS + 1, dtype=jnp.int32)

    def scores_of(block_keys, block_index):
        raw = (
            jnp.einsum(
                "qhd,khd->hqk",
                query_heads,
                block_keys.reshape(-1, HEADS, HEAD_DIM),
                preferred_element_type=jnp.float32,
            )
            * scale
        )
        return jnp.where(block_mask(block_index)[None], raw, NEGATIVE)

    def max_step(state, inputs):
        run_max, run_sum = state
        block_keys, block_index = inputs
        scores = scores_of(block_keys, block_index)
        new_max = jnp.maximum(run_max, jnp.max(scores, axis=-1))
        run_sum = run_sum * jnp.exp(run_max - new_max) + jnp.sum(
            jnp.exp(scores - new_max[..., None]), axis=-1
        )
        return ((new_max, run_sum), None)

    start_state = (
        jnp.full((HEADS, tok_dev), NEGATIVE, jnp.float32),
        jnp.zeros((HEADS, tok_dev), jnp.float32),
    )
    (top_score, total_exp), unused_max = lax.scan(
        max_step, start_state, (key_blocks, block_numbers)
    )
    log_total = top_score + jnp.log(total_exp)

    def value_step(total, inputs):
        block_keys, block_values, block_index = inputs
        probs = jnp.exp(scores_of(block_keys, block_index) - log_total[..., None]).astype(
            jnp.bfloat16
        )
        return (
            total
            + jnp.einsum(
                "hqk,khd->qhd",
                probs,
                block_values.reshape(-1, HEADS, HEAD_DIM),
                preferred_element_type=jnp.float32,
            ),
            None,
        )

    attn, unused_value = lax.scan(
        value_step,
        jnp.zeros((tok_dev, HEADS, HEAD_DIM), jnp.float32),
        (key_blocks, value_blocks, block_numbers),
    )
    attn_low = attn.reshape(tok_dev, width).astype(jnp.bfloat16)
    hidden = xfull + matmul(attn_low, full_out) + bias_out.astype(jnp.float32)
    normed_two, inverse_two = norm_rows(hidden)
    ln_two = (normed_two * gain_ffn.astype(jnp.float32) + beta_ffn.astype(jnp.float32)).astype(
        jnp.bfloat16
    )
    pre_act = matmul(ln_two, full_up) + bias_up.astype(jnp.float32)
    act_value, act_slope = gelu_pair(pre_act)
    act_low = act_value.astype(jnp.bfloat16)
    result = hidden + matmul(act_low, full_down) + bias_down.astype(jnp.float32)
    output = result.astype(jnp.bfloat16)
    (
        back_query,
        back_key,
        back_value,
        back_out,
        back_up,
        back_down,
        back_gain_attn,
        back_gain_ffn,
    ) = (
        lax.all_gather(w_query, "grp", axis=0, tiled=True),
        lax.all_gather(w_key, "grp", axis=0, tiled=True),
        lax.all_gather(w_value, "grp", axis=0, tiled=True),
        lax.all_gather(w_out, "grp", axis=0, tiled=True),
        lax.all_gather(w_up, "grp", axis=0, tiled=True),
        lax.all_gather(w_down, "grp", axis=0, tiled=True),
        lax.all_gather(attn_gain, "grp", axis=0, tiled=True),
        lax.all_gather(ffn_gain, "grp", axis=0, tiled=True),
    )
    grad_res = cotangent.astype(jnp.float32)
    grad_w_down = matmul_tn(act_low, cotangent)
    grad_b_down = jnp.sum(grad_res, axis=0)
    grad_pre = (matmul_nt(cotangent, back_down) * act_slope).astype(jnp.bfloat16)
    grad_w_up = matmul_tn(ln_two, grad_pre)
    grad_b_up = jnp.sum(grad_pre.astype(jnp.float32), axis=0)
    grad_ln_two = matmul_nt(grad_pre, back_up)
    grad_ffn_gain = jnp.sum(grad_ln_two * normed_two, axis=0)
    grad_ffn_beta = jnp.sum(grad_ln_two, axis=0)
    grad_hidden = grad_res + norm_grad(
        grad_ln_two, normed_two, inverse_two, back_gain_ffn.astype(jnp.float32)
    )
    grad_mix = grad_hidden.astype(jnp.bfloat16)
    grad_w_out = matmul_tn(attn_low, grad_mix)
    grad_b_out = jnp.sum(grad_mix.astype(jnp.float32), axis=0)
    grad_heads = (
        matmul_nt(grad_mix, back_out).astype(jnp.bfloat16).reshape(tok_dev, HEADS, HEAD_DIM)
    )
    delta = jnp.sum(grad_heads.astype(jnp.float32) * attn, axis=-1).T

    def block_grads(block_keys, block_values, block_index):
        probs = jnp.exp(scores_of(block_keys, block_index) - log_total[..., None])
        key_heads = block_keys.reshape(-1, HEADS, HEAD_DIM)
        value_heads = block_values.reshape(-1, HEADS, HEAD_DIM)
        grad_probs = jnp.einsum(
            "qhd,khd->hqk", grad_heads, value_heads, preferred_element_type=jnp.float32
        )
        grad_scores = (probs * (grad_probs - delta[..., None])).astype(jnp.bfloat16)
        part_query = (
            jnp.einsum("hqk,khd->qhd", grad_scores, key_heads, preferred_element_type=jnp.float32)
            * scale
        )
        part_key = (
            jnp.einsum("hqk,qhd->khd", grad_scores, query_heads, preferred_element_type=jnp.float32)
            * scale
        )
        part_value = jnp.einsum(
            "hqk,qhd->khd",
            probs.astype(jnp.bfloat16),
            grad_heads,
            preferred_element_type=jnp.float32,
        )
        return (part_query, part_key, part_value)

    again = from_behind((keys, values), "rep", 1)
    back_block = (
        jnp.concatenate([again[0], keys], axis=0),
        jnp.concatenate([again[1], values], axis=0),
    )
    query_sum, key_acc, value_acc = block_grads(back_block[0], back_block[1], 0)

    def travel_step(carry, inputs):
        query_total, key_total, value_total, block_keys, block_values = carry
        block_index, kept_keys, kept_values = inputs
        block_keys, block_values = from_behind((block_keys, block_values), "rep", 2)
        key_total, value_total = (
            passed_along(key_total.astype(jnp.bfloat16), "rep", 2).astype(key_total.dtype),
            passed_along(value_total.astype(jnp.bfloat16), "rep", 2).astype(value_total.dtype),
        )
        part_query, part_key, part_value = block_grads(block_keys, block_values, block_index)
        return (
            (
                query_total + part_query,
                key_total + part_key,
                value_total + part_value,
                block_keys,
                block_values,
            ),
            None,
        )

    carry_end, unused_travel = lax.scan(
        travel_step,
        (query_sum, key_acc, value_acc, back_block[0], back_block[1]),
        (block_numbers[1:], key_blocks[1:], value_blocks[1:]),
    )
    query_sum, key_acc, value_acc = (carry_end[0], carry_end[1], carry_end[2])
    from_next = (
        passed_along(key_acc[:tok_dev].astype(jnp.bfloat16), "rep", -1).astype(jnp.float32),
        passed_along(value_acc[:tok_dev].astype(jnp.bfloat16), "rep", -1).astype(jnp.float32),
    )
    joined_key = key_acc[tok_dev:] + from_next[0]
    joined_value = value_acc[tok_dev:] + from_next[1]
    returned = (
        passed_along(joined_key.astype(jnp.bfloat16), "rep", -2 * PAIRS).astype(joined_key.dtype),
        passed_along(joined_value.astype(jnp.bfloat16), "rep", -2 * PAIRS).astype(
            joined_value.dtype
        ),
    )
    grad_query_low = query_sum.reshape(tok_dev, width).astype(jnp.bfloat16)
    grad_key_low = returned[0].reshape(tok_dev, width).astype(jnp.bfloat16)
    grad_value_low = returned[1].reshape(tok_dev, width).astype(jnp.bfloat16)
    grad_w_query = matmul_tn(ln_one, grad_query_low)
    grad_b_query = jnp.sum(grad_query_low.astype(jnp.float32), axis=0)
    grad_w_key = matmul_tn(ln_one, grad_key_low)
    grad_w_value = matmul_tn(ln_one, grad_value_low)
    grad_b_value = jnp.sum(grad_value_low.astype(jnp.float32), axis=0)
    grad_ln_one = (
        matmul_nt(grad_query_low, back_query)
        + matmul_nt(grad_key_low, back_key)
        + matmul_nt(grad_value_low, back_value)
    )
    grad_attn_gain = jnp.sum(grad_ln_one * normed_one, axis=0)
    grad_attn_beta = jnp.sum(grad_ln_one, axis=0)
    grad_input = grad_hidden + norm_grad(
        grad_ln_one, normed_one, inverse_one, back_gain_attn.astype(jnp.float32)
    )
    shares = (
        lax.psum_scatter(
            grad_w_query.astype(jnp.bfloat16), "grp", scatter_dimension=0, tiled=True
        ).astype(jnp.float32),
        lax.psum_scatter(
            grad_w_key.astype(jnp.bfloat16), "grp", scatter_dimension=0, tiled=True
        ).astype(jnp.float32),
        lax.psum_scatter(
            grad_w_value.astype(jnp.bfloat16), "grp", scatter_dimension=0, tiled=True
        ).astype(jnp.float32),
        lax.psum_scatter(
            grad_w_out.astype(jnp.bfloat16), "grp", scatter_dimension=0, tiled=True
        ).astype(jnp.float32),
        lax.psum_scatter(
            grad_w_up.astype(jnp.bfloat16), "grp", scatter_dimension=0, tiled=True
        ).astype(jnp.float32),
        lax.psum_scatter(
            grad_w_down.astype(jnp.bfloat16), "grp", scatter_dimension=0, tiled=True
        ).astype(jnp.float32),
        lax.psum_scatter(
            grad_b_query.astype(jnp.bfloat16), "grp", scatter_dimension=0, tiled=True
        ).astype(jnp.float32),
        lax.psum_scatter(
            grad_b_value.astype(jnp.bfloat16), "grp", scatter_dimension=0, tiled=True
        ).astype(jnp.float32),
        lax.psum_scatter(
            grad_b_out.astype(jnp.bfloat16), "grp", scatter_dimension=0, tiled=True
        ).astype(jnp.float32),
        lax.psum_scatter(
            grad_b_up.astype(jnp.bfloat16), "grp", scatter_dimension=0, tiled=True
        ).astype(jnp.float32),
        lax.psum_scatter(
            grad_b_down.astype(jnp.bfloat16), "grp", scatter_dimension=0, tiled=True
        ).astype(jnp.float32),
        lax.psum_scatter(
            grad_attn_gain.astype(jnp.bfloat16), "grp", scatter_dimension=0, tiled=True
        ).astype(jnp.float32),
        lax.psum_scatter(
            grad_attn_beta.astype(jnp.bfloat16), "grp", scatter_dimension=0, tiled=True
        ).astype(jnp.float32),
        lax.psum_scatter(
            grad_ffn_gain.astype(jnp.bfloat16), "grp", scatter_dimension=0, tiled=True
        ).astype(jnp.float32),
        lax.psum_scatter(
            grad_ffn_beta.astype(jnp.bfloat16), "grp", scatter_dimension=0, tiled=True
        ).astype(jnp.float32),
    )
    totals = (
        lax.psum(shares[0].astype(jnp.bfloat16), "rep").astype(jnp.float32),
        lax.psum(shares[1].astype(jnp.bfloat16), "rep").astype(jnp.float32),
        lax.psum(shares[2].astype(jnp.bfloat16), "rep").astype(jnp.float32),
        lax.psum(shares[3].astype(jnp.bfloat16), "rep").astype(jnp.float32),
        lax.psum(shares[4].astype(jnp.bfloat16), "rep").astype(jnp.float32),
        lax.psum(shares[5].astype(jnp.bfloat16), "rep").astype(jnp.float32),
        lax.psum(shares[6].astype(jnp.bfloat16), "rep").astype(jnp.float32),
        lax.psum(shares[7].astype(jnp.bfloat16), "rep").astype(jnp.float32),
        lax.psum(shares[8].astype(jnp.bfloat16), "rep").astype(jnp.float32),
        lax.psum(shares[9].astype(jnp.bfloat16), "rep").astype(jnp.float32),
        lax.psum(shares[10].astype(jnp.bfloat16), "rep").astype(jnp.float32),
        lax.psum(shares[11].astype(jnp.bfloat16), "rep").astype(jnp.float32),
        lax.psum(shares[12].astype(jnp.bfloat16), "rep").astype(jnp.float32),
        lax.psum(shares[13].astype(jnp.bfloat16), "rep").astype(jnp.float32),
        lax.psum(shares[14].astype(jnp.bfloat16), "rep").astype(jnp.float32),
    )
    return (
        output,
        grad_input,
        totals[0],
        totals[1],
        totals[2],
        totals[3],
        totals[4],
        totals[5],
        totals[6],
        totals[7],
        totals[8],
        totals[9],
        totals[10],
        totals[11],
        totals[12],
        totals[13],
        totals[14],
    )


def fits_pair(mesh):
    return mesh.shape["grp"] == 2 and mesh.shape["rep"] == 16


REACH = 9
CHUNK = 128
WINDOW = (REACH + 1) * CHUNK
HALF_LANES = 64


def iota(shape, dim):
    return lax.broadcasted_iota(jnp.int32, shape, dim)


def head_half(block, which):
    first = iota(block.shape, 1) < HALF_LANES
    return jnp.where(first if which == 0 else jnp.logical_not(first), block, jnp.zeros_like(block))


def join_halves(first, second):
    return jnp.where(iota(first.shape, 1) < HALF_LANES, first, second)


def attn_forward(q_ref, k_ref, v_ref, qid_ref, kid_ref, out_ref, lse_ref):
    span = k_ref.shape[1]
    query = q_ref[0] * jnp.bfloat16(HEAD_DIM**-0.5)
    keys, values = k_ref[0], v_ref[0]
    allowed = (qid_ref[0] == kid_ref[0]) & (
        iota((CHUNK, span), 1) <= iota((CHUNK, span), 0) + REACH * CHUNK
    )
    outs, lses = [], []
    for which in range(2):
        scores = jnp.where(allowed, matmul_nt(head_half(query, which), keys), NEGATIVE)
        top = jnp.max(scores, axis=-1, keepdims=True)
        probs = jnp.exp(scores - top)
        total = jnp.sum(probs, axis=-1, keepdims=True)
        outs.append(matmul((probs * (1.0 / total)).astype(jnp.bfloat16), values))
        lses.append(jnp.broadcast_to(top + jnp.log(total), (CHUNK, CHUNK)))
    out_ref[0] = join_halves(*outs)
    lse_ref[0] = join_halves(*lses)


def attn_query_grad(q_ref, k_ref, v_ref, qid_ref, kid_ref, do_ref, out_ref, lse_ref, dq_ref):
    span = k_ref.shape[1]
    query = q_ref[0] * jnp.bfloat16(HEAD_DIM**-0.5)
    keys, values, grad = k_ref[0], v_ref[0], do_ref[0]
    allowed = (qid_ref[0] == kid_ref[0]) & (
        iota((CHUNK, span), 1) <= iota((CHUNK, span), 0) + REACH * CHUNK
    )
    weighed = grad.astype(jnp.float32) * out_ref[0]
    parts = []
    for which in range(2):
        lse = lse_ref[0][:, which * HALF_LANES : which * HALF_LANES + 1]
        delta = jnp.sum(head_half(weighed, which), axis=-1, keepdims=True)
        scores = jnp.where(allowed, matmul_nt(head_half(query, which), keys), NEGATIVE)
        probs = jnp.exp(scores - lse)
        grad_probs = matmul_nt(head_half(grad, which), values)
        grad_scores = (probs * (grad_probs - delta)).astype(jnp.bfloat16)
        parts.append(matmul(grad_scores, keys))
    dq_ref[0] = (join_halves(*parts) * HEAD_DIM**-0.5).astype(jnp.bfloat16)


def attn_key_grad(k_ref, v_ref, q_ref, do_ref, kid_ref, qid_ref, lse_ref, delta_ref, dk_ref, dv_ref):
    span = q_ref.shape[1]
    keys = k_ref[0] * jnp.bfloat16(HEAD_DIM**-0.5)
    values, queries, grads = v_ref[0], q_ref[0], do_ref[0]
    allowed = (kid_ref[0] == qid_ref[0]) & (iota((CHUNK, span), 1) >= iota((CHUNK, span), 0))
    key_parts, value_parts = [], []
    for which in range(2):
        scores = jnp.where(allowed, matmul_nt(head_half(keys, which), queries), NEGATIVE)
        probs = jnp.exp(scores - lse_ref[0, 0, which : which + 1, :])
        value_parts.append(matmul(probs.astype(jnp.bfloat16), grads))
        grad_probs = matmul_nt(head_half(values, which), grads)
        grad_scores = (probs * (grad_probs - delta_ref[0, 0, which : which + 1, :])).astype(
            jnp.bfloat16
        )
        key_parts.append(matmul(grad_scores, queries))
    dk_ref[0] = (join_halves(*key_parts) * HEAD_DIM**-0.5).astype(jnp.bfloat16)
    dv_ref[0] = join_halves(*value_parts).astype(jnp.bfloat16)


def pair_shards(
    tokens,
    doc_ids,
    w_query,
    w_key,
    w_value,
    w_out,
    w_up,
    w_down,
    b_query,
    b_value,
    b_out,
    b_up,
    b_down,
    attn_gain,
    attn_beta,
    ffn_gain,
    ffn_beta,
    cotangent,
):
    f32, bf16 = jnp.float32, jnp.bfloat16
    chunk, width = tokens.shape
    half = width // 2
    row_len = doc_ids.shape[1]
    side = lax.axis_index("grp")
    place = lax.axis_index("rep")

    def swap(array):
        return lax.ppermute(array, "grp", [(0, 1), (1, 0)])

    def cols(array, which, size):
        return lax.dynamic_slice_in_dim(array, which * size, size, axis=array.ndim - 1)

    def both(own, other, axis):
        return jnp.where(
            side == 0,
            jnp.concatenate([own, other], axis=axis),
            jnp.concatenate([other, own], axis=axis),
        )

    small = jnp.concatenate([b_out, b_down, attn_gain, attn_beta, ffn_gain, ffn_beta]).reshape(6, half)
    small = both(small, swap(small), 1).astype(f32)
    bias_out, bias_down, gain_one, beta_one, gain_two, beta_two = [small[i] for i in range(6)]
    ids = jnp.concatenate([doc_ids, swap(doc_ids)], axis=0)
    moved = swap(jnp.concatenate([tokens, cotangent], axis=0))
    x_all = jnp.concatenate([tokens, moved[:chunk]], axis=0).astype(f32)
    cot_all = jnp.concatenate([cotangent, moved[chunk:]], axis=0)
    w_qkv = jnp.concatenate(
        [cols(w, side, half) for w in (w_query, w_key, w_value)], axis=1
    )
    w_qkv_other = swap(
        jnp.concatenate([cols(w, 1 - side, half) for w in (w_query, w_key, w_value)], axis=1)
    )
    ff_half = w_up.shape[1] // 2
    w_up_own = cols(w_up, side, ff_half)
    w_up_other = swap(cols(w_up, 1 - side, ff_half))

    normed_one, inverse_one = norm_rows(x_all)
    ln_one = (normed_one * gain_one + beta_one).astype(bf16)
    ln_one_own, ln_one_other = cols(ln_one, side, half), cols(ln_one, 1 - side, half)
    bias_qkv = jnp.concatenate([b_query.astype(f32), jnp.zeros((half,), f32), b_value.astype(f32)])
    qkv = (matmul(ln_one_own, w_qkv) + matmul(ln_one_other, w_qkv_other) + bias_qkv).astype(bf16)
    qkv = qkv.reshape(2, chunk, 3 * half)
    gathered = lax.all_gather(qkv, "rep", axis=1, tiled=True)
    front = jnp.pad(gathered[:, :, half:], ((0, 0), (REACH * chunk, 0), (0, 0)))
    kv_win = lax.dynamic_slice_in_dim(front, place * chunk, WINDOW, axis=1)
    k_win, v_win = kv_win[:, :, :half], kv_win[:, :, half:]
    q_own, k_own, v_own = qkv[:, :, :half], qkv[:, :, half : 2 * half], qkv[:, :, 2 * half :]
    own_ids = lax.dynamic_slice_in_dim(ids, place * chunk, chunk, axis=1)
    front_ids = jnp.pad(ids, ((0, 0), (REACH * chunk, 0)), constant_values=-1)
    key_ids = lax.dynamic_slice_in_dim(front_ids, place * chunk, WINDOW, axis=1)
    back_ids = jnp.pad(ids, ((0, 0), (0, REACH * chunk)), constant_values=-2)
    query_ids = lax.dynamic_slice_in_dim(back_ids, place * chunk, WINDOW, axis=1)

    pairs = half // CHUNK
    own_spec = pl.BlockSpec((1, CHUNK, CHUNK), lambda r, p: (r, 0, p))
    win_spec = pl.BlockSpec((1, WINDOW, CHUNK), lambda r, p: (r, 0, p))
    col_spec = pl.BlockSpec((1, CHUNK, 1), lambda r, p: (r, 0, 0))
    row_spec = pl.BlockSpec((1, 1, WINDOW), lambda r, p: (r, 0, 0))
    stat_spec = pl.BlockSpec((1, 1, 2, WINDOW), lambda r, p: (r, p, 0, 0))
    own_shape = (2, chunk, half)
    attn, lse = pl.pallas_call(
        attn_forward,
        grid=(2, pairs),
        in_specs=[own_spec, win_spec, win_spec, col_spec, row_spec],
        out_specs=[own_spec, own_spec],
        out_shape=[jax.ShapeDtypeStruct(own_shape, f32)] * 2,
    )(q_own, k_win, v_win, own_ids[:, :, None], key_ids[:, None, :])

    attn_low = attn.reshape(2 * chunk, half).astype(bf16)
    mixed = matmul(attn_low, w_out)
    mixed_other = swap(mixed.astype(bf16)).astype(f32)
    mixed_other = jnp.concatenate([mixed_other[chunk:], mixed_other[:chunk]], axis=0)
    hidden = x_all + mixed + mixed_other + bias_out
    normed_two, inverse_two = norm_rows(hidden)
    ln_two = (normed_two * gain_two + beta_two).astype(bf16)
    ln_two_own, ln_two_other = cols(ln_two, side, half), cols(ln_two, 1 - side, half)
    pre_act = matmul(ln_two_own, w_up_own) + matmul(ln_two_other, w_up_other) + b_up.astype(f32)
    act_value, act_slope = gelu_pair(pre_act)
    act_low = act_value.astype(bf16)
    down = matmul(act_low, w_down)
    down_other = swap(down[chunk:].astype(bf16)).astype(f32)
    output = (hidden[:chunk] + down[:chunk] + down_other + bias_down).astype(bf16)

    grad_res = cot_all.astype(f32)
    grad_w_down = matmul_tn(act_low, cot_all).astype(bf16)
    grad_pre = (matmul_nt(cot_all, w_down) * act_slope).astype(bf16)
    grad_up_keep = matmul_tn(ln_two_own, grad_pre).astype(bf16)
    grad_up_send = matmul_tn(ln_two_other, grad_pre).astype(bf16)
    back_two = both(matmul_nt(grad_pre, w_up_own), matmul_nt(grad_pre, w_up_other), 1)
    back_other = swap(back_two.astype(bf16)).astype(f32)
    grad_ln_two = back_two + jnp.concatenate([back_other[chunk:], back_other[:chunk]], axis=0)
    grad_hidden = grad_res + norm_grad(grad_ln_two, normed_two, inverse_two, gain_two)
    grad_mix = grad_hidden.astype(bf16)
    grad_w_out = matmul_tn(attn_low, grad_mix).astype(bf16)
    grad_heads = matmul_nt(grad_mix, w_out).astype(bf16)

    delta = jnp.sum(
        (grad_heads.astype(f32) * attn.reshape(2 * chunk, half)).reshape(2, chunk, half // HEAD_DIM, HEAD_DIM),
        axis=-1,
    )
    stats = jnp.concatenate(
        [lse.reshape(2, chunk, half // HEAD_DIM, HEAD_DIM)[..., 0], delta], axis=-1
    )
    stats = jnp.swapaxes(stats, 1, 2)
    all_stats = lax.all_gather(stats, "rep", axis=2, tiled=True)
    all_grads = lax.all_gather(grad_heads.reshape(own_shape), "rep", axis=1, tiled=True)
    tail = ((0, 0), (0, REACH * chunk), (0, 0))
    q_win = lax.dynamic_slice_in_dim(jnp.pad(gathered[:, :, :half], tail), place * chunk, WINDOW, axis=1)
    do_win = lax.dynamic_slice_in_dim(jnp.pad(all_grads, tail), place * chunk, WINDOW, axis=1)
    stat_win = lax.dynamic_slice_in_dim(
        jnp.pad(all_stats, ((0, 0), (0, 0), (0, REACH * chunk))), place * chunk, WINDOW, axis=2
    ).reshape(2, 2, pairs, 2, WINDOW)

    grad_query = pl.pallas_call(
        attn_query_grad,
        grid=(2, pairs),
        in_specs=[own_spec, win_spec, win_spec, col_spec, row_spec, own_spec, own_spec, own_spec],
        out_specs=own_spec,
        out_shape=jax.ShapeDtypeStruct(own_shape, bf16),
    )(
        q_own,
        k_win,
        v_win,
        own_ids[:, :, None],
        key_ids[:, None, :],
        grad_heads.reshape(own_shape),
        attn,
        lse,
    )
    grad_key, grad_value = pl.pallas_call(
        attn_key_grad,
        grid=(2, pairs),
        in_specs=[own_spec, own_spec, win_spec, win_spec, col_spec, row_spec, stat_spec, stat_spec],
        out_specs=[own_spec, own_spec],
        out_shape=[jax.ShapeDtypeStruct(own_shape, bf16)] * 2,
    )(
        k_own,
        v_own,
        q_win,
        do_win,
        own_ids[:, :, None],
        query_ids[:, None, :],
        stat_win[:, 0],
        stat_win[:, 1],
    )
    grad_qkv = jnp.concatenate([grad_query, grad_key, grad_value], axis=2).reshape(2 * chunk, 3 * half)
    grad_qkv_keep = matmul_tn(ln_one_own, grad_qkv).astype(bf16)
    grad_qkv_send = matmul_tn(ln_one_other, grad_qkv).astype(bf16)
    back_one = both(matmul_nt(grad_qkv, w_qkv), matmul_nt(grad_qkv, w_qkv_other), 1)
    back_other = swap(back_one.astype(bf16)).astype(f32)
    grad_ln_one = back_one + jnp.concatenate([back_other[chunk:], back_other[:chunk]], axis=0)
    grad_input = grad_hidden + norm_grad(grad_ln_one, normed_one, inverse_one, gain_one)

    def total(array):
        return jnp.sum(array.astype(f32), axis=0)

    qkv_vec = total(grad_qkv)
    vectors = [
        qkv_vec[:half],
        qkv_vec[2 * half :],
        cols(total(grad_mix), side, half),
        total(grad_pre),
        cols(total(grad_res), side, half),
        cols(total(grad_ln_one * normed_one), side, half),
        cols(total(grad_ln_one), side, half),
        cols(total(grad_ln_two * normed_two), side, half),
        cols(total(grad_ln_two), side, half),
    ]
    vec_sum = lax.psum(jnp.concatenate(vectors).astype(bf16), "rep").astype(f32)
    cuts, at = [], 0
    for vector in vectors:
        cuts.append(vec_sum[at : at + vector.shape[0]])
        at += vector.shape[0]

    keep_down, keep_out, keep_up, keep_qkv, send_up, send_qkv = [
        lax.psum_scatter(a, "rep", scatter_dimension=0, tiled=True)
        for a in (grad_w_down, grad_w_out, grad_up_keep, grad_qkv_keep, grad_up_send, grad_qkv_send)
    ]
    other_up, other_qkv = swap(send_up), swap(send_qkv)
    sum_down, sum_out, sum_up, sum_qkv, sum_up_other, sum_qkv_other = [
        lax.all_gather(a, "rep", axis=0, tiled=True).astype(f32)
        for a in (keep_down, keep_out, keep_up, keep_qkv, other_up, other_qkv)
    ]
    three = [
        both(sum_qkv[:, i * half : (i + 1) * half], sum_qkv_other[:, i * half : (i + 1) * half], 1)
        for i in range(3)
    ]
    return (
        output,
        grad_input[:chunk],
        three[0],
        three[1],
        three[2],
        sum_out,
        both(sum_up, sum_up_other, 1),
        sum_down,
        *cuts,
    )


def solution(mesh):
    in_specs = (
        P(("grp", "rep"), None),
        P("grp", None),
        P("grp", None),
        P("grp", None),
        P("grp", None),
        P("grp", None),
        P("grp", None),
        P("grp", None),
        P("grp"),
        P("grp"),
        P("grp"),
        P("grp"),
        P("grp"),
        P("grp"),
        P("grp"),
        P("grp"),
        P("grp"),
        P(("grp", "rep"), None),
    )
    out_specs = (
        P(("grp", "rep"), None),
        P(("grp", "rep"), None),
        P("grp", None),
        P("grp", None),
        P("grp", None),
        P("grp", None),
        P("grp", None),
        P("grp", None),
        P("grp"),
        P("grp"),
        P("grp"),
        P("grp"),
        P("grp"),
        P("grp"),
        P("grp"),
        P("grp"),
        P("grp"),
    )
    plan = pair_shards if fits_pair(mesh) else shards
    return jax.shard_map(plan, mesh=mesh, in_specs=in_specs, out_specs=out_specs, check_vma=False)
```

```python
import jax
import jax.numpy as jnp
from jax import lax
from jax.experimental import pallas as pl
from jax.experimental.pallas import tpu as pltpu
from jax.sharding import PartitionSpec as P

HEADS = 20
HEAD_DIM = 64
PAIRS = 4


EPSILON = 1e-05
NEGATIVE = -1e30
GELU_SCALE = 0.7978845608028654
GELU_CUBIC = 0.044715


def from_behind(array, axis, by):
    length = lax.axis_size(axis)
    pairs = [(i, i + by) for i in range(length) if 0 <= i + by < length]
    return lax.ppermute(array, axis, pairs)


def passed_along(block, axis, distance):
    devices = range(lax.axis_size(axis))
    route = [((i - distance) % len(devices), i) for i in devices]
    return lax.ppermute(block, axis, route)


def norm_rows(values):
    center = values - jnp.mean(values, axis=-1, keepdims=True)
    inverse = lax.rsqrt(jnp.mean(center * center, axis=-1, keepdims=True) + EPSILON)
    return (center * inverse, inverse)


def norm_grad(grad_norm, normed, inverse, gain):
    scaled = grad_norm * gain
    return inverse * (
        scaled
        - jnp.mean(scaled, axis=-1, keepdims=True)
        - normed * jnp.mean(scaled * normed, axis=-1, keepdims=True)
    )


def gelu_pair(inputs):
    inner = jnp.tanh(GELU_SCALE * (inputs + GELU_CUBIC * inputs * inputs * inputs))
    value = 0.5 * inputs * (1.0 + inner)
    slope = 0.5 * (1.0 + inner) + 0.5 * inputs * (1.0 - inner * inner) * GELU_SCALE * (
        1.0 + 3.0 * GELU_CUBIC * inputs * inputs
    )
    return (value, slope)


def matmul(left, right):
    return jnp.dot(left, right, preferred_element_type=jnp.float32)


def matmul_tn(left, right):
    return lax.dot_general(
        left, right, (((0,), (0,)), ((), ())), preferred_element_type=jnp.float32
    )


def matmul_nt(left, right):
    return lax.dot_general(
        left, right, (((1,), (1,)), ((), ())), preferred_element_type=jnp.float32
    )


def shards(
    tokens,
    doc_ids,
    w_query,
    w_key,
    w_value,
    w_out,
    w_up,
    w_down,
    b_query,
    b_value,
    b_out,
    b_up,
    b_down,
    attn_gain,
    attn_beta,
    ffn_gain,
    ffn_beta,
    cotangent,
):
    tok_dev = tokens.shape[0]
    width = tokens.shape[1]
    scale = HEAD_DIM ** (-0.5)
    (
        full_query,
        full_key,
        full_value,
        full_out,
        full_up,
        full_down,
        bias_query,
        bias_value,
        bias_out,
        bias_up,
        bias_down,
        gain_attn,
        beta_attn,
        gain_ffn,
        beta_ffn,
    ) = (
        lax.all_gather(w_query, "grp", axis=0, tiled=True),
        lax.all_gather(w_key, "grp", axis=0, tiled=True),
        lax.all_gather(w_value, "grp", axis=0, tiled=True),
        lax.all_gather(w_out, "grp", axis=0, tiled=True),
        lax.all_gather(w_up, "grp", axis=0, tiled=True),
        lax.all_gather(w_down, "grp", axis=0, tiled=True),
        lax.all_gather(b_query, "grp", axis=0, tiled=True),
        lax.all_gather(b_value, "grp", axis=0, tiled=True),
        lax.all_gather(b_out, "grp", axis=0, tiled=True),
        lax.all_gather(b_up, "grp", axis=0, tiled=True),
        lax.all_gather(b_down, "grp", axis=0, tiled=True),
        lax.all_gather(attn_gain, "grp", axis=0, tiled=True),
        lax.all_gather(attn_beta, "grp", axis=0, tiled=True),
        lax.all_gather(ffn_gain, "grp", axis=0, tiled=True),
        lax.all_gather(ffn_beta, "grp", axis=0, tiled=True),
    )
    rep_index = lax.axis_index("rep")
    pad_front = (2 * PAIRS + 1) * tok_dev
    row_ids = doc_ids[0]
    padded_ids = jnp.concatenate([jnp.full((pad_front,), -1, jnp.int32), row_ids])
    query_pos = rep_index * tok_dev + jnp.arange(tok_dev, dtype=jnp.int32)
    query_doc = lax.dynamic_slice_in_dim(row_ids, rep_index * tok_dev, tok_dev)

    def block_mask(block_index):
        first = (rep_index - 2 * block_index - 1) * tok_dev
        key_pos = first + jnp.arange(2 * tok_dev, dtype=jnp.int32)
        key_doc = lax.dynamic_slice_in_dim(padded_ids, first + pad_front, 2 * tok_dev)
        return (key_doc[None, :] == query_doc[:, None]) & (key_pos[None, :] <= query_pos[:, None])

    xfull = tokens.astype(jnp.float32)
    normed_one, inverse_one = norm_rows(xfull)
    ln_one = (normed_one * gain_attn.astype(jnp.float32) + beta_attn.astype(jnp.float32)).astype(
        jnp.bfloat16
    )
    query = (matmul(ln_one, full_query) + bias_query.astype(jnp.float32)).astype(jnp.bfloat16)
    keys = matmul(ln_one, full_key).astype(jnp.bfloat16)
    values = (matmul(ln_one, full_value) + bias_value.astype(jnp.float32)).astype(jnp.bfloat16)
    query_heads = query.reshape(tok_dev, HEADS, HEAD_DIM)
    earlier = from_behind((keys, values), "rep", 1)
    first_block = (
        jnp.concatenate([earlier[0], keys], axis=0),
        jnp.concatenate([earlier[1], values], axis=0),
    )

    def fetch_pair(block, unused):
        moved = from_behind((block[0], block[1]), "rep", 2)
        return (moved, moved)

    unused_end, following = lax.scan(fetch_pair, first_block, None, length=PAIRS)
    key_blocks = jnp.concatenate([first_block[0][None], following[0]], axis=0)
    value_blocks = jnp.concatenate([first_block[1][None], following[1]], axis=0)
    block_numbers = jnp.arange(PAIRS + 1, dtype=jnp.int32)

    def scores_of(block_keys, block_index):
        raw = (
            jnp.einsum(
                "qhd,khd->hqk",
                query_heads,
                block_keys.reshape(-1, HEADS, HEAD_DIM),
                preferred_element_type=jnp.float32,
            )
            * scale
        )
        return jnp.where(block_mask(block_index)[None], raw, NEGATIVE)

    def max_step(state, inputs):
        run_max, run_sum = state
        block_keys, block_index = inputs
        scores = scores_of(block_keys, block_index)
        new_max = jnp.maximum(run_max, jnp.max(scores, axis=-1))
        run_sum = run_sum * jnp.exp(run_max - new_max) + jnp.sum(
            jnp.exp(scores - new_max[..., None]), axis=-1
        )
        return ((new_max, run_sum), None)

    start_state = (
        jnp.full((HEADS, tok_dev), NEGATIVE, jnp.float32),
        jnp.zeros((HEADS, tok_dev), jnp.float32),
    )
    (top_score, total_exp), unused_max = lax.scan(
        max_step, start_state, (key_blocks, block_numbers)
    )
    log_total = top_score + jnp.log(total_exp)

    def value_step(total, inputs):
        block_keys, block_values, block_index = inputs
        probs = jnp.exp(scores_of(block_keys, block_index) - log_total[..., None]).astype(
            jnp.bfloat16
        )
        return (
            total
            + jnp.einsum(
                "hqk,khd->qhd",
                probs,
                block_values.reshape(-1, HEADS, HEAD_DIM),
                preferred_element_type=jnp.float32,
            ),
            None,
        )

    attn, unused_value = lax.scan(
        value_step,
        jnp.zeros((tok_dev, HEADS, HEAD_DIM), jnp.float32),
        (key_blocks, value_blocks, block_numbers),
    )
    attn_low = attn.reshape(tok_dev, width).astype(jnp.bfloat16)
    hidden = xfull + matmul(attn_low, full_out) + bias_out.astype(jnp.float32)
    normed_two, inverse_two = norm_rows(hidden)
    ln_two = (normed_two * gain_ffn.astype(jnp.float32) + beta_ffn.astype(jnp.float32)).astype(
        jnp.bfloat16
    )
    pre_act = matmul(ln_two, full_up) + bias_up.astype(jnp.float32)
    act_value, act_slope = gelu_pair(pre_act)
    act_low = act_value.astype(jnp.bfloat16)
    result = hidden + matmul(act_low, full_down) + bias_down.astype(jnp.float32)
    output = result.astype(jnp.bfloat16)
    (
        back_query,
        back_key,
        back_value,
        back_out,
        back_up,
        back_down,
        back_gain_attn,
        back_gain_ffn,
    ) = (
        lax.all_gather(w_query, "grp", axis=0, tiled=True),
        lax.all_gather(w_key, "grp", axis=0, tiled=True),
        lax.all_gather(w_value, "grp", axis=0, tiled=True),
        lax.all_gather(w_out, "grp", axis=0, tiled=True),
        lax.all_gather(w_up, "grp", axis=0, tiled=True),
        lax.all_gather(w_down, "grp", axis=0, tiled=True),
        lax.all_gather(attn_gain, "grp", axis=0, tiled=True),
        lax.all_gather(ffn_gain, "grp", axis=0, tiled=True),
    )
    grad_res = cotangent.astype(jnp.float32)
    grad_w_down = matmul_tn(act_low, cotangent)
    grad_b_down = jnp.sum(grad_res, axis=0)
    grad_pre = (matmul_nt(cotangent, back_down) * act_slope).astype(jnp.bfloat16)
    grad_w_up = matmul_tn(ln_two, grad_pre)
    grad_b_up = jnp.sum(grad_pre.astype(jnp.float32), axis=0)
    grad_ln_two = matmul_nt(grad_pre, back_up)
    grad_ffn_gain = jnp.sum(grad_ln_two * normed_two, axis=0)
    grad_ffn_beta = jnp.sum(grad_ln_two, axis=0)
    grad_hidden = grad_res + norm_grad(
        grad_ln_two, normed_two, inverse_two, back_gain_ffn.astype(jnp.float32)
    )
    grad_mix = grad_hidden.astype(jnp.bfloat16)
    grad_w_out = matmul_tn(attn_low, grad_mix)
    grad_b_out = jnp.sum(grad_mix.astype(jnp.float32), axis=0)
    grad_heads = (
        matmul_nt(grad_mix, back_out).astype(jnp.bfloat16).reshape(tok_dev, HEADS, HEAD_DIM)
    )
    delta = jnp.sum(grad_heads.astype(jnp.float32) * attn, axis=-1).T

    def block_grads(block_keys, block_values, block_index):
        probs = jnp.exp(scores_of(block_keys, block_index) - log_total[..., None])
        key_heads = block_keys.reshape(-1, HEADS, HEAD_DIM)
        value_heads = block_values.reshape(-1, HEADS, HEAD_DIM)
        grad_probs = jnp.einsum(
            "qhd,khd->hqk", grad_heads, value_heads, preferred_element_type=jnp.float32
        )
        grad_scores = (probs * (grad_probs - delta[..., None])).astype(jnp.bfloat16)
        part_query = (
            jnp.einsum("hqk,khd->qhd", grad_scores, key_heads, preferred_element_type=jnp.float32)
            * scale
        )
        part_key = (
            jnp.einsum("hqk,qhd->khd", grad_scores, query_heads, preferred_element_type=jnp.float32)
            * scale
        )
        part_value = jnp.einsum(
            "hqk,qhd->khd",
            probs.astype(jnp.bfloat16),
            grad_heads,
            preferred_element_type=jnp.float32,
        )
        return (part_query, part_key, part_value)

    again = from_behind((keys, values), "rep", 1)
    back_block = (
        jnp.concatenate([again[0], keys], axis=0),
        jnp.concatenate([again[1], values], axis=0),
    )
    query_sum, key_acc, value_acc = block_grads(back_block[0], back_block[1], 0)

    def travel_step(carry, inputs):
        query_total, key_total, value_total, block_keys, block_values = carry
        block_index, kept_keys, kept_values = inputs
        block_keys, block_values = from_behind((block_keys, block_values), "rep", 2)
        key_total, value_total = (
            passed_along(key_total.astype(jnp.bfloat16), "rep", 2).astype(key_total.dtype),
            passed_along(value_total.astype(jnp.bfloat16), "rep", 2).astype(value_total.dtype),
        )
        part_query, part_key, part_value = block_grads(block_keys, block_values, block_index)
        return (
            (
                query_total + part_query,
                key_total + part_key,
                value_total + part_value,
                block_keys,
                block_values,
            ),
            None,
        )

    carry_end, unused_travel = lax.scan(
        travel_step,
        (query_sum, key_acc, value_acc, back_block[0], back_block[1]),
        (block_numbers[1:], key_blocks[1:], value_blocks[1:]),
    )
    query_sum, key_acc, value_acc = (carry_end[0], carry_end[1], carry_end[2])
    from_next = (
        passed_along(key_acc[:tok_dev].astype(jnp.bfloat16), "rep", -1).astype(jnp.float32),
        passed_along(value_acc[:tok_dev].astype(jnp.bfloat16), "rep", -1).astype(jnp.float32),
    )
    joined_key = key_acc[tok_dev:] + from_next[0]
    joined_value = value_acc[tok_dev:] + from_next[1]
    returned = (
        passed_along(joined_key.astype(jnp.bfloat16), "rep", -2 * PAIRS).astype(joined_key.dtype),
        passed_along(joined_value.astype(jnp.bfloat16), "rep", -2 * PAIRS).astype(
            joined_value.dtype
        ),
    )
    grad_query_low = query_sum.reshape(tok_dev, width).astype(jnp.bfloat16)
    grad_key_low = returned[0].reshape(tok_dev, width).astype(jnp.bfloat16)
    grad_value_low = returned[1].reshape(tok_dev, width).astype(jnp.bfloat16)
    grad_w_query = matmul_tn(ln_one, grad_query_low)
    grad_b_query = jnp.sum(grad_query_low.astype(jnp.float32), axis=0)
    grad_w_key = matmul_tn(ln_one, grad_key_low)
    grad_w_value = matmul_tn(ln_one, grad_value_low)
    grad_b_value = jnp.sum(grad_value_low.astype(jnp.float32), axis=0)
    grad_ln_one = (
        matmul_nt(grad_query_low, back_query)
        + matmul_nt(grad_key_low, back_key)
        + matmul_nt(grad_value_low, back_value)
    )
    grad_attn_gain = jnp.sum(grad_ln_one * normed_one, axis=0)
    grad_attn_beta = jnp.sum(grad_ln_one, axis=0)
    grad_input = grad_hidden + norm_grad(
        grad_ln_one, normed_one, inverse_one, back_gain_attn.astype(jnp.float32)
    )
    shares = (
        lax.psum_scatter(
            grad_w_query.astype(jnp.bfloat16), "grp", scatter_dimension=0, tiled=True
        ).astype(jnp.float32),
        lax.psum_scatter(
            grad_w_key.astype(jnp.bfloat16), "grp", scatter_dimension=0, tiled=True
        ).astype(jnp.float32),
        lax.psum_scatter(
            grad_w_value.astype(jnp.bfloat16), "grp", scatter_dimension=0, tiled=True
        ).astype(jnp.float32),
        lax.psum_scatter(
            grad_w_out.astype(jnp.bfloat16), "grp", scatter_dimension=0, tiled=True
        ).astype(jnp.float32),
        lax.psum_scatter(
            grad_w_up.astype(jnp.bfloat16), "grp", scatter_dimension=0, tiled=True
        ).astype(jnp.float32),
        lax.psum_scatter(
            grad_w_down.astype(jnp.bfloat16), "grp", scatter_dimension=0, tiled=True
        ).astype(jnp.float32),
        lax.psum_scatter(
            grad_b_query.astype(jnp.bfloat16), "grp", scatter_dimension=0, tiled=True
        ).astype(jnp.float32),
        lax.psum_scatter(
            grad_b_value.astype(jnp.bfloat16), "grp", scatter_dimension=0, tiled=True
        ).astype(jnp.float32),
        lax.psum_scatter(
            grad_b_out.astype(jnp.bfloat16), "grp", scatter_dimension=0, tiled=True
        ).astype(jnp.float32),
        lax.psum_scatter(
            grad_b_up.astype(jnp.bfloat16), "grp", scatter_dimension=0, tiled=True
        ).astype(jnp.float32),
        lax.psum_scatter(
            grad_b_down.astype(jnp.bfloat16), "grp", scatter_dimension=0, tiled=True
        ).astype(jnp.float32),
        lax.psum_scatter(
            grad_attn_gain.astype(jnp.bfloat16), "grp", scatter_dimension=0, tiled=True
        ).astype(jnp.float32),
        lax.psum_scatter(
            grad_attn_beta.astype(jnp.bfloat16), "grp", scatter_dimension=0, tiled=True
        ).astype(jnp.float32),
        lax.psum_scatter(
            grad_ffn_gain.astype(jnp.bfloat16), "grp", scatter_dimension=0, tiled=True
        ).astype(jnp.float32),
        lax.psum_scatter(
            grad_ffn_beta.astype(jnp.bfloat16), "grp", scatter_dimension=0, tiled=True
        ).astype(jnp.float32),
    )
    totals = (
        lax.psum(shares[0].astype(jnp.bfloat16), "rep").astype(jnp.float32),
        lax.psum(shares[1].astype(jnp.bfloat16), "rep").astype(jnp.float32),
        lax.psum(shares[2].astype(jnp.bfloat16), "rep").astype(jnp.float32),
        lax.psum(shares[3].astype(jnp.bfloat16), "rep").astype(jnp.float32),
        lax.psum(shares[4].astype(jnp.bfloat16), "rep").astype(jnp.float32),
        lax.psum(shares[5].astype(jnp.bfloat16), "rep").astype(jnp.float32),
        lax.psum(shares[6].astype(jnp.bfloat16), "rep").astype(jnp.float32),
        lax.psum(shares[7].astype(jnp.bfloat16), "rep").astype(jnp.float32),
        lax.psum(shares[8].astype(jnp.bfloat16), "rep").astype(jnp.float32),
        lax.psum(shares[9].astype(jnp.bfloat16), "rep").astype(jnp.float32),
        lax.psum(shares[10].astype(jnp.bfloat16), "rep").astype(jnp.float32),
        lax.psum(shares[11].astype(jnp.bfloat16), "rep").astype(jnp.float32),
        lax.psum(shares[12].astype(jnp.bfloat16), "rep").astype(jnp.float32),
        lax.psum(shares[13].astype(jnp.bfloat16), "rep").astype(jnp.float32),
        lax.psum(shares[14].astype(jnp.bfloat16), "rep").astype(jnp.float32),
    )
    return (
        output,
        grad_input,
        totals[0],
        totals[1],
        totals[2],
        totals[3],
        totals[4],
        totals[5],
        totals[6],
        totals[7],
        totals[8],
        totals[9],
        totals[10],
        totals[11],
        totals[12],
        totals[13],
        totals[14],
    )


def fits_pair(mesh):
    return mesh.shape["grp"] == 2 and mesh.shape["rep"] == 16


REACH = 9
CHUNK = 128
WINDOW = (REACH + 1) * CHUNK
HALF_LANES = 64


def iota(shape, dim):
    return lax.broadcasted_iota(jnp.int32, shape, dim)


def head_half(block, which):
    first = iota(block.shape, 1) < HALF_LANES
    return jnp.where(first if which == 0 else jnp.logical_not(first), block, jnp.zeros_like(block))


def join_halves(first, second):
    return jnp.where(iota(first.shape, 1) < HALF_LANES, first, second)


def attn_forward(q_ref, k_ref, v_ref, qid_ref, kid_ref, out_ref, lse_ref):
    span = k_ref.shape[1]
    query = q_ref[0] * jnp.bfloat16(HEAD_DIM**-0.5)
    keys, values = k_ref[0], v_ref[0]
    allowed = (qid_ref[0] == kid_ref[0]) & (
        iota((CHUNK, span), 1) <= iota((CHUNK, span), 0) + REACH * CHUNK
    )
    outs, lses = [], []
    for which in range(2):
        scores = jnp.where(allowed, matmul_nt(head_half(query, which), keys), NEGATIVE)
        top = jnp.max(scores, axis=-1, keepdims=True)
        probs = jnp.exp(scores - top)
        total = jnp.sum(probs, axis=-1, keepdims=True)
        outs.append(matmul((probs * (1.0 / total)).astype(jnp.bfloat16), values))
        lses.append(jnp.broadcast_to(top + jnp.log(total), (CHUNK, CHUNK)))
    out_ref[0] = join_halves(*outs)
    lse_ref[0] = join_halves(*lses)


def attn_query_grad(q_ref, k_ref, v_ref, qid_ref, kid_ref, do_ref, out_ref, lse_ref, dq_ref):
    span = k_ref.shape[1]
    query = q_ref[0] * jnp.bfloat16(HEAD_DIM**-0.5)
    keys, values, grad = k_ref[0], v_ref[0], do_ref[0]
    allowed = (qid_ref[0] == kid_ref[0]) & (
        iota((CHUNK, span), 1) <= iota((CHUNK, span), 0) + REACH * CHUNK
    )
    weighed = grad.astype(jnp.float32) * out_ref[0]
    parts = []
    for which in range(2):
        lse = lse_ref[0][:, which * HALF_LANES : which * HALF_LANES + 1]
        delta = jnp.sum(head_half(weighed, which), axis=-1, keepdims=True)
        scores = jnp.where(allowed, matmul_nt(head_half(query, which), keys), NEGATIVE)
        probs = jnp.exp(scores - lse)
        grad_probs = matmul_nt(head_half(grad, which), values)
        grad_scores = (probs * (grad_probs - delta)).astype(jnp.bfloat16)
        parts.append(matmul(grad_scores, keys))
    dq_ref[0] = (join_halves(*parts) * HEAD_DIM**-0.5).astype(jnp.bfloat16)


def attn_key_grad(k_ref, v_ref, q_ref, do_ref, kid_ref, qid_ref, lse_ref, delta_ref, dk_ref, dv_ref):
    span = q_ref.shape[1]
    keys = k_ref[0] * jnp.bfloat16(HEAD_DIM**-0.5)
    values, queries, grads = v_ref[0], q_ref[0], do_ref[0]
    allowed = (kid_ref[0] == qid_ref[0]) & (iota((CHUNK, span), 1) >= iota((CHUNK, span), 0))
    key_parts, value_parts = [], []
    for which in range(2):
        scores = jnp.where(allowed, matmul_nt(head_half(keys, which), queries), NEGATIVE)
        probs = jnp.exp(scores - lse_ref[0, 0, which : which + 1, :])
        value_parts.append(matmul(probs.astype(jnp.bfloat16), grads))
        grad_probs = matmul_nt(head_half(values, which), grads)
        grad_scores = (probs * (grad_probs - delta_ref[0, 0, which : which + 1, :])).astype(
            jnp.bfloat16
        )
        key_parts.append(matmul(grad_scores, queries))
    dk_ref[0] = (join_halves(*key_parts) * HEAD_DIM**-0.5).astype(jnp.bfloat16)
    dv_ref[0] = join_halves(*value_parts).astype(jnp.bfloat16)


MESH_ID = pl.DeviceIdType.MESH
RING = 8
SHARD = 240
PARTS = ((0, 128), (128, 112))
UP_CUT = 160
QKV_CUT = 176


def device_at(side, level, column, core):
    return (side, (level * 2 + column) * 2 + core)


def ring_device(side, spot, core):
    level = jnp.where(spot < 4, spot, 7 - spot)
    return device_at(side, level, spot // 4, core)


def greet(partners):
    barrier = pltpu.get_barrier_semaphore()
    for partner in partners:
        pl.semaphore_signal(barrier, inc=1, device_id=partner, device_id_type=MESH_ID)
    pl.semaphore_wait(barrier, len(partners))


def sum_kernel(
    in_ref,
    vec_ref,
    out_ref,
    vec_out_ref,
    mine,
    theirs,
    landed,
    swapped,
    vec_steps,
    vec_landed,
    load_sem,
    core_sems,
    ring_sems,
    back_sems,
    share_sems,
    swap_sems,
    vec_sems,
    keep_sem,
):
    side = lax.axis_index("grp")
    place = lax.axis_index("rep")
    level, column, core = place // 4, (place // 2) % 2, place % 2
    spot = jnp.where(column == 0, level, 7 - level)
    sibling = device_at(side, level, column, 1 - core)
    across = device_at(1 - side, level, column, core)
    ahead = ring_device(side, (spot + 1) % RING, core)
    behind = ring_device(side, (spot + RING - 1) % RING, core)
    near = level + 1 - 2 * (level % 2)
    far = (level + 2) % 4
    vec_partners = (
        sibling,
        device_at(side, level, 1 - column, core),
        device_at(side, near, column, core),
        device_at(side, far, column, core),
    )
    greet((ahead, behind, across) + vec_partners)
    targets = (ahead, behind)

    def remote(source, target, sems, where, device):
        return pltpu.make_async_remote_copy(
            source,
            target,
            sems.at[(0,) + where],
            sems.at[(1,) + where],
            device_id=device,
            device_id_type=MESH_ID,
        )

    def shard_at(way, offset):
        return (spot + RING + (1 - 2 * way) * offset) % RING

    def load(way, shard):
        return pltpu.make_async_copy(
            in_ref.at[core, way, shard], mine.at[way, shard], load_sem.at[way, shard]
        )

    def cross(way, shard):
        return remote(
            in_ref.at[1 - core, way, shard],
            theirs.at[way, shard],
            core_sems,
            (way, shard),
            sibling,
        )

    def start_inputs(step, unused):
        for way in range(2):
            shard = shard_at(way, RING - 1 - step)
            load(way, shard).start()
            cross(way, shard).start()
        return unused

    lax.fori_loop(0, RING, start_inputs, 0)

    vec_steps[0] = vec_ref[...]
    vec_copy = [
        remote(vec_steps.at[k], vec_landed.at[k], vec_sems, (k,), vec_partners[k])
        for k in range(4)
    ]
    vec_copy[0].start()

    def ring_copy(way, part, step):
        first, rows = PARTS[part]
        shard = shard_at(way, RING - 1 - step)
        return remote(
            mine.at[way, shard, pl.ds(first, rows)],
            landed.at[way, step, pl.ds(first, rows)],
            ring_sems,
            (way, part, step),
            targets[way],
        )

    def add_inputs(way, part, shard, step):
        first, rows = PARTS[part]
        here = pl.ds(first, rows)
        value = mine[way, shard, here, :].astype(jnp.float32) + theirs[
            way, shard, here, :
        ].astype(jnp.float32)
        if step is not None:
            value = value + landed[way, step, here, :].astype(jnp.float32)
        mine[way, shard, here, :] = value.astype(jnp.bfloat16)

    for way in range(2):
        shard = shard_at(way, RING - 1)
        load(way, shard).wait()
        cross(way, shard).wait()
    for part in range(2):
        for way in range(2):
            add_inputs(way, part, shard_at(way, RING - 1), None)
            ring_copy(way, part, 0).start()
    for k in range(4):
        vec_copy[k].wait()
        vec_steps[k + 1] = vec_steps[k] + vec_landed[k]
        if k < 3:
            vec_copy[k + 1].start()
    vec_out_ref[...] = vec_steps[4]

    def ring_step(step, unused):
        for way in range(2):
            shard = shard_at(way, RING - 1 - step)
            load(way, shard).wait()
            cross(way, shard).wait()
        for part in range(2):
            for way in range(2):
                ring_copy(way, part, step - 1).wait()
                add_inputs(way, part, shard_at(way, RING - 1 - step), step - 1)
                ring_copy(way, part, step).start()
        return unused

    lax.fori_loop(1, RING - 1, ring_step, 0)
    for way in range(2):
        load(way, spot).wait()
        cross(way, spot).wait()

    def back_copy(way, part, step):
        first, rows = PARTS[part]
        here = pl.ds(first, rows)
        shard = shard_at(way, RING - step)
        source = mine if isinstance(step, int) and step == 0 else out_ref.at[core]
        return remote(
            source.at[way, shard, here],
            out_ref.at[core, way, shard, here],
            back_sems,
            (way, part, step),
            targets[way],
        )

    def share(way, part, step):
        first, rows = PARTS[part]
        here = pl.ds(first, rows)
        shard = shard_at(way, RING - step)
        source = mine if isinstance(step, int) and step == 0 else out_ref.at[core]
        return remote(
            source.at[way, shard, here],
            out_ref.at[core, way, shard, here],
            share_sems,
            (way, part, step),
            sibling,
        )

    def keep(way, part):
        first, rows = PARTS[part]
        here = pl.ds(first, rows)
        return pltpu.make_async_copy(
            mine.at[way, spot, here], out_ref.at[core, way, spot, here], keep_sem.at[way, part]
        )

    def publish(way, part):
        back_copy(way, part, 0).start()
        share(way, part, 0).start()
        keep(way, part).start()

    last = RING - 2
    swaps = (pl.ds(UP_CUT, SHARD - UP_CUT), pl.ds(QKV_CUT, SHARD - QKV_CUT))
    trades = core * RING + spot < 2 * RING - 1

    def swap_copy(way):
        return remote(
            mine.at[way, spot, swaps[way]],
            swapped.at[way, pl.ds(0, SHARD - (UP_CUT, QKV_CUT)[way])],
            swap_sems,
            (way,),
            across,
        )

    for way in range(2):
        ring_copy(way, 0, last).wait()
        add_inputs(way, 0, spot, last)
        publish(way, 0)
    for way in range(2):
        ring_copy(way, 1, last).wait()
        add_inputs(way, 1, spot, last)
        if way == 0:
            swap_copy(0).start()
        else:

            @pl.when(trades)
            def _():
                swap_copy(1).start()

    swap_copy(0).wait()
    mine[0, spot, swaps[0], :] = swapped[0]
    publish(0, 1)

    @pl.when(trades)
    def _():
        swap_copy(1).wait()
        mine[1, spot, swaps[1], :] = swapped[1, : SHARD - QKV_CUT, :]

    publish(1, 1)

    for part in range(2):
        for way in range(2):
            back_copy(way, part, 0).wait()
            back_copy(way, part, jnp.int32(1)).start()
            share(way, part, jnp.int32(1)).start()

    def back_step(step, unused):
        for part in range(2):
            for way in range(2):
                back_copy(way, part, step).wait()
                back_copy(way, part, step + 1).start()
                share(way, part, step + 1).start()
        return unused

    lax.fori_loop(1, last, back_step, 0)
    for part in range(2):
        for way in range(2):
            back_copy(way, part, jnp.int32(last)).wait()
            share(way, part, jnp.int32(RING - 1)).start()
            keep(way, part).wait()
            share(way, part, 0).wait()

    def share_end(step, unused):
        for part in range(2):
            for way in range(2):
                share(way, part, step).wait()
        return unused

    lax.fori_loop(1, RING, share_end, 0)


def sum_over_rep(buffer, vectors, number):
    dma = pltpu.SemaphoreType.DMA
    return pl.pallas_call(
        sum_kernel,
        out_shape=[
            jax.ShapeDtypeStruct(buffer.shape, jnp.bfloat16),
            jax.ShapeDtypeStruct(vectors.shape, jnp.float32),
        ],
        in_specs=[
            pl.BlockSpec(memory_space=pl.ANY),
            pl.BlockSpec(memory_space=pltpu.VMEM),
        ],
        out_specs=[
            pl.BlockSpec(memory_space=pl.ANY),
            pl.BlockSpec(memory_space=pltpu.VMEM),
        ],
        scratch_shapes=[
            pltpu.VMEM((2, RING, SHARD, 1280), jnp.bfloat16),
            pltpu.VMEM((2, RING, SHARD, 1280), jnp.bfloat16),
            pltpu.VMEM((2, RING - 1, SHARD, 1280), jnp.bfloat16),
            pltpu.VMEM((2, SHARD - UP_CUT, 1280), jnp.bfloat16),
            pltpu.VMEM((5,) + vectors.shape, jnp.float32),
            pltpu.VMEM((4,) + vectors.shape, jnp.float32),
            dma((2, RING)),
            dma((2, 2, RING)),
            dma((2, 2, 2, RING - 1)),
            dma((2, 2, 2, RING - 1)),
            dma((2, 2, 2, RING)),
            dma((2, 2)),
            dma((2, 4)),
            dma((2, 2)),
        ],
        compiler_params=pltpu.CompilerParams(
            collective_id=number, has_side_effects=True, vmem_limit_bytes=56 * 2**20
        ),
    )(buffer, vectors)


def tall(array):
    blocks = [array[:, i : i + 1280] for i in range(0, array.shape[1] - 1279, 1280)]
    if array.shape[1] % 1280:
        rest = array[:, -640:]
        blocks.append(jnp.concatenate([rest[:320], rest[320:]], axis=1))
    return jnp.concatenate(blocks, axis=0)


def wide(array):
    blocks = [array[i : i + 640] for i in range(0, array.shape[0] - 639, 640)]
    if array.shape[0] % 640:
        rest = array[-320:]
        blocks.append(jnp.concatenate([rest[:, :640], rest[:, 640:]], axis=0))
    return jnp.concatenate(blocks, axis=1)


def pack_shards(down, out, up_keep, up_send, qkv_keep, qkv_send):
    count = 2 * RING
    first = jnp.concatenate(
        [down.reshape(count, UP_CUT, -1), tall(up_send).reshape(count, SHARD - UP_CUT, -1)],
        axis=1,
    )
    keep = jnp.concatenate([out, tall(up_keep), tall(qkv_keep)], axis=0)
    send = tall(qkv_send)
    edge = (count - 1) * QKV_CUT
    second = jnp.concatenate(
        [
            jnp.concatenate(
                [
                    keep[:edge].reshape(count - 1, QKV_CUT, -1),
                    send.reshape(count - 1, SHARD - QKV_CUT, -1),
                ],
                axis=1,
            ),
            keep[edge:][None],
        ],
        axis=0,
    )
    shape = (2, RING, SHARD, down.shape[1])
    return jnp.stack([first.reshape(shape), second.reshape(shape)], axis=1)


def unpack_shards(sums):
    count = 2 * RING
    width = sums.shape[-1]
    first = sums[:, 0].reshape(count, SHARD, width)
    second = sums[:, 1].reshape(count, SHARD, width)
    down = first[:, :UP_CUT].reshape(-1, width)
    up_send = wide(first[:, UP_CUT:].reshape(-1, width))
    keep = jnp.concatenate([second[:-1, :QKV_CUT].reshape(-1, width), second[-1]], axis=0)
    qkv_send = wide(second[:-1, QKV_CUT:].reshape(-1, width))
    return (down, keep[:640], wide(keep[640:1920]), up_send, wide(keep[1920:]), qkv_send)


def pair_shards(
    tokens,
    doc_ids,
    w_query,
    w_key,
    w_value,
    w_out,
    w_up,
    w_down,
    b_query,
    b_value,
    b_out,
    b_up,
    b_down,
    attn_gain,
    attn_beta,
    ffn_gain,
    ffn_beta,
    cotangent,
):
    f32, bf16 = jnp.float32, jnp.bfloat16
    chunk, width = tokens.shape
    half = width // 2
    row_len = doc_ids.shape[1]
    side = lax.axis_index("grp")
    place = lax.axis_index("rep")

    def swap(array):
        return lax.ppermute(array, "grp", [(0, 1), (1, 0)])

    def cols(array, which, size):
        return lax.dynamic_slice_in_dim(array, which * size, size, axis=array.ndim - 1)

    def both(own, other, axis):
        return jnp.where(
            side == 0,
            jnp.concatenate([own, other], axis=axis),
            jnp.concatenate([other, own], axis=axis),
        )

    small = jnp.concatenate([b_out, b_down, attn_gain, attn_beta, ffn_gain, ffn_beta]).reshape(6, half)
    small = both(small, swap(small), 1).astype(f32)
    bias_out, bias_down, gain_one, beta_one, gain_two, beta_two = [small[i] for i in range(6)]
    ids = jnp.concatenate([doc_ids, swap(doc_ids)], axis=0)
    moved = swap(jnp.concatenate([tokens, cotangent], axis=0))
    x_all = jnp.concatenate([tokens, moved[:chunk]], axis=0).astype(f32)
    cot_all = jnp.concatenate([cotangent, moved[chunk:]], axis=0)
    w_qkv = jnp.concatenate(
        [cols(w, side, half) for w in (w_query, w_key, w_value)], axis=1
    )
    w_qkv_other = swap(
        jnp.concatenate([cols(w, 1 - side, half) for w in (w_query, w_key, w_value)], axis=1)
    )
    ff_half = w_up.shape[1] // 2
    w_up_own = cols(w_up, side, ff_half)
    w_up_other = swap(cols(w_up, 1 - side, ff_half))

    normed_one, inverse_one = norm_rows(x_all)
    ln_one = (normed_one * gain_one + beta_one).astype(bf16)
    ln_one_own, ln_one_other = cols(ln_one, side, half), cols(ln_one, 1 - side, half)
    bias_qkv = jnp.concatenate([b_query.astype(f32), jnp.zeros((half,), f32), b_value.astype(f32)])
    qkv = (matmul(ln_one_own, w_qkv) + matmul(ln_one_other, w_qkv_other) + bias_qkv).astype(bf16)
    qkv = qkv.reshape(2, chunk, 3 * half)
    gathered = lax.all_gather(qkv, "rep", axis=1, tiled=True)
    front = jnp.pad(gathered[:, :, half:], ((0, 0), (REACH * chunk, 0), (0, 0)))
    kv_win = lax.dynamic_slice_in_dim(front, place * chunk, WINDOW, axis=1)
    k_win, v_win = kv_win[:, :, :half], kv_win[:, :, half:]
    q_own, k_own, v_own = qkv[:, :, :half], qkv[:, :, half : 2 * half], qkv[:, :, 2 * half :]
    own_ids = lax.dynamic_slice_in_dim(ids, place * chunk, chunk, axis=1)
    front_ids = jnp.pad(ids, ((0, 0), (REACH * chunk, 0)), constant_values=-1)
    key_ids = lax.dynamic_slice_in_dim(front_ids, place * chunk, WINDOW, axis=1)
    back_ids = jnp.pad(ids, ((0, 0), (0, REACH * chunk)), constant_values=-2)
    query_ids = lax.dynamic_slice_in_dim(back_ids, place * chunk, WINDOW, axis=1)

    pairs = half // CHUNK
    own_spec = pl.BlockSpec((1, CHUNK, CHUNK), lambda r, p: (r, 0, p))
    win_spec = pl.BlockSpec((1, WINDOW, CHUNK), lambda r, p: (r, 0, p))
    col_spec = pl.BlockSpec((1, CHUNK, 1), lambda r, p: (r, 0, 0))
    row_spec = pl.BlockSpec((1, 1, WINDOW), lambda r, p: (r, 0, 0))
    stat_spec = pl.BlockSpec((1, 1, 2, WINDOW), lambda r, p: (r, p, 0, 0))
    own_shape = (2, chunk, half)
    attn, lse = pl.pallas_call(
        attn_forward,
        grid=(2, pairs),
        in_specs=[own_spec, win_spec, win_spec, col_spec, row_spec],
        out_specs=[own_spec, own_spec],
        out_shape=[jax.ShapeDtypeStruct(own_shape, f32)] * 2,
    )(q_own, k_win, v_win, own_ids[:, :, None], key_ids[:, None, :])

    attn_low = attn.reshape(2 * chunk, half).astype(bf16)
    mixed = matmul(attn_low, w_out)
    mixed_other = swap(mixed.astype(bf16)).astype(f32)
    mixed_other = jnp.concatenate([mixed_other[chunk:], mixed_other[:chunk]], axis=0)
    hidden = x_all + mixed + mixed_other + bias_out
    normed_two, inverse_two = norm_rows(hidden)
    ln_two = (normed_two * gain_two + beta_two).astype(bf16)
    ln_two_own, ln_two_other = cols(ln_two, side, half), cols(ln_two, 1 - side, half)
    pre_act = matmul(ln_two_own, w_up_own) + matmul(ln_two_other, w_up_other) + b_up.astype(f32)
    act_value, act_slope = gelu_pair(pre_act)
    act_low = act_value.astype(bf16)
    down = matmul(act_low, w_down)
    down_other = swap(down[chunk:].astype(bf16)).astype(f32)
    output = (hidden[:chunk] + down[:chunk] + down_other + bias_down).astype(bf16)

    grad_res = cot_all.astype(f32)
    grad_w_down = matmul_tn(act_low, cot_all).astype(bf16)
    grad_pre = (matmul_nt(cot_all, w_down) * act_slope).astype(bf16)
    grad_up_keep = matmul_tn(ln_two_own, grad_pre).astype(bf16)
    grad_up_send = matmul_tn(ln_two_other, grad_pre).astype(bf16)
    back_two = both(matmul_nt(grad_pre, w_up_own), matmul_nt(grad_pre, w_up_other), 1)
    back_other = swap(back_two.astype(bf16)).astype(f32)
    grad_ln_two = back_two + jnp.concatenate([back_other[chunk:], back_other[:chunk]], axis=0)
    grad_hidden = grad_res + norm_grad(grad_ln_two, normed_two, inverse_two, gain_two)
    grad_mix = grad_hidden.astype(bf16)
    grad_w_out = matmul_tn(attn_low, grad_mix).astype(bf16)
    grad_heads = matmul_nt(grad_mix, w_out).astype(bf16)

    delta = jnp.sum(
        (grad_heads.astype(f32) * attn.reshape(2 * chunk, half)).reshape(2, chunk, half // HEAD_DIM, HEAD_DIM),
        axis=-1,
    )
    stats = jnp.concatenate(
        [lse.reshape(2, chunk, half // HEAD_DIM, HEAD_DIM)[..., 0], delta], axis=-1
    )
    stats = jnp.swapaxes(stats, 1, 2)
    all_stats = lax.all_gather(stats, "rep", axis=2, tiled=True)
    all_grads = lax.all_gather(grad_heads.reshape(own_shape), "rep", axis=1, tiled=True)
    tail = ((0, 0), (0, REACH * chunk), (0, 0))
    q_win = lax.dynamic_slice_in_dim(jnp.pad(gathered[:, :, :half], tail), place * chunk, WINDOW, axis=1)
    do_win = lax.dynamic_slice_in_dim(jnp.pad(all_grads, tail), place * chunk, WINDOW, axis=1)
    stat_win = lax.dynamic_slice_in_dim(
        jnp.pad(all_stats, ((0, 0), (0, 0), (0, REACH * chunk))), place * chunk, WINDOW, axis=2
    ).reshape(2, 2, pairs, 2, WINDOW)

    grad_query = pl.pallas_call(
        attn_query_grad,
        grid=(2, pairs),
        in_specs=[own_spec, win_spec, win_spec, col_spec, row_spec, own_spec, own_spec, own_spec],
        out_specs=own_spec,
        out_shape=jax.ShapeDtypeStruct(own_shape, bf16),
    )(
        q_own,
        k_win,
        v_win,
        own_ids[:, :, None],
        key_ids[:, None, :],
        grad_heads.reshape(own_shape),
        attn,
        lse,
    )
    grad_key, grad_value = pl.pallas_call(
        attn_key_grad,
        grid=(2, pairs),
        in_specs=[own_spec, own_spec, win_spec, win_spec, col_spec, row_spec, stat_spec, stat_spec],
        out_specs=[own_spec, own_spec],
        out_shape=[jax.ShapeDtypeStruct(own_shape, bf16)] * 2,
    )(
        k_own,
        v_own,
        q_win,
        do_win,
        own_ids[:, :, None],
        query_ids[:, None, :],
        stat_win[:, 0],
        stat_win[:, 1],
    )
    grad_qkv = jnp.concatenate([grad_query, grad_key, grad_value], axis=2).reshape(2 * chunk, 3 * half)
    grad_qkv_keep = matmul_tn(ln_one_own, grad_qkv).astype(bf16)
    grad_qkv_send = matmul_tn(ln_one_other, grad_qkv).astype(bf16)
    back_one = both(matmul_nt(grad_qkv, w_qkv), matmul_nt(grad_qkv, w_qkv_other), 1)
    back_other = swap(back_one.astype(bf16)).astype(f32)
    grad_ln_one = back_one + jnp.concatenate([back_other[chunk:], back_other[:chunk]], axis=0)
    grad_input = grad_hidden + norm_grad(grad_ln_one, normed_one, inverse_one, gain_one)

    def total(array):
        return jnp.sum(array.astype(f32), axis=0)

    qkv_vec = total(grad_qkv)
    vectors = [
        qkv_vec[:half],
        qkv_vec[2 * half :],
        cols(total(grad_mix), side, half),
        total(grad_pre),
        cols(total(grad_res), side, half),
        cols(total(grad_ln_one * normed_one), side, half),
        cols(total(grad_ln_one), side, half),
        cols(total(grad_ln_two * normed_two), side, half),
        cols(total(grad_ln_two), side, half),
    ]
    packed = jnp.concatenate(vectors)
    lanes = 128
    packed = jnp.pad(packed, (0, 64 * lanes - packed.shape[0])).reshape(64, lanes)
    buffer = pack_shards(
        grad_w_down, grad_w_out, grad_up_keep, grad_up_send, grad_qkv_keep, grad_qkv_send
    )
    sums, vec_sum = sum_over_rep(buffer, packed, 1)
    vec_sum = vec_sum.reshape(-1)
    cuts, at = [], 0
    for vector in vectors:
        cuts.append(vec_sum[at : at + vector.shape[0]])
        at += vector.shape[0]
    sum_down, sum_out, sum_up, sum_up_other, sum_qkv, sum_qkv_other = unpack_shards(
        sums.astype(f32)
    )
    three = [
        both(sum_qkv[:, i * half : (i + 1) * half], sum_qkv_other[:, i * half : (i + 1) * half], 1)
        for i in range(3)
    ]
    return (
        output,
        grad_input[:chunk],
        three[0],
        three[1],
        three[2],
        sum_out,
        both(sum_up, sum_up_other, 1),
        sum_down,
        *cuts,
    )


def solution(mesh):
    in_specs = (
        P(("grp", "rep"), None),
        P("grp", None),
        P("grp", None),
        P("grp", None),
        P("grp", None),
        P("grp", None),
        P("grp", None),
        P("grp", None),
        P("grp"),
        P("grp"),
        P("grp"),
        P("grp"),
        P("grp"),
        P("grp"),
        P("grp"),
        P("grp"),
        P("grp"),
        P(("grp", "rep"), None),
    )
    out_specs = (
        P(("grp", "rep"), None),
        P(("grp", "rep"), None),
        P("grp", None),
        P("grp", None),
        P("grp", None),
        P("grp", None),
        P("grp", None),
        P("grp", None),
        P("grp"),
        P("grp"),
        P("grp"),
        P("grp"),
        P("grp"),
        P("grp"),
        P("grp"),
        P("grp"),
        P("grp"),
    )
    plan = pair_shards if fits_pair(mesh) else shards
    return jax.shard_map(plan, mesh=mesh, in_specs=in_specs, out_specs=out_specs, check_vma=False)
```

```python
import jax
import jax.numpy as jnp
from jax import lax
from jax.experimental import pallas as pl
from jax.experimental.pallas import tpu as pltpu
from jax.sharding import PartitionSpec as P

HEADS = 20
HEAD_DIM = 64
PAIRS = 4


EPSILON = 1e-05
NEGATIVE = -1e30
GELU_SCALE = 0.7978845608028654
GELU_CUBIC = 0.044715


def from_behind(array, axis, by):
    length = lax.axis_size(axis)
    pairs = [(i, i + by) for i in range(length) if 0 <= i + by < length]
    return lax.ppermute(array, axis, pairs)


def passed_along(block, axis, distance):
    devices = range(lax.axis_size(axis))
    route = [((i - distance) % len(devices), i) for i in devices]
    return lax.ppermute(block, axis, route)


def norm_rows(values):
    center = values - jnp.mean(values, axis=-1, keepdims=True)
    inverse = lax.rsqrt(jnp.mean(center * center, axis=-1, keepdims=True) + EPSILON)
    return (center * inverse, inverse)


def norm_grad(grad_norm, normed, inverse, gain):
    scaled = grad_norm * gain
    return inverse * (
        scaled
        - jnp.mean(scaled, axis=-1, keepdims=True)
        - normed * jnp.mean(scaled * normed, axis=-1, keepdims=True)
    )


def gelu_pair(inputs):
    inner = jnp.tanh(GELU_SCALE * (inputs + GELU_CUBIC * inputs * inputs * inputs))
    value = 0.5 * inputs * (1.0 + inner)
    slope = 0.5 * (1.0 + inner) + 0.5 * inputs * (1.0 - inner * inner) * GELU_SCALE * (
        1.0 + 3.0 * GELU_CUBIC * inputs * inputs
    )
    return (value, slope)


def matmul(left, right):
    return jnp.dot(left, right, preferred_element_type=jnp.float32)


def matmul_tn(left, right):
    return lax.dot_general(
        left, right, (((0,), (0,)), ((), ())), preferred_element_type=jnp.float32
    )


def matmul_nt(left, right):
    return lax.dot_general(
        left, right, (((1,), (1,)), ((), ())), preferred_element_type=jnp.float32
    )


def shards(
    tokens,
    doc_ids,
    w_query,
    w_key,
    w_value,
    w_out,
    w_up,
    w_down,
    b_query,
    b_value,
    b_out,
    b_up,
    b_down,
    attn_gain,
    attn_beta,
    ffn_gain,
    ffn_beta,
    cotangent,
):
    tok_dev = tokens.shape[0]
    width = tokens.shape[1]
    scale = HEAD_DIM ** (-0.5)
    (
        full_query,
        full_key,
        full_value,
        full_out,
        full_up,
        full_down,
        bias_query,
        bias_value,
        bias_out,
        bias_up,
        bias_down,
        gain_attn,
        beta_attn,
        gain_ffn,
        beta_ffn,
    ) = (
        lax.all_gather(w_query, "grp", axis=0, tiled=True),
        lax.all_gather(w_key, "grp", axis=0, tiled=True),
        lax.all_gather(w_value, "grp", axis=0, tiled=True),
        lax.all_gather(w_out, "grp", axis=0, tiled=True),
        lax.all_gather(w_up, "grp", axis=0, tiled=True),
        lax.all_gather(w_down, "grp", axis=0, tiled=True),
        lax.all_gather(b_query, "grp", axis=0, tiled=True),
        lax.all_gather(b_value, "grp", axis=0, tiled=True),
        lax.all_gather(b_out, "grp", axis=0, tiled=True),
        lax.all_gather(b_up, "grp", axis=0, tiled=True),
        lax.all_gather(b_down, "grp", axis=0, tiled=True),
        lax.all_gather(attn_gain, "grp", axis=0, tiled=True),
        lax.all_gather(attn_beta, "grp", axis=0, tiled=True),
        lax.all_gather(ffn_gain, "grp", axis=0, tiled=True),
        lax.all_gather(ffn_beta, "grp", axis=0, tiled=True),
    )
    rep_index = lax.axis_index("rep")
    pad_front = (2 * PAIRS + 1) * tok_dev
    row_ids = doc_ids[0]
    padded_ids = jnp.concatenate([jnp.full((pad_front,), -1, jnp.int32), row_ids])
    query_pos = rep_index * tok_dev + jnp.arange(tok_dev, dtype=jnp.int32)
    query_doc = lax.dynamic_slice_in_dim(row_ids, rep_index * tok_dev, tok_dev)

    def block_mask(block_index):
        first = (rep_index - 2 * block_index - 1) * tok_dev
        key_pos = first + jnp.arange(2 * tok_dev, dtype=jnp.int32)
        key_doc = lax.dynamic_slice_in_dim(padded_ids, first + pad_front, 2 * tok_dev)
        return (key_doc[None, :] == query_doc[:, None]) & (key_pos[None, :] <= query_pos[:, None])

    xfull = tokens.astype(jnp.float32)
    normed_one, inverse_one = norm_rows(xfull)
    ln_one = (normed_one * gain_attn.astype(jnp.float32) + beta_attn.astype(jnp.float32)).astype(
        jnp.bfloat16
    )
    query = (matmul(ln_one, full_query) + bias_query.astype(jnp.float32)).astype(jnp.bfloat16)
    keys = matmul(ln_one, full_key).astype(jnp.bfloat16)
    values = (matmul(ln_one, full_value) + bias_value.astype(jnp.float32)).astype(jnp.bfloat16)
    query_heads = query.reshape(tok_dev, HEADS, HEAD_DIM)
    earlier = from_behind((keys, values), "rep", 1)
    first_block = (
        jnp.concatenate([earlier[0], keys], axis=0),
        jnp.concatenate([earlier[1], values], axis=0),
    )

    def fetch_pair(block, unused):
        moved = from_behind((block[0], block[1]), "rep", 2)
        return (moved, moved)

    unused_end, following = lax.scan(fetch_pair, first_block, None, length=PAIRS)
    key_blocks = jnp.concatenate([first_block[0][None], following[0]], axis=0)
    value_blocks = jnp.concatenate([first_block[1][None], following[1]], axis=0)
    block_numbers = jnp.arange(PAIRS + 1, dtype=jnp.int32)

    def scores_of(block_keys, block_index):
        raw = (
            jnp.einsum(
                "qhd,khd->hqk",
                query_heads,
                block_keys.reshape(-1, HEADS, HEAD_DIM),
                preferred_element_type=jnp.float32,
            )
            * scale
        )
        return jnp.where(block_mask(block_index)[None], raw, NEGATIVE)

    def max_step(state, inputs):
        run_max, run_sum = state
        block_keys, block_index = inputs
        scores = scores_of(block_keys, block_index)
        new_max = jnp.maximum(run_max, jnp.max(scores, axis=-1))
        run_sum = run_sum * jnp.exp(run_max - new_max) + jnp.sum(
            jnp.exp(scores - new_max[..., None]), axis=-1
        )
        return ((new_max, run_sum), None)

    start_state = (
        jnp.full((HEADS, tok_dev), NEGATIVE, jnp.float32),
        jnp.zeros((HEADS, tok_dev), jnp.float32),
    )
    (top_score, total_exp), unused_max = lax.scan(
        max_step, start_state, (key_blocks, block_numbers)
    )
    log_total = top_score + jnp.log(total_exp)

    def value_step(total, inputs):
        block_keys, block_values, block_index = inputs
        probs = jnp.exp(scores_of(block_keys, block_index) - log_total[..., None]).astype(
            jnp.bfloat16
        )
        return (
            total
            + jnp.einsum(
                "hqk,khd->qhd",
                probs,
                block_values.reshape(-1, HEADS, HEAD_DIM),
                preferred_element_type=jnp.float32,
            ),
            None,
        )

    attn, unused_value = lax.scan(
        value_step,
        jnp.zeros((tok_dev, HEADS, HEAD_DIM), jnp.float32),
        (key_blocks, value_blocks, block_numbers),
    )
    attn_low = attn.reshape(tok_dev, width).astype(jnp.bfloat16)
    hidden = xfull + matmul(attn_low, full_out) + bias_out.astype(jnp.float32)
    normed_two, inverse_two = norm_rows(hidden)
    ln_two = (normed_two * gain_ffn.astype(jnp.float32) + beta_ffn.astype(jnp.float32)).astype(
        jnp.bfloat16
    )
    pre_act = matmul(ln_two, full_up) + bias_up.astype(jnp.float32)
    act_value, act_slope = gelu_pair(pre_act)
    act_low = act_value.astype(jnp.bfloat16)
    result = hidden + matmul(act_low, full_down) + bias_down.astype(jnp.float32)
    output = result.astype(jnp.bfloat16)
    (
        back_query,
        back_key,
        back_value,
        back_out,
        back_up,
        back_down,
        back_gain_attn,
        back_gain_ffn,
    ) = (
        lax.all_gather(w_query, "grp", axis=0, tiled=True),
        lax.all_gather(w_key, "grp", axis=0, tiled=True),
        lax.all_gather(w_value, "grp", axis=0, tiled=True),
        lax.all_gather(w_out, "grp", axis=0, tiled=True),
        lax.all_gather(w_up, "grp", axis=0, tiled=True),
        lax.all_gather(w_down, "grp", axis=0, tiled=True),
        lax.all_gather(attn_gain, "grp", axis=0, tiled=True),
        lax.all_gather(ffn_gain, "grp", axis=0, tiled=True),
    )
    grad_res = cotangent.astype(jnp.float32)
    grad_w_down = matmul_tn(act_low, cotangent)
    grad_b_down = jnp.sum(grad_res, axis=0)
    grad_pre = (matmul_nt(cotangent, back_down) * act_slope).astype(jnp.bfloat16)
    grad_w_up = matmul_tn(ln_two, grad_pre)
    grad_b_up = jnp.sum(grad_pre.astype(jnp.float32), axis=0)
    grad_ln_two = matmul_nt(grad_pre, back_up)
    grad_ffn_gain = jnp.sum(grad_ln_two * normed_two, axis=0)
    grad_ffn_beta = jnp.sum(grad_ln_two, axis=0)
    grad_hidden = grad_res + norm_grad(
        grad_ln_two, normed_two, inverse_two, back_gain_ffn.astype(jnp.float32)
    )
    grad_mix = grad_hidden.astype(jnp.bfloat16)
    grad_w_out = matmul_tn(attn_low, grad_mix)
    grad_b_out = jnp.sum(grad_mix.astype(jnp.float32), axis=0)
    grad_heads = (
        matmul_nt(grad_mix, back_out).astype(jnp.bfloat16).reshape(tok_dev, HEADS, HEAD_DIM)
    )
    delta = jnp.sum(grad_heads.astype(jnp.float32) * attn, axis=-1).T

    def block_grads(block_keys, block_values, block_index):
        probs = jnp.exp(scores_of(block_keys, block_index) - log_total[..., None])
        key_heads = block_keys.reshape(-1, HEADS, HEAD_DIM)
        value_heads = block_values.reshape(-1, HEADS, HEAD_DIM)
        grad_probs = jnp.einsum(
            "qhd,khd->hqk", grad_heads, value_heads, preferred_element_type=jnp.float32
        )
        grad_scores = (probs * (grad_probs - delta[..., None])).astype(jnp.bfloat16)
        part_query = (
            jnp.einsum("hqk,khd->qhd", grad_scores, key_heads, preferred_element_type=jnp.float32)
            * scale
        )
        part_key = (
            jnp.einsum("hqk,qhd->khd", grad_scores, query_heads, preferred_element_type=jnp.float32)
            * scale
        )
        part_value = jnp.einsum(
            "hqk,qhd->khd",
            probs.astype(jnp.bfloat16),
            grad_heads,
            preferred_element_type=jnp.float32,
        )
        return (part_query, part_key, part_value)

    again = from_behind((keys, values), "rep", 1)
    back_block = (
        jnp.concatenate([again[0], keys], axis=0),
        jnp.concatenate([again[1], values], axis=0),
    )
    query_sum, key_acc, value_acc = block_grads(back_block[0], back_block[1], 0)

    def travel_step(carry, inputs):
        query_total, key_total, value_total, block_keys, block_values = carry
        block_index, kept_keys, kept_values = inputs
        block_keys, block_values = from_behind((block_keys, block_values), "rep", 2)
        key_total, value_total = (
            passed_along(key_total.astype(jnp.bfloat16), "rep", 2).astype(key_total.dtype),
            passed_along(value_total.astype(jnp.bfloat16), "rep", 2).astype(value_total.dtype),
        )
        part_query, part_key, part_value = block_grads(block_keys, block_values, block_index)
        return (
            (
                query_total + part_query,
                key_total + part_key,
                value_total + part_value,
                block_keys,
                block_values,
            ),
            None,
        )

    carry_end, unused_travel = lax.scan(
        travel_step,
        (query_sum, key_acc, value_acc, back_block[0], back_block[1]),
        (block_numbers[1:], key_blocks[1:], value_blocks[1:]),
    )
    query_sum, key_acc, value_acc = (carry_end[0], carry_end[1], carry_end[2])
    from_next = (
        passed_along(key_acc[:tok_dev].astype(jnp.bfloat16), "rep", -1).astype(jnp.float32),
        passed_along(value_acc[:tok_dev].astype(jnp.bfloat16), "rep", -1).astype(jnp.float32),
    )
    joined_key = key_acc[tok_dev:] + from_next[0]
    joined_value = value_acc[tok_dev:] + from_next[1]
    returned = (
        passed_along(joined_key.astype(jnp.bfloat16), "rep", -2 * PAIRS).astype(joined_key.dtype),
        passed_along(joined_value.astype(jnp.bfloat16), "rep", -2 * PAIRS).astype(
            joined_value.dtype
        ),
    )
    grad_query_low = query_sum.reshape(tok_dev, width).astype(jnp.bfloat16)
    grad_key_low = returned[0].reshape(tok_dev, width).astype(jnp.bfloat16)
    grad_value_low = returned[1].reshape(tok_dev, width).astype(jnp.bfloat16)
    grad_w_query = matmul_tn(ln_one, grad_query_low)
    grad_b_query = jnp.sum(grad_query_low.astype(jnp.float32), axis=0)
    grad_w_key = matmul_tn(ln_one, grad_key_low)
    grad_w_value = matmul_tn(ln_one, grad_value_low)
    grad_b_value = jnp.sum(grad_value_low.astype(jnp.float32), axis=0)
    grad_ln_one = (
        matmul_nt(grad_query_low, back_query)
        + matmul_nt(grad_key_low, back_key)
        + matmul_nt(grad_value_low, back_value)
    )
    grad_attn_gain = jnp.sum(grad_ln_one * normed_one, axis=0)
    grad_attn_beta = jnp.sum(grad_ln_one, axis=0)
    grad_input = grad_hidden + norm_grad(
        grad_ln_one, normed_one, inverse_one, back_gain_attn.astype(jnp.float32)
    )
    shares = (
        lax.psum_scatter(
            grad_w_query.astype(jnp.bfloat16), "grp", scatter_dimension=0, tiled=True
        ).astype(jnp.float32),
        lax.psum_scatter(
            grad_w_key.astype(jnp.bfloat16), "grp", scatter_dimension=0, tiled=True
        ).astype(jnp.float32),
        lax.psum_scatter(
            grad_w_value.astype(jnp.bfloat16), "grp", scatter_dimension=0, tiled=True
        ).astype(jnp.float32),
        lax.psum_scatter(
            grad_w_out.astype(jnp.bfloat16), "grp", scatter_dimension=0, tiled=True
        ).astype(jnp.float32),
        lax.psum_scatter(
            grad_w_up.astype(jnp.bfloat16), "grp", scatter_dimension=0, tiled=True
        ).astype(jnp.float32),
        lax.psum_scatter(
            grad_w_down.astype(jnp.bfloat16), "grp", scatter_dimension=0, tiled=True
        ).astype(jnp.float32),
        lax.psum_scatter(
            grad_b_query.astype(jnp.bfloat16), "grp", scatter_dimension=0, tiled=True
        ).astype(jnp.float32),
        lax.psum_scatter(
            grad_b_value.astype(jnp.bfloat16), "grp", scatter_dimension=0, tiled=True
        ).astype(jnp.float32),
        lax.psum_scatter(
            grad_b_out.astype(jnp.bfloat16), "grp", scatter_dimension=0, tiled=True
        ).astype(jnp.float32),
        lax.psum_scatter(
            grad_b_up.astype(jnp.bfloat16), "grp", scatter_dimension=0, tiled=True
        ).astype(jnp.float32),
        lax.psum_scatter(
            grad_b_down.astype(jnp.bfloat16), "grp", scatter_dimension=0, tiled=True
        ).astype(jnp.float32),
        lax.psum_scatter(
            grad_attn_gain.astype(jnp.bfloat16), "grp", scatter_dimension=0, tiled=True
        ).astype(jnp.float32),
        lax.psum_scatter(
            grad_attn_beta.astype(jnp.bfloat16), "grp", scatter_dimension=0, tiled=True
        ).astype(jnp.float32),
        lax.psum_scatter(
            grad_ffn_gain.astype(jnp.bfloat16), "grp", scatter_dimension=0, tiled=True
        ).astype(jnp.float32),
        lax.psum_scatter(
            grad_ffn_beta.astype(jnp.bfloat16), "grp", scatter_dimension=0, tiled=True
        ).astype(jnp.float32),
    )
    totals = (
        lax.psum(shares[0].astype(jnp.bfloat16), "rep").astype(jnp.float32),
        lax.psum(shares[1].astype(jnp.bfloat16), "rep").astype(jnp.float32),
        lax.psum(shares[2].astype(jnp.bfloat16), "rep").astype(jnp.float32),
        lax.psum(shares[3].astype(jnp.bfloat16), "rep").astype(jnp.float32),
        lax.psum(shares[4].astype(jnp.bfloat16), "rep").astype(jnp.float32),
        lax.psum(shares[5].astype(jnp.bfloat16), "rep").astype(jnp.float32),
        lax.psum(shares[6].astype(jnp.bfloat16), "rep").astype(jnp.float32),
        lax.psum(shares[7].astype(jnp.bfloat16), "rep").astype(jnp.float32),
        lax.psum(shares[8].astype(jnp.bfloat16), "rep").astype(jnp.float32),
        lax.psum(shares[9].astype(jnp.bfloat16), "rep").astype(jnp.float32),
        lax.psum(shares[10].astype(jnp.bfloat16), "rep").astype(jnp.float32),
        lax.psum(shares[11].astype(jnp.bfloat16), "rep").astype(jnp.float32),
        lax.psum(shares[12].astype(jnp.bfloat16), "rep").astype(jnp.float32),
        lax.psum(shares[13].astype(jnp.bfloat16), "rep").astype(jnp.float32),
        lax.psum(shares[14].astype(jnp.bfloat16), "rep").astype(jnp.float32),
    )
    return (
        output,
        grad_input,
        totals[0],
        totals[1],
        totals[2],
        totals[3],
        totals[4],
        totals[5],
        totals[6],
        totals[7],
        totals[8],
        totals[9],
        totals[10],
        totals[11],
        totals[12],
        totals[13],
        totals[14],
    )


def fits_pair(mesh):
    return mesh.shape["grp"] == 2 and mesh.shape["rep"] == 16


REACH = 9
CHUNK = 128
WINDOW = (REACH + 1) * CHUNK
HALF_LANES = 64


def iota(shape, dim):
    return lax.broadcasted_iota(jnp.int32, shape, dim)


def head_half(block, which):
    first = iota(block.shape, 1) < HALF_LANES
    return jnp.where(first if which == 0 else jnp.logical_not(first), block, jnp.zeros_like(block))


def join_halves(first, second):
    return jnp.where(iota(first.shape, 1) < HALF_LANES, first, second)


SLOTS = 12
LEVELS = 4


class Stream:
    def __init__(self, side, spot, mirrored, view, sems):
        self.side, self.mirrored, self.view, self.sems = side, mirrored, view, sems
        level, column, core = spot
        if mirrored:
            level, column, core = LEVELS - 1 - level, 1 - column, 1 - core
        self.level, self.column, self.core = level, column, core

    def device(self, level, column, core):
        if self.mirrored:
            level, column, core = LEVELS - 1 - level, 1 - column, 1 - core
        return device_at(self.side, level, column, core)

    def slot(self, holder, chunk):
        gaps = [c - h for c, h in zip(chunk, holder)]
        return SLOTS - 1 + 4 * gaps[0] + 2 * gaps[1] + gaps[2]

    def copy(self, kind, chunk, target):
        me = (self.level, self.column, self.core)
        return remote(
            self.view(self.slot(me, chunk)),
            self.view(self.slot(target, chunk)),
            self.sems,
            (kind,),
            self.device(*target),
        )

    def arrived(self, kind):
        here = self.view(SLOTS - 1)
        twin = self.device(self.level, self.column, 1 - self.core)
        remote(here, here, self.sems, (kind,), twin).wait_recv()

    def up(self, back):
        chunk = (self.level - back, self.column, self.core)
        target = ((self.level + 1) % LEVELS, self.column, self.core)
        if back == 2:
            chunk, target = (self.level - 1, 1, 1), ((self.level + 2) % LEVELS, 0, 0)
        return self.copy(back, chunk, target)

    def over(self, back):
        chunk = (self.level - back, self.column, self.core)
        return self.copy(3 + back, chunk, (self.level, 1 - self.column, self.core))

    def twin(self, back):
        chunk = (self.level - back, self.column, self.core)
        return self.copy(6 + back, chunk, (self.level, self.column, 1 - self.core))

    def pass_on(self, back):
        chunk = (self.level - back, 1 - self.column, self.core)
        return self.copy(9 + back, chunk, (self.level, self.column, 1 - self.core))

    def sends_up(self, back):
        if back == 2:
            return (self.level == LEVELS - 3) & (self.column == 0) & (self.core == 1)
        return (self.level >= back) & (self.level < LEVELS - 1)

    def gets_up(self, back):
        if back == 2:
            return (self.level == LEVELS - 1) & (self.column + self.core == 0)
        return self.level >= back + 1

    def sends_over(self, back):
        if back == 0:
            return self.column == 0
        if back == 1:
            return self.level >= 1
        return (self.level >= 2) & (self.column + self.core >= 1)

    def gets_over(self, back):
        if back == 0:
            return self.column == 1
        if back == 1:
            return self.level >= 1
        return (self.level >= 2) & (1 - self.column + self.core >= 1)

    def sends_twin(self, back):
        return self.core == 0 if back == 0 else self.level >= back

    def gets_twin(self, back):
        return self.core == 1 if back == 0 else self.level >= back

    def gets_pass(self, back):
        if back < 2:
            return self.gets_over(back)
        return (self.level >= 2) & (2 - self.column - self.core >= 1)

    def start_own(self, wide=True):
        pl.when(self.sends_up(0))(lambda: self.up(0).start())
        pl.when(self.sends_twin(0))(lambda: self.twin(0).start())
        self.start_over(0, wide)

    def start_over(self, back, wide=True):
        pl.when(self.sends_over(back) & wide)(lambda: self.over(back).start())

    def after_up(self, back, wide=True):
        @pl.when(self.gets_up(back))
        def _():
            self.arrived(back)

        if back == 0:
            pl.when(self.sends_up(1))(lambda: self.up(1).start())
        self.start_over(back + 1, wide)
        pl.when(self.sends_twin(back + 1))(lambda: self.twin(back + 1).start())

    def after_over(self, back):
        @pl.when(self.gets_over(back))
        def _():
            self.arrived(3 + back)
            self.pass_on(back).start()

        if back == 1:
            pl.when(self.sends_up(2))(lambda: self.up(2).start())

    def after_twins(self):
        for back in range(3):
            pl.when(self.gets_twin(back))(lambda: self.arrived(6 + back))
            pl.when(self.gets_pass(back))(lambda: self.arrived(9 + back))
        pl.when(self.gets_up(2))(lambda: self.arrived(2))

    def finish(self):
        for back in range(3):
            pl.when(self.sends_up(back))(lambda: self.up(back).wait_send())
            pl.when(self.sends_over(back))(lambda: self.over(back).wait_send())
            pl.when(self.sends_twin(back))(lambda: self.twin(back).wait_send())
            pl.when(self.gets_over(back))(lambda: self.pass_on(back).wait_send())


def spot_of(place):
    return (place // 4, (place // 2) % 2, place % 2)


def neighbours(side, spot):
    level, column, core = spot
    return (
        device_at(1 - side, level, column, core),
        device_at(side, level, column, 1 - core),
        device_at(side, level, 1 - column, core),
        device_at(side, (level + 1) % LEVELS, column, core),
        device_at(side, (level + LEVELS - 1) % LEVELS, column, core),
    )


def rows_of(ref):
    return lambda slot: ref.at[:, tile(CHUNK * slot, CHUNK, CHUNK), :]


def row_of(ref, row):
    return lambda slot: ref.at[row, tile(CHUNK * slot, CHUNK, CHUNK), :]


def far_corners(side, spot):
    level, column, core = spot
    return (device_at(side, (level + 2) % LEVELS, column, 1 - core),)


def front_kernel(
    tok_ref,
    cot_ref,
    ids_ref,
    small_ref,
    wk_ref,
    wv_ref,
    wq_ref,
    wup_ref,
    w_out_ref,
    kwin_out,
    vwin_out,
    qwin_out,
    k_own,
    v_own,
    q_own,
    ln_out,
    tok_other,
    cot_other,
    ids_other,
    small_all,
    w_other_out,
    wup_other,
    attn_ref,
    lse_ref,
    mixed_ref,
    ids_all,
    kwin,
    vwin,
    qwin,
    w_other,
    w_own,
    ln_all,
    sent,
    came,
    own_sem,
    y_sems,
    w_sems,
    flow_sems,
    mix_sems,
    out_sem,
):
    side = lax.axis_index("grp")
    spot = spot_of(lax.axis_index("rep"))
    level, column, core = spot
    across, twin, over, above, below = neighbours(side, spot)
    near = device_at(side, level + 1 - 2 * (level % 2), column, core)
    f32, bf16 = jnp.float32, jnp.bfloat16
    half = w_own.shape[1]
    for win in (kwin, vwin, qwin):
        win[...] = jnp.zeros_like(win)
    greet((across, twin, over, above, below) + far_corners(side, spot))

    weights = (wk_ref, wv_ref, wq_ref)
    quarter = half // 4

    def part(owner):
        return tile(quarter * owner, quarter)

    mine = 2 * (level % 2) + core
    own_cols, other_cols = tile(half * side, half, 128), tile(half * (1 - side), half, 128)
    y_small = remote(small_ref, small_all.at[:, own_cols], y_sems, (0,), across)
    y_ids = remote(ids_ref, ids_other, y_sems, (1,), across)
    y_tok = remote(tok_ref, tok_other, y_sems, (2,), across)
    y_cot = remote(cot_ref, cot_other, y_sems, (3,), across)
    ff_half = wup_other.shape[1]

    def w_part(m, owner):
        return wup_other.at[part(owner)] if m == 3 else w_other.at[m, part(owner)]

    def w_across(m):
        if m == 3:
            source = wup_ref.at[part(mine), tile(ff_half * (1 - side), ff_half, 128)]
        else:
            source = weights[m].at[part(mine), other_cols]
        return remote(source, w_part(m, mine), w_sems, (0, m), across)

    def w_over(m):
        here = w_part(m, mine)
        return remote(here, here, w_sems, (1, m), near)

    def w_twin(m):
        here = w_part(m, mine)
        return remote(here, here, w_sems, (2, m), twin)

    def w_pass(m):
        here = w_part(m, 2 * (1 - level % 2) + core)
        return remote(here, here, w_sems, (3, m), twin)

    def w_load(m):
        return pltpu.make_async_copy(weights[m].at[:, own_cols], w_own.at[m], own_sem.at[m])

    y_small.start()
    w_across(0).start()
    w_across(1).start()
    for m in range(3):
        w_load(m).start()

    small_all[:, own_cols] = small_ref[...]

    def norm_into(rows, ref):
        x = ref[...].astype(f32)
        center = x - jnp.mean(x, axis=-1, keepdims=True)
        inverse = lax.rsqrt(jnp.mean(center * center, axis=-1, keepdims=True) + EPSILON)
        gain, beta = small_all[2:3, :].astype(f32), small_all[3:4, :].astype(f32)
        ln_all[rows, :] = (center * inverse * gain + beta).astype(bf16)
        ln_out[rows, :half] = ln_all[rows, own_cols]
        ln_out[rows, half:] = ln_all[rows, other_cols]

    def w_forward(m):
        w_across(m).wait_recv()
        w_over(m).start()
        w_twin(m).start()

    def w_second(m):
        w_over(m).wait_recv()
        w_pass(m).start()

    wins, biases = (kwin, vwin, qwin), (None, 7, 6)

    def project(m, row):
        rows = pl.ds(CHUNK * row, CHUNK)
        value = matmul(ln_out[rows, :half], w_own[m]) + matmul(ln_out[rows, half:], w_other[m])
        if biases[m] is not None:
            value = value + small_ref[biases[m] : biases[m] + 1, :].astype(f32)
        wins[m][row, pl.ds((SLOTS - 1) * CHUNK, CHUNK), :] = value.astype(bf16)
        (k_own, v_own, q_own)[m][rows, :] = value.astype(bf16)

    def win_out(m, row):
        target = (kwin_out, vwin_out, qwin_out)[m]
        return pltpu.make_async_copy(wins[m].at[row], target.at[row], out_sem.at[m, row])

    w_out_copy = pltpu.make_async_copy(w_other, w_other_out, out_sem.at[3, 0])

    def w_ready(m):
        w_load(m).wait()
        w_twin(m).wait_recv()
        w_pass(m).wait_recv()

    flows = [
        [
            Stream(side, spot, m == 2, row_of(wins[m], row), flow_sems.at[3 * row + m])
            for m in range(3)
        ]
        for row in range(2)
    ]
    pairs_of = [flow[:2] for flow in flows]
    queries = [flow[2] for flow in flows]

    def each(streams, event, *args):
        for stream in streams:
            getattr(stream, event)(*args)

    w_forward(0)
    y_ids.start()
    y_small.wait()
    y_tok.start()
    norm_into(pl.ds(0, CHUNK), tok_ref)
    w_forward(1)
    w_across(2).start()
    w_second(0)
    w_ready(0)
    project(0, 0)
    flows[0][0].start_own()
    w_second(1)
    w_ready(1)
    project(1, 0)
    flows[0][1].start_own()
    y_tok.wait_recv()
    norm_into(pl.ds(CHUNK, CHUNK), tok_other)
    project(0, 1)
    flows[1][0].start_own()
    project(1, 1)
    flows[1][1].start_own()
    each(pairs_of[0], "after_up", 0)
    w_forward(2)
    w_across(3).start()
    y_cot.start()
    each(pairs_of[0], "after_over", 0)
    w_second(2)
    each(pairs_of[1], "after_up", 0)
    w_ready(2)
    project(2, 0)
    project(2, 1)
    light = level < 2
    each(queries, "start_own", light)
    w_out_copy.start()
    each(pairs_of[0], "after_up", 1)
    each(pairs_of[1], "after_over", 0)
    each(pairs_of[1], "after_up", 1)
    each(pairs_of[0], "after_over", 1)
    each(queries, "after_up", 0, light)
    w_forward(3)
    each(pairs_of[0], "after_over", 2)
    each(pairs_of[1], "after_over", 1)
    each(queries, "after_up", 1, light)
    for back in range(3):
        each(queries, "start_over", back, jnp.logical_not(light))
    y_ids.wait()
    place = lax.axis_index("rep")
    ids_all[:, : REACH * CHUNK] = jnp.full((8, REACH * CHUNK), -1, jnp.int32)
    row_end = REACH * CHUNK + ids_ref.shape[1]
    ids_all[:, row_end:] = jnp.full((8, REACH * CHUNK), -2, jnp.int32)
    ids_all[:, REACH * CHUNK : row_end] = jnp.zeros((8, ids_ref.shape[1]), jnp.int32)
    ids_all[0:1, REACH * CHUNK : row_end] = ids_ref[...]
    ids_all[1:2, REACH * CHUNK : row_end] = ids_other[...]
    each(pairs_of[0], "after_twins")
    win_out(0, 0).start()
    win_out(1, 0).start()
    pairs = half // CHUNK
    window = pl.ds((SLOTS - 1 - REACH) * CHUNK, WINDOW)
    own_slot = pl.ds((SLOTS - 1) * CHUNK, CHUNK)
    upper, lower = pl.ds(0, CHUNK), pl.ds(CHUNK, CHUNK)
    mix_copy = (
        remote(sent.at[upper], came.at[lower], mix_sems, (0,), across),
        remote(sent.at[lower], came.at[upper], mix_sems, (1,), across),
    )

    def mix(row):
        rows = pl.ds(CHUNK * row, CHUNK)
        mixed = matmul(attn_ref[rows, :].astype(bf16), w_out_ref[...])
        mixed_ref[rows, :] = mixed
        sent[rows, :] = mixed.astype(bf16)
        mix_copy[row].start()

    def unit(i, unused):
        row, block = i // pairs, i % pairs
        rows, lanes = tile(CHUNK * row, CHUNK, CHUNK), tile(CHUNK * block, CHUNK, CHUNK)
        query = qwin[row, own_slot, lanes] * jnp.bfloat16(HEAD_DIM**-0.5)
        key_block, value_block = kwin[row, window, lanes], vwin[row, window, lanes]
        key_ids = ids_all[:2, tile(CHUNK * place, WINDOW, CHUNK)].astype(f32)
        key_ids = jnp.where(row == 0, key_ids[0:1], key_ids[1:2])
        query_ids = jnp.broadcast_to(key_ids[:, -CHUNK:], (CHUNK, CHUNK)).T[:, :1]
        allowed = (query_ids == key_ids) & (
            iota((CHUNK, WINDOW), 1) <= iota((CHUNK, WINDOW), 0) + REACH * CHUNK
        )
        outs, lses = [], []
        for which in range(2):
            scores = jnp.where(allowed, matmul_nt(head_half(query, which), key_block), NEGATIVE)
            top = jnp.max(scores, axis=-1, keepdims=True)
            probs = jnp.exp(scores - top)
            total = jnp.sum(probs, axis=-1, keepdims=True)
            outs.append(matmul((probs * (1.0 / total)).astype(bf16), value_block))
            lses.append(jnp.broadcast_to(top + jnp.log(total), (CHUNK, CHUNK)))
        attn_ref[rows, lanes] = join_halves(*outs)
        lse_ref[rows, lanes] = join_halves(*lses)
        pl.when(i == 2)(lambda: each(pairs_of[1], "after_over", 2))
        return unused

    lax.fori_loop(0, pairs, unit, 0)
    mix(0)
    each(pairs_of[1], "after_twins")
    win_out(0, 1).start()
    win_out(1, 1).start()
    lax.fori_loop(pairs, 2 * pairs, unit, 0)
    mix(1)
    w_second(3)
    for back in range(3):
        each(queries, "after_over", back)
    each(queries, "after_twins")
    for flow in flows:
        each(flow, "finish")
    for row in range(2):
        win_out(2, row).start()
    for copy in mix_copy:
        copy.wait()
    mixed_ref[...] += came[...].astype(f32)
    w_twin(3).wait_recv()
    w_pass(3).wait_recv()
    for m in range(4):
        w_across(m).wait_send()
        w_over(m).wait_send()
        w_twin(m).wait_send()
        w_pass(m).wait_send()
    y_tok.wait_send()
    for row in range(2):
        for m in range(3):
            win_out(m, row).wait()
    w_out_copy.wait()
    y_cot.wait()


def front(tokens, cotangent, doc_ids, small, w_key, w_value, w_query, w_up, w_out, number):
    dma = pltpu.SemaphoreType.DMA
    bf16 = jnp.bfloat16
    chunk, width = tokens.shape
    half, ff = w_up.shape
    hbm, vmem = pl.BlockSpec(memory_space=pl.ANY), pl.BlockSpec(memory_space=pltpu.VMEM)
    window = jax.ShapeDtypeStruct((2, SLOTS * CHUNK, half), bf16)
    return pl.pallas_call(
        front_kernel,
        out_shape=[
            window,
            window,
            window,
            *[jax.ShapeDtypeStruct((2 * chunk, half), bf16)] * 3,
            jax.ShapeDtypeStruct((2 * chunk, width), bf16),
            jax.ShapeDtypeStruct((chunk, width), bf16),
            jax.ShapeDtypeStruct((chunk, width), bf16),
            jax.ShapeDtypeStruct(doc_ids.shape, jnp.int32),
            jax.ShapeDtypeStruct((small.shape[0], width), bf16),
            jax.ShapeDtypeStruct((3, half, half), bf16),
            jax.ShapeDtypeStruct((half, ff // 2), bf16),
            jax.ShapeDtypeStruct((2 * chunk, half), jnp.float32),
            jax.ShapeDtypeStruct((2 * chunk, half), jnp.float32),
            jax.ShapeDtypeStruct((2 * chunk, width), jnp.float32),
            jax.ShapeDtypeStruct((8, 2 * REACH * CHUNK + doc_ids.shape[1]), jnp.int32),
        ],
        in_specs=[vmem, hbm, vmem, vmem, hbm, hbm, hbm, hbm, vmem],
        out_specs=[hbm] * 3 + [vmem] * 5 + [hbm] + [vmem] * 2 + [hbm] * 2 + [vmem] * 4,
        scratch_shapes=[
            *[pltpu.VMEM(window.shape, bf16)] * 3,
            pltpu.VMEM((3, half, half), bf16),
            pltpu.VMEM((3, half, half), bf16),
            pltpu.VMEM((2 * chunk, width), bf16),
            pltpu.VMEM((2 * chunk, width), bf16),
            pltpu.VMEM((2 * chunk, width), bf16),
            dma((3,)),
            dma((2, 4)),
            dma((2, 4, 4)),
            dma((6, 2, 12)),
            dma((2, 2)),
            dma((4, 2)),
        ],
        compiler_params=pltpu.CompilerParams(
            collective_id=number, has_side_effects=True, vmem_limit_bytes=56 * 2**20
        ),
    )(tokens, cotangent, doc_ids, small, w_key, w_value, w_query, w_up, w_out)


MESH_ID = pl.DeviceIdType.MESH
RING = 8
VEC_ROWS = 16
CHAINS = (
    (0, 160, 640, False),
    (1, 160, 640, False),
    (0, 80, 1280, True),
    (1, 80, 1280, True),
    (0, 80, 640, True),
    (0, 80, 640, True),
    (1, 80, 640, True),
    (1, 80, 640, False),
)
EARLY, LATE = (0, 1, 2, 3), (4, 5, 6, 7)


def device_at(side, level, column, core):
    return (side, (level * 2 + column) * 2 + core)


def ring_device(side, spot, core):
    level = jnp.where(spot < 4, spot, 7 - spot)
    return device_at(side, level, spot // 4, core)


def greet(partners):
    barrier = pltpu.get_barrier_semaphore()
    for partner in partners:
        pl.semaphore_signal(barrier, inc=1, device_id=partner, device_id_type=MESH_ID)
    pl.semaphore_wait(barrier, len(partners))


def tile(first, size, step=16):
    return pl.ds(first if isinstance(first, int) else pl.multiple_of(first, step), size)


def remote(source, target, sems, where, device):
    return pltpu.make_async_remote_copy(
        source,
        target,
        sems.at[(0,) + where],
        sems.at[(1,) + where],
        device_id=device,
        device_id_type=MESH_ID,
    )


class Rings:
    def __init__(self, side, spot_on_ring, core, devices, source_of, result_of, buffers, sems):
        self.side, self.spot, self.core = side, spot_on_ring, core
        self.sibling, self.across, ahead, behind = devices
        self.targets = (ahead, behind)
        self.source_of, self.result_of = source_of, result_of
        self.mine, self.theirs, self.landed, self.swapped = buffers
        (
            self.load_sem,
            self.core_sems,
            self.ring_sems,
            self.back_sems,
            self.share_sems,
            self.swap_sems,
            self.keep_sem,
        ) = sems

    def shard_at(self, chain, offset):
        return (self.spot + RING + (1 - 2 * CHAINS[chain][0]) * offset) % RING

    def load(self, chain, step):
        return pltpu.make_async_copy(
            self.source_of(chain, self.core, self.shard_at(chain, RING - 1 - step)),
            self.mine[chain].at[step % 3],
            self.load_sem.at[chain, step % 3],
        )

    def cross(self, chain, step):
        return remote(
            self.source_of(chain, 1 - self.core, self.shard_at(chain, RING - 1 - step)),
            self.theirs[chain].at[step],
            self.core_sems,
            (chain, step),
            self.sibling,
        )

    def start_inputs(self, chains, step):
        for chain in chains:
            self.load(chain, step).start()
            self.cross(chain, step).start()

    def ring_copy(self, chain, step):
        return remote(
            self.mine[chain].at[step % 3],
            self.landed[chain].at[step],
            self.ring_sems,
            (chain, step),
            self.targets[CHAINS[chain][0]],
        )

    def add(self, chain, step, first=False):
        self.load(chain, step).wait()
        self.cross(chain, step).wait()
        f32 = jnp.float32
        value = self.mine[chain][step % 3].astype(f32) + self.theirs[chain][step].astype(f32)
        if not first:
            value = value + self.landed[chain][step - 1].astype(f32)
        self.mine[chain][step % 3] = value.astype(jnp.bfloat16)

    def begin(self, chains):
        for chain in chains:
            self.add(chain, 0, True)
            self.ring_copy(chain, 0).start()
        self.start_inputs(chains, 2)

    def middle(self, chains, step):
        for chain in chains:
            self.ring_copy(chain, step - 1).wait()

            @pl.when(step < RING - 2)
            def _():
                self.load(chain, step + 2).start()
                self.cross(chain, step + 2).start()

            self.add(chain, step)
            self.ring_copy(chain, step).start()

    def back_copy(self, chain, step, own=False):
        shard = self.shard_at(chain, RING - step)
        return remote(
            self.mine[chain].at[(RING - 1) % 3] if own else self.result_of(chain, shard),
            self.result_of(chain, shard),
            self.back_sems,
            (chain, step),
            self.targets[CHAINS[chain][0]],
        )

    def share(self, chain, step, own=False):
        shard = self.shard_at(chain, RING - step)
        return remote(
            self.mine[chain].at[(RING - 1) % 3] if own else self.result_of(chain, shard),
            self.result_of(chain, shard),
            self.share_sems,
            (chain, step),
            self.sibling,
        )

    def keep(self, chain):
        return pltpu.make_async_copy(
            self.mine[chain].at[(RING - 1) % 3],
            self.result_of(chain, self.spot),
            self.keep_sem.at[chain],
        )

    def publish(self, chain):
        self.back_copy(chain, 0, True).start()
        self.share(chain, 0, True).start()
        self.keep(chain).start()

    def trade(self, chain):
        return remote(
            self.mine[chain].at[(RING - 1) % 3],
            self.swapped[chain],
            self.swap_sems,
            (chain,),
            self.across,
        )

    def last(self, chains):
        for chain in chains:
            self.ring_copy(chain, RING - 2).wait()
            self.add(chain, RING - 1)
            if CHAINS[chain][3]:

                @pl.when(self.core == 1)
                def _():
                    self.trade(chain).start()

                @pl.when(self.core == 0)
                def _():
                    self.publish(chain)

            else:
                self.publish(chain)

    def traded(self, chains):
        for chain in chains:
            if CHAINS[chain][3]:

                @pl.when(self.core == 1)
                def _():
                    self.trade(chain).wait()
                    self.mine[chain][(RING - 1) % 3] = self.swapped[chain][...]
                    self.publish(chain)

    def back_begin(self, chains):
        for chain in chains:
            self.back_copy(chain, 0, True).wait()
            self.back_copy(chain, 1).start()
            self.share(chain, 1).start()

    def back_middle(self, chains, step):
        for chain in chains:
            self.back_copy(chain, step).wait()

            @pl.when(step < RING - 2)
            def _():
                self.back_copy(chain, step + 1).start()

            self.share(chain, step + 1).start()

    def end(self, chains):
        for chain in chains:
            self.keep(chain).wait()
            self.share(chain, 0, True).wait()

        def rest(step, unused):
            for chain in chains:
                self.share(chain, step).wait()
            return unused

        lax.fori_loop(1, RING, rest, 0)


def tail_kernel(
    gdown_ref,
    gup_ref,
    part_two_ref,
    hidden_ref,
    small_ref,
    cot_ref,
    w_out_ref,
    attn_ref,
    lse_ref,
    q_ref,
    k_ref,
    v_ref,
    kwin_ref,
    vwin_ref,
    qwin_ref,
    ids_ref,
    ln_ref,
    wk_ref,
    wv_ref,
    wq_ref,
    w_other_ref,
    x_ref,
    bias_up_ref,
    down_ref,
    sum_down,
    sum_out,
    sum_up,
    sum_query,
    sum_key,
    sum_value,
    vec_out_ref,
    grad_input_ref,
    output_ref,
    *refs,
):
    count = len(CHAINS)
    buffers = [refs[i * count : (i + 1) * count] for i in range(4)]
    (
        dowin,
        statwin,
        sent,
        came,
        grad_hidden,
        grad_mix,
        grad_heads,
        gout,
        gqkv,
        grad_three,
        w_own,
        w_other,
        first_buf,
        second_buf,
        grad_one,
        sums,
        sent_down,
        came_down,
        query_ids,
        key_ids,
        later_ids,
        vec_steps,
        vec_landed,
        block_sem,
        weight_sem,
        y_sems,
        do_sems,
        stat_sems,
        vec_sems,
        *ring_sems,
    ) = refs[4 * count :]
    f32, bf16 = jnp.float32, jnp.bfloat16
    side = lax.axis_index("grp")
    spot = spot_of(lax.axis_index("rep"))
    level, column, core = spot
    on_ring = jnp.where(column == 0, level, 7 - level)
    near_by = neighbours(side, spot)
    across, sibling, over = near_by[:3]
    ahead = ring_device(side, (on_ring + 1) % RING, core)
    behind = ring_device(side, (on_ring + RING - 1) % RING, core)
    near = device_at(side, level + 1 - 2 * (level % 2), column, core)
    far = device_at(side, (level + 2) % 4, column, core)
    vec_partners = (sibling, over, near, far)
    block = side + core - 2 * side * core
    half = w_own.shape[1]
    pairs = half // CHUNK
    own_cols = tile(half * side, half, 128)

    def source_of(chain, which, shard):
        if chain < 2:
            return gdown_ref.at[tile(320 * shard + 160 * chain, 160), tile(640 * which, 640, 128)]
        rows = tile(640 * which + 80 * shard, 80)
        if chain < 4:
            return gup_ref.at[rows, pl.ds(1280 * (chain - 2), 1280)]
        if chain < 7:
            return gqkv.at[rows, pl.ds(640 * (chain - 4), 640)]
        return gout.at[tile(80 * shard, 80), tile(640 * which, 640, 128)]

    def result_of(chain, shard):
        if chain < 2:
            return sum_down.at[tile(320 * shard + 160 * chain, 160), tile(640 * core, 640, 128)]
        rows = tile(80 * shard, 80)
        if chain < 4:
            return sum_up.at[rows, tile(2560 * block + 1280 * (chain - 2), 1280, 128)]
        if chain < 7:
            return (sum_query, sum_key, sum_value)[chain - 4].at[rows, tile(640 * block, 640, 128)]
        return sum_out.at[rows, tile(640 * core, 640, 128)]

    rings = Rings(
        side,
        on_ring,
        core,
        (sibling, across, ahead, behind),
        source_of,
        result_of,
        buffers,
        ring_sems,
    )
    stats = Stream(
        side, spot, True, lambda slot: statwin.at[:, tile(CHUNK * slot, CHUNK, CHUNK)], stat_sems
    )
    grads = Stream(side, spot, True, rows_of(dowin), do_sems)
    streams = (stats, grads)
    own_slot = pl.ds((SLOTS - 1) * CHUNK, CHUNK)
    upper, lower = pl.ds(0, CHUNK), pl.ds(CHUNK, CHUNK)

    def exchange(which):
        return (
            remote(sent.at[lower], came.at[which, upper], y_sems, (which, 0), across),
            remote(sent.at[upper], came.at[which, lower], y_sems, (which, 1), across),
        )

    down_copy = remote(sent_down, came_down, y_sems, (2, 0), across)
    dowin[...] = jnp.zeros_like(dowin)
    statwin[...] = jnp.zeros_like(statwin)
    sent[...] = part_two_ref[...].astype(bf16)
    greet(near_by + far_corners(side, spot) + (far, ahead, behind))
    for copy in exchange(0):
        copy.start()
    sent_down[...] = down_ref[CHUNK:, :].astype(bf16)
    down_copy.start()
    rings.start_inputs(EARLY, 0)
    rings.start_inputs(EARLY, 1)
    weights = (wq_ref, wk_ref, wv_ref)
    weight_loads = [
        pltpu.make_async_copy(weights[m].at[:, own_cols], w_own.at[m], weight_sem.at[m])
        for m in range(3)
    ] + [
        pltpu.make_async_copy(w_other_ref.at[(m + 2) % 3], w_other.at[m], weight_sem.at[3 + m])
        for m in range(3)
    ]
    for copy in weight_loads:
        copy.start()
    rings.begin(EARLY)

    for row in range(2):
        line = slice(row, row + 1)
        first = REACH * CHUNK
        own = ids_ref[line, tile(first + CHUNK * lax.axis_index("rep"), CHUNK, CHUNK)].astype(f32)
        query_ids[row] = jnp.broadcast_to(own, (CHUNK, CHUNK)).T
        key_ids[row] = ids_ref[line, tile(CHUNK * lax.axis_index("rep"), WINDOW, CHUNK)].astype(f32)
        for k in range(REACH + 1):
            at = tile(first + CHUNK * (lax.axis_index("rep") + k), CHUNK, CHUNK)
            later_ids[row, :, (REACH - k) * CHUNK : (REACH + 1 - k) * CHUNK] = ids_ref[
                line, at
            ].astype(f32)

    def back_through_norm(which, part_ref, input_ref, gain_line, base, finish):
        zero = jnp.zeros((8, part_ref.shape[1]), f32)

        def some_rows(i, carry):
            rows = tile(32 * i, 32, 32)
            grad = part_ref[rows, :] + came[which, rows, :].astype(f32)
            inputs = input_ref[rows, :].astype(f32)
            center = inputs - jnp.mean(inputs, axis=-1, keepdims=True)
            inverse = lax.rsqrt(jnp.mean(center * center, axis=-1, keepdims=True) + EPSILON)
            normed = center * inverse
            scaled = grad * small_ref[gain_line : gain_line + 1, :].astype(f32)
            value = inverse * (
                scaled
                - jnp.mean(scaled, axis=-1, keepdims=True)
                - normed * jnp.mean(scaled * normed, axis=-1, keepdims=True)
            )
            extra = finish(rows, value)
            parts = [grad * normed, grad] + extra
            return tuple(
                c + jnp.sum(p.reshape(4, 8, -1), axis=0) for c, p in zip(carry, parts)
            )

        totals = lax.fori_loop(0, 8, some_rows, (zero,) * (3 if base == 0 else 2))
        for k, total in enumerate(totals):
            sums[base + k : base + k + 1, :] = jnp.sum(total, axis=0, keepdims=True)

    def finish_two(rows, value):
        hidden = cot_ref[rows, :].astype(f32) + value
        low = hidden.astype(bf16)
        grad_hidden[rows, :] = hidden
        grad_mix[rows, :] = low
        return [low.astype(f32)]

    rings.middle(EARLY, 1)
    for copy in exchange(0):
        copy.wait()
    back_through_norm(0, part_two_ref, hidden_ref, 4, 0, finish_two)
    grad_heads[...] = matmul_nt(grad_mix[...], w_out_ref[...]).astype(bf16)

    def own_stats(i, unused):
        row, pair = i // pairs, i % pairs
        rows, lanes = tile(CHUNK * row, CHUNK, CHUNK), tile(CHUNK * pair, CHUNK, CHUNK)
        weighed = (grad_heads[rows, lanes].astype(f32) * attn_ref[rows, lanes]).T
        level_of = lse_ref[rows, lanes].T
        zero = jnp.zeros((4, CHUNK), f32)
        statwin[tile(8 * i, 8, 8), own_slot] = jnp.concatenate(
            [
                level_of[:1],
                level_of[HALF_LANES : HALF_LANES + 1],
                jnp.sum(weighed[:HALF_LANES], axis=0, keepdims=True),
                jnp.sum(weighed[HALF_LANES:], axis=0, keepdims=True),
                zero,
            ],
            axis=0,
        )
        return unused

    lax.fori_loop(0, 2 * pairs, own_stats, 0)
    dowin[0, own_slot, :] = grad_heads[:CHUNK, :]
    dowin[1, own_slot, :] = grad_heads[CHUNK:, :]
    for stream in streams:
        stream.start_own()

    window = pl.ds((SLOTS - 1 - REACH) * CHUNK, WINDOW)

    def block_loads(refs_bufs, i):
        row, pair = i // pairs, i % pairs
        lanes = tile(CHUNK * pair, CHUNK, CHUNK)
        return [
            pltpu.make_async_copy(
                ref.at[row, window, lanes], buf.at[i % 2], block_sem.at[k, i % 2]
            )
            for k, (ref, buf) in enumerate(refs_bufs)
        ]

    kv_blocks = ((kwin_ref, first_buf), (vwin_ref, second_buf))
    q_blocks = ((qwin_ref, first_buf),)

    def start_blocks(refs_bufs, i):
        for copy in block_loads(refs_bufs, i):
            copy.start()

    def use_blocks(refs_bufs, i):
        for copy in block_loads(refs_bufs, i):
            copy.wait()
        pl.when(i + 1 < 2 * pairs)(lambda: start_blocks(refs_bufs, i + 1))

    scale = HEAD_DIM**-0.5
    start_blocks(kv_blocks, 0)
    attn_low = attn_ref[...].astype(bf16)
    gout[...] = matmul_tn(attn_low, grad_mix[...]).astype(bf16)

    def query_unit(i, unused):
        row, pair = i // pairs, i % pairs
        rows, lanes = tile(CHUNK * row, CHUNK, CHUNK), tile(CHUNK * pair, CHUNK, CHUNK)
        use_blocks(kv_blocks, i)
        query = q_ref[rows, lanes] * jnp.bfloat16(scale)
        keys, values = first_buf[i % 2], second_buf[i % 2]
        grad = grad_heads[rows, lanes]
        allowed = (query_ids[row][:, :1] == key_ids[row]) & (
            iota((CHUNK, WINDOW), 1) <= iota((CHUNK, WINDOW), 0) + REACH * CHUNK
        )
        weighed = grad.astype(f32) * attn_ref[rows, lanes]
        lse_pair = lse_ref[rows, lanes]
        parts = []
        for which in range(2):
            lse = lse_pair[:, which * HALF_LANES : which * HALF_LANES + 1]
            delta = jnp.sum(head_half(weighed, which), axis=-1, keepdims=True)
            scores = jnp.where(allowed, matmul_nt(head_half(query, which), keys), NEGATIVE)
            probs = jnp.exp(scores - lse)
            grad_probs = matmul_nt(head_half(grad, which), values)
            grad_scores = (probs * (grad_probs - delta)).astype(bf16)
            parts.append(matmul(grad_scores, keys))
        grad_three[0, rows, lanes] = (join_halves(*parts) * scale).astype(bf16)
        events = {
            1: (lambda s: s.after_up(0),),
            5: (lambda s: s.after_over(0), lambda s: s.after_up(1)),
            9: (lambda s: s.after_over(1),),
        }
        for at, what in events.items():

            @pl.when(i == at)
            def _():
                rings.middle(EARLY, 2 + at // 4)
                for event in what:
                    for stream in streams:
                        event(stream)

        return unused

    lax.fori_loop(0, 2 * pairs, query_unit, 0)
    start_blocks(q_blocks, 0)
    rings.middle(EARLY, 5)
    for stream in streams:
        stream.after_over(2)
    for stream in streams:
        stream.after_twins()

    def key_unit(i, unused):
        row, pair = i // pairs, i % pairs
        rows, lanes = tile(CHUNK * row, CHUNK, CHUNK), tile(CHUNK * pair, CHUNK, CHUNK)
        use_blocks(q_blocks, i)
        keys = k_ref[rows, lanes] * jnp.bfloat16(scale)
        values = v_ref[rows, lanes]
        queries = first_buf[i % 2]
        after = dowin[row, window, lanes]
        lane = iota((CHUNK, WINDOW), 1)
        ahead_by = (REACH - lane // CHUNK) * CHUNK + lane % CHUNK
        allowed = (query_ids[row][:, :1] == later_ids[row]) & (ahead_by >= iota((CHUNK, WINDOW), 0))
        lines = statwin[tile(8 * i, 8, 8), window]
        key_parts, value_parts = [], []
        for which in range(2):
            lse, delta = lines[which : which + 1], lines[2 + which : 3 + which]
            scores = jnp.where(allowed, matmul_nt(head_half(keys, which), queries), NEGATIVE)
            probs = jnp.exp(scores - lse)
            value_parts.append(matmul(probs.astype(bf16), after))
            grad_probs = matmul_nt(head_half(values, which), after)
            grad_scores = (probs * (grad_probs - delta)).astype(bf16)
            key_parts.append(matmul(grad_scores, queries))
        grad_three[1, rows, lanes] = (join_halves(*key_parts) * scale).astype(bf16)
        grad_three[2, rows, lanes] = join_halves(*value_parts).astype(bf16)
        pl.when(i == 3)(lambda: rings.middle(EARLY, 6))
        pl.when(i == 8)(lambda: rings.last(EARLY))
        return unused

    lax.fori_loop(0, 2 * pairs, key_unit, 0)
    rings.traded(EARLY)
    for stream in streams:
        stream.finish()

    for copy in weight_loads:
        copy.wait()
    rings.back_begin(EARLY)
    for m in range(3):

        def weight_rows(i, unused):
            lanes = tile(256 * i, 256, 256)
            gqkv[lanes, m * half : (m + 1) * half] = matmul_tn(
                ln_ref[:, lanes], grad_three[m]
            ).astype(bf16)
            return unused

        lax.fori_loop(0, 2 * half // 256, weight_rows, 0)
    rings.start_inputs(LATE, 0)
    rings.start_inputs(LATE, 1)
    rings.begin(LATE)

    own_part, other_part = 0.0, 0.0
    for m in range(3):
        own_part = own_part + matmul_nt(grad_three[m], w_own[m])
        other_part = other_part + matmul_nt(grad_three[m], w_other[m])
    grad_one[:, own_cols] = own_part
    grad_one[:, tile(half * (1 - side), half, 128)] = other_part
    sent[...] = grad_one[...].astype(bf16)
    for copy in exchange(1):
        copy.start()
    for k, m in ((0, 0), (1, 2)):
        sums[6 + k : 7 + k, :half] = jnp.sum(grad_three[m].astype(f32), axis=0, keepdims=True)

    def both_rings(step, unused):
        rings.back_middle(EARLY, step)
        rings.middle(LATE, step)
        return unused

    both_rings(jnp.int32(1), 0)
    for copy in exchange(1):
        copy.wait()

    def finish_one(rows, value):
        grad_hidden[rows, :] = grad_hidden[rows, :] + value
        return []

    back_through_norm(1, grad_one, x_ref, 2, 3, finish_one)
    grad_input_ref[...] = grad_hidden[:CHUNK, :]
    sums[5:6, :] = jnp.sum(cot_ref[...].astype(f32), axis=0, keepdims=True)
    vec_steps[0] = jnp.zeros(vec_steps.shape[1:], f32)
    for k in range(4):
        vec_steps[0, 3 + k : 4 + k, :] = bias_up_ref[:1, k * half : (k + 1) * half]
    for row, (line, cols) in {
        0: (6, pl.ds(0, half)),
        1: (7, pl.ds(0, half)),
        2: (2, own_cols),
        7: (5, own_cols),
        8: (3, own_cols),
        9: (4, own_cols),
        10: (0, own_cols),
        11: (1, own_cols),
    }.items():
        vec_steps[0, row : row + 1, :] = sums[line : line + 1, cols]
    vec_copy = [
        remote(vec_steps.at[k], vec_landed.at[k], vec_sems, (k,), vec_partners[k])
        for k in range(4)
    ]
    vec_copy[0].start()
    for k in range(4):
        both_rings(jnp.int32(2 + k), 0)
        vec_copy[k].wait()
        vec_steps[k + 1] = vec_steps[k] + vec_landed[k]
        if k < 3:
            vec_copy[k + 1].start()
    vec_out_ref[...] = vec_steps[4]
    both_rings(jnp.int32(6), 0)
    rings.last(LATE)
    rings.end(EARLY)
    down_copy.wait()
    output_ref[...] = (
        hidden_ref[:CHUNK, :]
        + down_ref[:CHUNK, :]
        + came_down[...].astype(f32)
        + small_ref[1:2, :].astype(f32)
    ).astype(bf16)
    rings.traded(LATE)
    rings.back_begin(LATE)

    def late_back(step, unused):
        rings.back_middle(LATE, step)
        return unused

    lax.fori_loop(1, RING - 1, late_back, 0)
    rings.end(LATE)


def tail(operands, width, half, ff, number):
    dma = pltpu.SemaphoreType.DMA
    f32, bf16 = jnp.float32, jnp.bfloat16
    count = len(CHAINS)
    rows = operands[3].shape[0]
    hbm, vmem = pl.BlockSpec(memory_space=pl.ANY), pl.BlockSpec(memory_space=pltpu.VMEM)
    in_hbm = (0, 1, 12, 13, 14, 17, 18, 19, 20)
    square = jax.ShapeDtypeStruct((half, width), bf16)

    def room(depth):
        return [pltpu.VMEM(depth + (tall, wide), bf16) for _, tall, wide, _ in CHAINS]

    return pl.pallas_call(
        tail_kernel,
        out_shape=[
            jax.ShapeDtypeStruct((ff, width), bf16),
            square,
            jax.ShapeDtypeStruct((half, 2 * ff), bf16),
            square,
            square,
            square,
            jax.ShapeDtypeStruct((VEC_ROWS, half), f32),
            jax.ShapeDtypeStruct((CHUNK, width), f32),
            jax.ShapeDtypeStruct((CHUNK, width), bf16),
        ],
        in_specs=[hbm if i in in_hbm else vmem for i in range(len(operands))],
        out_specs=[hbm] * 6 + [vmem] * 3,
        scratch_shapes=[
            *room((3,)),
            *room((RING,)),
            *room((RING - 1,)),
            *room(()),
            pltpu.VMEM((2, SLOTS * CHUNK, half), bf16),
            pltpu.VMEM((16 * half // CHUNK, SLOTS * CHUNK), f32),
            pltpu.VMEM((rows, width), bf16),
            pltpu.VMEM((2, rows, width), bf16),
            pltpu.VMEM((rows, width), f32),
            pltpu.VMEM((rows, width), bf16),
            pltpu.VMEM((rows, half), bf16),
            pltpu.VMEM((half, width), bf16),
            pltpu.VMEM((width, 3 * half), bf16),
            pltpu.VMEM((3, rows, half), bf16),
            pltpu.VMEM((3, half, half), bf16),
            pltpu.VMEM((3, half, half), bf16),
            pltpu.VMEM((2, WINDOW, CHUNK), bf16),
            pltpu.VMEM((2, WINDOW, CHUNK), bf16),
            pltpu.VMEM((rows, width), f32),
            pltpu.VMEM((8, width), f32),
            pltpu.VMEM((CHUNK, width), bf16),
            pltpu.VMEM((CHUNK, width), bf16),
            pltpu.VMEM((2, CHUNK, CHUNK), f32),
            pltpu.VMEM((2, 1, WINDOW), f32),
            pltpu.VMEM((2, 1, WINDOW), f32),
            pltpu.VMEM((5, VEC_ROWS, half), f32),
            pltpu.VMEM((4, VEC_ROWS, half), f32),
            dma((2, 2)),
            dma((6,)),
            dma((2, 3, 2)),
            dma((2, 12)),
            dma((2, 12)),
            dma((2, 4)),
            dma((count, 3)),
            dma((2, count, RING)),
            dma((2, count, RING - 1)),
            dma((2, count, RING - 1)),
            dma((2, count, RING)),
            dma((2, count)),
            dma((count,)),
        ],
        compiler_params=pltpu.CompilerParams(
            collective_id=number, has_side_effects=True, vmem_limit_bytes=60 * 2**20
        ),
    )(*operands)


FF_BLOCK = 512


def ff_kernel(
    side_ref,
    tok_ref,
    tok_other_ref,
    mixed_ref,
    small_ref,
    cot_ref,
    cot_other_ref,
    up_own_ref,
    up_other_ref,
    down_ref,
    bias_ref,
    hidden_ref,
    x_ref,
    cot_all_ref,
    result_ref,
    back_ref,
    grad_up_ref,
    grad_down_ref,
    grad_bias_ref,
    ln_ref,
    own_first,
    turned,
):
    f32, bf16 = jnp.float32, jnp.bfloat16
    side = side_ref[0]
    step = pl.program_id(0)
    chunk, width = tok_ref.shape
    half = width // 2
    own_cols, other_cols = tile(half * side, half, 128), tile(half * (1 - side), half, 128)

    @pl.when(step == 0)
    def _():
        x_ref[:chunk, :] = tok_ref[...]
        x_ref[chunk:, :] = tok_other_ref[...]
        cot_all_ref[:chunk, :] = cot_ref[...]
        cot_all_ref[chunk:, :] = cot_other_ref[...]

        def some_rows(i, unused):
            rows = tile(32 * i, 32, 32)
            hidden = x_ref[rows, :].astype(f32) + mixed_ref[rows, :] + small_ref[:1, :].astype(f32)
            hidden_ref[rows, :] = hidden
            normed, _ = norm_rows(hidden)
            ln_ref[rows, :] = (
                normed * small_ref[4:5, :].astype(f32) + small_ref[5:6, :].astype(f32)
            ).astype(bf16)
            return unused

        lax.fori_loop(0, 2 * chunk // 32, some_rows, 0)
        own_first[:, :half] = ln_ref[:, own_cols]
        own_first[:, half:] = ln_ref[:, other_cols]
        turned[...] = own_first[...].T
        result_ref[...] = jnp.zeros_like(result_ref)
        back_ref[...] = jnp.zeros_like(back_ref)

    pre_act = (
        matmul(own_first[:, :half], up_own_ref[...])
        + matmul(own_first[:, half:], up_other_ref[...])
        + bias_ref[...].astype(f32)
    )
    value, slope = gelu_pair(pre_act)
    act = value.astype(bf16)
    cot = cot_all_ref[...]
    result_ref[...] += matmul(act, down_ref[...])
    grad_pre = (matmul_nt(cot, down_ref[...]) * slope).astype(bf16)
    grad_bias_ref[...] = jnp.sum(grad_pre.astype(f32), axis=0, keepdims=True)
    grad_down_ref[...] = matmul_tn(act, cot).astype(bf16)
    grad_up_ref[...] = matmul(turned[...], grad_pre).astype(bf16)
    back_ref[:, own_cols] += matmul_nt(grad_pre, up_own_ref[...])
    back_ref[:, other_cols] += matmul_nt(grad_pre, up_other_ref[...])


def feed_forward(side, tokens, tok_other, mixed, small, cotangent, cot_other, w_up, up_other, w_down, b_up):
    f32, bf16 = jnp.float32, jnp.bfloat16
    chunk, width = tokens.shape
    half = width // 2
    ff = w_down.shape[0]
    steps = ff // FF_BLOCK

    def whole(shape):
        return pl.BlockSpec(shape, lambda j, s: (0, 0))

    rows = 2 * chunk
    columns = pl.BlockSpec((half, FF_BLOCK), lambda j, s: (0, j))
    return pl.pallas_call(
        ff_kernel,
        grid_spec=pltpu.PrefetchScalarGridSpec(
            num_scalar_prefetch=1,
            grid=(steps,),
            in_specs=[
                whole((chunk, width)),
                whole((chunk, width)),
                whole((rows, width)),
                whole(small.shape),
                whole((chunk, width)),
                whole((chunk, width)),
                pl.BlockSpec((half, FF_BLOCK), lambda j, s: (0, s[0] * steps + j)),
                columns,
                pl.BlockSpec((FF_BLOCK, width), lambda j, s: (j, 0)),
                pl.BlockSpec((1, FF_BLOCK), lambda j, s: (0, j)),
            ],
            out_specs=[
                whole((rows, width)),
                whole((rows, width)),
                whole((rows, width)),
                whole((rows, width)),
                whole((rows, width)),
                pl.BlockSpec((width, FF_BLOCK), lambda j, s: (0, j)),
                pl.BlockSpec((FF_BLOCK, width), lambda j, s: (j, 0)),
                pl.BlockSpec((1, FF_BLOCK), lambda j, s: (0, j)),
            ],
            scratch_shapes=[
                pltpu.VMEM((rows, width), bf16),
                pltpu.VMEM((rows, width), bf16),
                pltpu.VMEM((width, rows), bf16),
            ],
        ),
        out_shape=[
            jax.ShapeDtypeStruct((rows, width), f32),
            jax.ShapeDtypeStruct((rows, width), bf16),
            jax.ShapeDtypeStruct((rows, width), bf16),
            jax.ShapeDtypeStruct((rows, width), f32),
            jax.ShapeDtypeStruct((rows, width), f32),
            jax.ShapeDtypeStruct((width, ff), bf16),
            jax.ShapeDtypeStruct((ff, width), bf16),
            jax.ShapeDtypeStruct((1, ff), f32),
        ],
        compiler_params=pltpu.CompilerParams(vmem_limit_bytes=56 * 2**20),
    )(
        side.reshape(1).astype(jnp.int32),
        tokens,
        tok_other,
        mixed,
        small,
        cotangent,
        cot_other,
        w_up,
        up_other,
        w_down,
        b_up.reshape(1, -1),
    )


def widen_kernel(*refs):
    count = len(refs) // 2
    for source, target in zip(refs[:count], refs[count:]):
        target[...] = source[...].astype(jnp.float32)


def widen(arrays):
    steps = 4
    specs = [
        pl.BlockSpec((a.shape[0] // steps, a.shape[1]), lambda j: (j, 0)) for a in arrays
    ]
    return pl.pallas_call(
        widen_kernel,
        grid=(steps,),
        in_specs=specs,
        out_specs=specs,
        out_shape=[jax.ShapeDtypeStruct(a.shape, jnp.float32) for a in arrays],
        compiler_params=pltpu.CompilerParams(vmem_limit_bytes=56 * 2**20),
    )(*arrays)


def pair_shards(
    tokens,
    doc_ids,
    w_query,
    w_key,
    w_value,
    w_out,
    w_up,
    w_down,
    b_query,
    b_value,
    b_out,
    b_up,
    b_down,
    attn_gain,
    attn_beta,
    ffn_gain,
    ffn_beta,
    cotangent,
):
    f32, bf16 = jnp.float32, jnp.bfloat16
    chunk, width = tokens.shape
    half = width // 2
    side = lax.axis_index("grp")
    row_of_small = lax.broadcasted_iota(jnp.int32, (16, half), 0)
    small = jnp.zeros((16, half), bf16)
    for line, vector in enumerate(
        (b_out, b_down, attn_gain, attn_beta, ffn_gain, ffn_beta, b_query, b_value)
    ):
        small = jnp.where(row_of_small == line, vector[None, :], small)
    (
        k_win,
        v_win,
        q_win,
        k_own,
        v_own,
        q_own,
        ln_one,
        tok_other,
        cot_other,
        ids_other,
        small,
        w_other,
        w_up_other,
        attn,
        lse,
        mixed,
        ids,
    ) = front(tokens, cotangent, doc_ids, small, w_key, w_value, w_query, w_up, w_out, 2)
    hidden, x_all, cot_all, down, back_two, grad_w_up, grad_w_down, grad_b_up = feed_forward(
        side, tokens, tok_other, mixed, small, cotangent, cot_other, w_up, w_up_other, w_down, b_up
    )
    *sums, vec_sum, grad_input, output = tail(
        (
            grad_w_down,
            grad_w_up,
            back_two,
            hidden,
            small,
            cot_all,
            w_out,
            attn,
            lse,
            q_own,
            k_own,
            v_own,
            k_win,
            v_win,
            q_win,
            ids,
            ln_one,
            w_key,
            w_value,
            w_query,
            w_other,
            x_all,
            grad_b_up,
            down,
        ),
        width,
        half,
        w_down.shape[0],
        1,
    )
    sum_down, sum_out, sum_up, sum_query, sum_key, sum_value = widen(sums)
    cuts = [
        vec_sum[at : at + size].reshape(-1)
        for at, size in ((0, 1), (1, 1), (2, 1), (3, 4), (7, 1), (8, 1), (9, 1), (10, 1), (11, 1))
    ]
    return (
        output,
        grad_input,
        sum_query,
        sum_key,
        sum_value,
        sum_out,
        sum_up,
        sum_down,
        *cuts,
    )


def solution(mesh):
    in_specs = (
        P(("grp", "rep"), None),
        P("grp", None),
        P("grp", None),
        P("grp", None),
        P("grp", None),
        P("grp", None),
        P("grp", None),
        P("grp", None),
        P("grp"),
        P("grp"),
        P("grp"),
        P("grp"),
        P("grp"),
        P("grp"),
        P("grp"),
        P("grp"),
        P("grp"),
        P(("grp", "rep"), None),
    )
    out_specs = (
        P(("grp", "rep"), None),
        P(("grp", "rep"), None),
        P("grp", None),
        P("grp", None),
        P("grp", None),
        P("grp", None),
        P("grp", None),
        P("grp", None),
        P("grp"),
        P("grp"),
        P("grp"),
        P("grp"),
        P("grp"),
        P("grp"),
        P("grp"),
        P("grp"),
        P("grp"),
    )
    plan = pair_shards if fits_pair(mesh) else shards
    return jax.shard_map(plan, mesh=mesh, in_specs=in_specs, out_specs=out_specs, check_vma=False)
```

```python
import jax
import jax.numpy as jnp
from jax import lax
from jax.experimental import pallas as pl
from jax.experimental.pallas import tpu as pltpu
from jax.sharding import PartitionSpec as P

HEADS = 20
HEAD_DIM = 64
PAIRS = 4


EPSILON = 1e-05
NEGATIVE = -1e30
GELU_SCALE = 0.7978845608028654
GELU_CUBIC = 0.044715


def from_behind(array, axis, by):
    length = lax.axis_size(axis)
    pairs = [(i, i + by) for i in range(length) if 0 <= i + by < length]
    return lax.ppermute(array, axis, pairs)


def passed_along(block, axis, distance):
    devices = range(lax.axis_size(axis))
    route = [((i - distance) % len(devices), i) for i in devices]
    return lax.ppermute(block, axis, route)


def norm_rows(values):
    center = values - jnp.mean(values, axis=-1, keepdims=True)
    inverse = lax.rsqrt(jnp.mean(center * center, axis=-1, keepdims=True) + EPSILON)
    return (center * inverse, inverse)


def norm_grad(grad_norm, normed, inverse, gain):
    scaled = grad_norm * gain
    return inverse * (
        scaled
        - jnp.mean(scaled, axis=-1, keepdims=True)
        - normed * jnp.mean(scaled * normed, axis=-1, keepdims=True)
    )


def gelu_pair(inputs):
    inner = jnp.tanh(GELU_SCALE * (inputs + GELU_CUBIC * inputs * inputs * inputs))
    value = 0.5 * inputs * (1.0 + inner)
    slope = 0.5 * (1.0 + inner) + 0.5 * inputs * (1.0 - inner * inner) * GELU_SCALE * (
        1.0 + 3.0 * GELU_CUBIC * inputs * inputs
    )
    return (value, slope)


def matmul(left, right):
    return jnp.dot(left, right, preferred_element_type=jnp.float32)


def matmul_tn(left, right):
    return lax.dot_general(
        left, right, (((0,), (0,)), ((), ())), preferred_element_type=jnp.float32
    )


def matmul_nt(left, right):
    return lax.dot_general(
        left, right, (((1,), (1,)), ((), ())), preferred_element_type=jnp.float32
    )


def shards(
    tokens,
    doc_ids,
    w_query,
    w_key,
    w_value,
    w_out,
    w_up,
    w_down,
    b_query,
    b_value,
    b_out,
    b_up,
    b_down,
    attn_gain,
    attn_beta,
    ffn_gain,
    ffn_beta,
    cotangent,
):
    tok_dev = tokens.shape[0]
    width = tokens.shape[1]
    scale = HEAD_DIM ** (-0.5)
    (
        full_query,
        full_key,
        full_value,
        full_out,
        full_up,
        full_down,
        bias_query,
        bias_value,
        bias_out,
        bias_up,
        bias_down,
        gain_attn,
        beta_attn,
        gain_ffn,
        beta_ffn,
    ) = (
        lax.all_gather(w_query, "grp", axis=0, tiled=True),
        lax.all_gather(w_key, "grp", axis=0, tiled=True),
        lax.all_gather(w_value, "grp", axis=0, tiled=True),
        lax.all_gather(w_out, "grp", axis=0, tiled=True),
        lax.all_gather(w_up, "grp", axis=0, tiled=True),
        lax.all_gather(w_down, "grp", axis=0, tiled=True),
        lax.all_gather(b_query, "grp", axis=0, tiled=True),
        lax.all_gather(b_value, "grp", axis=0, tiled=True),
        lax.all_gather(b_out, "grp", axis=0, tiled=True),
        lax.all_gather(b_up, "grp", axis=0, tiled=True),
        lax.all_gather(b_down, "grp", axis=0, tiled=True),
        lax.all_gather(attn_gain, "grp", axis=0, tiled=True),
        lax.all_gather(attn_beta, "grp", axis=0, tiled=True),
        lax.all_gather(ffn_gain, "grp", axis=0, tiled=True),
        lax.all_gather(ffn_beta, "grp", axis=0, tiled=True),
    )
    rep_index = lax.axis_index("rep")
    pad_front = (2 * PAIRS + 1) * tok_dev
    row_ids = doc_ids[0]
    padded_ids = jnp.concatenate([jnp.full((pad_front,), -1, jnp.int32), row_ids])
    query_pos = rep_index * tok_dev + jnp.arange(tok_dev, dtype=jnp.int32)
    query_doc = lax.dynamic_slice_in_dim(row_ids, rep_index * tok_dev, tok_dev)

    def block_mask(block_index):
        first = (rep_index - 2 * block_index - 1) * tok_dev
        key_pos = first + jnp.arange(2 * tok_dev, dtype=jnp.int32)
        key_doc = lax.dynamic_slice_in_dim(padded_ids, first + pad_front, 2 * tok_dev)
        return (key_doc[None, :] == query_doc[:, None]) & (key_pos[None, :] <= query_pos[:, None])

    xfull = tokens.astype(jnp.float32)
    normed_one, inverse_one = norm_rows(xfull)
    ln_one = (normed_one * gain_attn.astype(jnp.float32) + beta_attn.astype(jnp.float32)).astype(
        jnp.bfloat16
    )
    query = (matmul(ln_one, full_query) + bias_query.astype(jnp.float32)).astype(jnp.bfloat16)
    keys = matmul(ln_one, full_key).astype(jnp.bfloat16)
    values = (matmul(ln_one, full_value) + bias_value.astype(jnp.float32)).astype(jnp.bfloat16)
    query_heads = query.reshape(tok_dev, HEADS, HEAD_DIM)
    earlier = from_behind((keys, values), "rep", 1)
    first_block = (
        jnp.concatenate([earlier[0], keys], axis=0),
        jnp.concatenate([earlier[1], values], axis=0),
    )

    def fetch_pair(block, unused):
        moved = from_behind((block[0], block[1]), "rep", 2)
        return (moved, moved)

    unused_end, following = lax.scan(fetch_pair, first_block, None, length=PAIRS)
    key_blocks = jnp.concatenate([first_block[0][None], following[0]], axis=0)
    value_blocks = jnp.concatenate([first_block[1][None], following[1]], axis=0)
    block_numbers = jnp.arange(PAIRS + 1, dtype=jnp.int32)

    def scores_of(block_keys, block_index):
        raw = (
            jnp.einsum(
                "qhd,khd->hqk",
                query_heads,
                block_keys.reshape(-1, HEADS, HEAD_DIM),
                preferred_element_type=jnp.float32,
            )
            * scale
        )
        return jnp.where(block_mask(block_index)[None], raw, NEGATIVE)

    def max_step(state, inputs):
        run_max, run_sum = state
        block_keys, block_index = inputs
        scores = scores_of(block_keys, block_index)
        new_max = jnp.maximum(run_max, jnp.max(scores, axis=-1))
        run_sum = run_sum * jnp.exp(run_max - new_max) + jnp.sum(
            jnp.exp(scores - new_max[..., None]), axis=-1
        )
        return ((new_max, run_sum), None)

    start_state = (
        jnp.full((HEADS, tok_dev), NEGATIVE, jnp.float32),
        jnp.zeros((HEADS, tok_dev), jnp.float32),
    )
    (top_score, total_exp), unused_max = lax.scan(
        max_step, start_state, (key_blocks, block_numbers)
    )
    log_total = top_score + jnp.log(total_exp)

    def value_step(total, inputs):
        block_keys, block_values, block_index = inputs
        probs = jnp.exp(scores_of(block_keys, block_index) - log_total[..., None]).astype(
            jnp.bfloat16
        )
        return (
            total
            + jnp.einsum(
                "hqk,khd->qhd",
                probs,
                block_values.reshape(-1, HEADS, HEAD_DIM),
                preferred_element_type=jnp.float32,
            ),
            None,
        )

    attn, unused_value = lax.scan(
        value_step,
        jnp.zeros((tok_dev, HEADS, HEAD_DIM), jnp.float32),
        (key_blocks, value_blocks, block_numbers),
    )
    attn_low = attn.reshape(tok_dev, width).astype(jnp.bfloat16)
    hidden = xfull + matmul(attn_low, full_out) + bias_out.astype(jnp.float32)
    normed_two, inverse_two = norm_rows(hidden)
    ln_two = (normed_two * gain_ffn.astype(jnp.float32) + beta_ffn.astype(jnp.float32)).astype(
        jnp.bfloat16
    )
    pre_act = matmul(ln_two, full_up) + bias_up.astype(jnp.float32)
    act_value, act_slope = gelu_pair(pre_act)
    act_low = act_value.astype(jnp.bfloat16)
    result = hidden + matmul(act_low, full_down) + bias_down.astype(jnp.float32)
    output = result.astype(jnp.bfloat16)
    (
        back_query,
        back_key,
        back_value,
        back_out,
        back_up,
        back_down,
        back_gain_attn,
        back_gain_ffn,
    ) = (
        lax.all_gather(w_query, "grp", axis=0, tiled=True),
        lax.all_gather(w_key, "grp", axis=0, tiled=True),
        lax.all_gather(w_value, "grp", axis=0, tiled=True),
        lax.all_gather(w_out, "grp", axis=0, tiled=True),
        lax.all_gather(w_up, "grp", axis=0, tiled=True),
        lax.all_gather(w_down, "grp", axis=0, tiled=True),
        lax.all_gather(attn_gain, "grp", axis=0, tiled=True),
        lax.all_gather(ffn_gain, "grp", axis=0, tiled=True),
    )
    grad_res = cotangent.astype(jnp.float32)
    grad_w_down = matmul_tn(act_low, cotangent)
    grad_b_down = jnp.sum(grad_res, axis=0)
    grad_pre = (matmul_nt(cotangent, back_down) * act_slope).astype(jnp.bfloat16)
    grad_w_up = matmul_tn(ln_two, grad_pre)
    grad_b_up = jnp.sum(grad_pre.astype(jnp.float32), axis=0)
    grad_ln_two = matmul_nt(grad_pre, back_up)
    grad_ffn_gain = jnp.sum(grad_ln_two * normed_two, axis=0)
    grad_ffn_beta = jnp.sum(grad_ln_two, axis=0)
    grad_hidden = grad_res + norm_grad(
        grad_ln_two, normed_two, inverse_two, back_gain_ffn.astype(jnp.float32)
    )
    grad_mix = grad_hidden.astype(jnp.bfloat16)
    grad_w_out = matmul_tn(attn_low, grad_mix)
    grad_b_out = jnp.sum(grad_mix.astype(jnp.float32), axis=0)
    grad_heads = (
        matmul_nt(grad_mix, back_out).astype(jnp.bfloat16).reshape(tok_dev, HEADS, HEAD_DIM)
    )
    delta = jnp.sum(grad_heads.astype(jnp.float32) * attn, axis=-1).T

    def block_grads(block_keys, block_values, block_index):
        probs = jnp.exp(scores_of(block_keys, block_index) - log_total[..., None])
        key_heads = block_keys.reshape(-1, HEADS, HEAD_DIM)
        value_heads = block_values.reshape(-1, HEADS, HEAD_DIM)
        grad_probs = jnp.einsum(
            "qhd,khd->hqk", grad_heads, value_heads, preferred_element_type=jnp.float32
        )
        grad_scores = (probs * (grad_probs - delta[..., None])).astype(jnp.bfloat16)
        part_query = (
            jnp.einsum("hqk,khd->qhd", grad_scores, key_heads, preferred_element_type=jnp.float32)
            * scale
        )
        part_key = (
            jnp.einsum("hqk,qhd->khd", grad_scores, query_heads, preferred_element_type=jnp.float32)
            * scale
        )
        part_value = jnp.einsum(
            "hqk,qhd->khd",
            probs.astype(jnp.bfloat16),
            grad_heads,
            preferred_element_type=jnp.float32,
        )
        return (part_query, part_key, part_value)

    again = from_behind((keys, values), "rep", 1)
    back_block = (
        jnp.concatenate([again[0], keys], axis=0),
        jnp.concatenate([again[1], values], axis=0),
    )
    query_sum, key_acc, value_acc = block_grads(back_block[0], back_block[1], 0)

    def travel_step(carry, inputs):
        query_total, key_total, value_total, block_keys, block_values = carry
        block_index, kept_keys, kept_values = inputs
        block_keys, block_values = from_behind((block_keys, block_values), "rep", 2)
        key_total, value_total = (
            passed_along(key_total.astype(jnp.bfloat16), "rep", 2).astype(key_total.dtype),
            passed_along(value_total.astype(jnp.bfloat16), "rep", 2).astype(value_total.dtype),
        )
        part_query, part_key, part_value = block_grads(block_keys, block_values, block_index)
        return (
            (
                query_total + part_query,
                key_total + part_key,
                value_total + part_value,
                block_keys,
                block_values,
            ),
            None,
        )

    carry_end, unused_travel = lax.scan(
        travel_step,
        (query_sum, key_acc, value_acc, back_block[0], back_block[1]),
        (block_numbers[1:], key_blocks[1:], value_blocks[1:]),
    )
    query_sum, key_acc, value_acc = (carry_end[0], carry_end[1], carry_end[2])
    from_next = (
        passed_along(key_acc[:tok_dev].astype(jnp.bfloat16), "rep", -1).astype(jnp.float32),
        passed_along(value_acc[:tok_dev].astype(jnp.bfloat16), "rep", -1).astype(jnp.float32),
    )
    joined_key = key_acc[tok_dev:] + from_next[0]
    joined_value = value_acc[tok_dev:] + from_next[1]
    returned = (
        passed_along(joined_key.astype(jnp.bfloat16), "rep", -2 * PAIRS).astype(joined_key.dtype),
        passed_along(joined_value.astype(jnp.bfloat16), "rep", -2 * PAIRS).astype(
            joined_value.dtype
        ),
    )
    grad_query_low = query_sum.reshape(tok_dev, width).astype(jnp.bfloat16)
    grad_key_low = returned[0].reshape(tok_dev, width).astype(jnp.bfloat16)
    grad_value_low = returned[1].reshape(tok_dev, width).astype(jnp.bfloat16)
    grad_w_query = matmul_tn(ln_one, grad_query_low)
    grad_b_query = jnp.sum(grad_query_low.astype(jnp.float32), axis=0)
    grad_w_key = matmul_tn(ln_one, grad_key_low)
    grad_w_value = matmul_tn(ln_one, grad_value_low)
    grad_b_value = jnp.sum(grad_value_low.astype(jnp.float32), axis=0)
    grad_ln_one = (
        matmul_nt(grad_query_low, back_query)
        + matmul_nt(grad_key_low, back_key)
        + matmul_nt(grad_value_low, back_value)
    )
    grad_attn_gain = jnp.sum(grad_ln_one * normed_one, axis=0)
    grad_attn_beta = jnp.sum(grad_ln_one, axis=0)
    grad_input = grad_hidden + norm_grad(
        grad_ln_one, normed_one, inverse_one, back_gain_attn.astype(jnp.float32)
    )
    shares = (
        lax.psum_scatter(
            grad_w_query.astype(jnp.bfloat16), "grp", scatter_dimension=0, tiled=True
        ).astype(jnp.float32),
        lax.psum_scatter(
            grad_w_key.astype(jnp.bfloat16), "grp", scatter_dimension=0, tiled=True
        ).astype(jnp.float32),
        lax.psum_scatter(
            grad_w_value.astype(jnp.bfloat16), "grp", scatter_dimension=0, tiled=True
        ).astype(jnp.float32),
        lax.psum_scatter(
            grad_w_out.astype(jnp.bfloat16), "grp", scatter_dimension=0, tiled=True
        ).astype(jnp.float32),
        lax.psum_scatter(
            grad_w_up.astype(jnp.bfloat16), "grp", scatter_dimension=0, tiled=True
        ).astype(jnp.float32),
        lax.psum_scatter(
            grad_w_down.astype(jnp.bfloat16), "grp", scatter_dimension=0, tiled=True
        ).astype(jnp.float32),
        lax.psum_scatter(
            grad_b_query.astype(jnp.bfloat16), "grp", scatter_dimension=0, tiled=True
        ).astype(jnp.float32),
        lax.psum_scatter(
            grad_b_value.astype(jnp.bfloat16), "grp", scatter_dimension=0, tiled=True
        ).astype(jnp.float32),
        lax.psum_scatter(
            grad_b_out.astype(jnp.bfloat16), "grp", scatter_dimension=0, tiled=True
        ).astype(jnp.float32),
        lax.psum_scatter(
            grad_b_up.astype(jnp.bfloat16), "grp", scatter_dimension=0, tiled=True
        ).astype(jnp.float32),
        lax.psum_scatter(
            grad_b_down.astype(jnp.bfloat16), "grp", scatter_dimension=0, tiled=True
        ).astype(jnp.float32),
        lax.psum_scatter(
            grad_attn_gain.astype(jnp.bfloat16), "grp", scatter_dimension=0, tiled=True
        ).astype(jnp.float32),
        lax.psum_scatter(
            grad_attn_beta.astype(jnp.bfloat16), "grp", scatter_dimension=0, tiled=True
        ).astype(jnp.float32),
        lax.psum_scatter(
            grad_ffn_gain.astype(jnp.bfloat16), "grp", scatter_dimension=0, tiled=True
        ).astype(jnp.float32),
        lax.psum_scatter(
            grad_ffn_beta.astype(jnp.bfloat16), "grp", scatter_dimension=0, tiled=True
        ).astype(jnp.float32),
    )
    totals = (
        lax.psum(shares[0].astype(jnp.bfloat16), "rep").astype(jnp.float32),
        lax.psum(shares[1].astype(jnp.bfloat16), "rep").astype(jnp.float32),
        lax.psum(shares[2].astype(jnp.bfloat16), "rep").astype(jnp.float32),
        lax.psum(shares[3].astype(jnp.bfloat16), "rep").astype(jnp.float32),
        lax.psum(shares[4].astype(jnp.bfloat16), "rep").astype(jnp.float32),
        lax.psum(shares[5].astype(jnp.bfloat16), "rep").astype(jnp.float32),
        lax.psum(shares[6].astype(jnp.bfloat16), "rep").astype(jnp.float32),
        lax.psum(shares[7].astype(jnp.bfloat16), "rep").astype(jnp.float32),
        lax.psum(shares[8].astype(jnp.bfloat16), "rep").astype(jnp.float32),
        lax.psum(shares[9].astype(jnp.bfloat16), "rep").astype(jnp.float32),
        lax.psum(shares[10].astype(jnp.bfloat16), "rep").astype(jnp.float32),
        lax.psum(shares[11].astype(jnp.bfloat16), "rep").astype(jnp.float32),
        lax.psum(shares[12].astype(jnp.bfloat16), "rep").astype(jnp.float32),
        lax.psum(shares[13].astype(jnp.bfloat16), "rep").astype(jnp.float32),
        lax.psum(shares[14].astype(jnp.bfloat16), "rep").astype(jnp.float32),
    )
    return (
        output,
        grad_input,
        totals[0],
        totals[1],
        totals[2],
        totals[3],
        totals[4],
        totals[5],
        totals[6],
        totals[7],
        totals[8],
        totals[9],
        totals[10],
        totals[11],
        totals[12],
        totals[13],
        totals[14],
    )


def fits_pair(mesh):
    return mesh.shape["grp"] == 2 and mesh.shape["rep"] == 16


REACH = 9
CHUNK = 128
WINDOW = (REACH + 1) * CHUNK
HALF_LANES = 64


def iota(shape, dim):
    return lax.broadcasted_iota(jnp.int32, shape, dim)


def head_half(block, which):
    first = iota(block.shape, 1) < HALF_LANES
    return jnp.where(first if which == 0 else jnp.logical_not(first), block, jnp.zeros_like(block))


def join_halves(first, second):
    return jnp.where(iota(first.shape, 1) < HALF_LANES, first, second)


SLOTS = 12
LEVELS = 4


class Stream:
    def __init__(self, side, spot, mirrored, view, sems):
        self.side, self.mirrored, self.view, self.sems = side, mirrored, view, sems
        level, column, core = spot
        if mirrored:
            level, column, core = LEVELS - 1 - level, 1 - column, 1 - core
        self.level, self.column, self.core = level, column, core

    def device(self, level, column, core):
        if self.mirrored:
            level, column, core = LEVELS - 1 - level, 1 - column, 1 - core
        return device_at(self.side, level, column, core)

    def slot(self, holder, chunk):
        gaps = [c - h for c, h in zip(chunk, holder)]
        return SLOTS - 1 + 4 * gaps[0] + 2 * gaps[1] + gaps[2]

    def copy(self, kind, chunk, target):
        me = (self.level, self.column, self.core)
        return remote(
            self.view(self.slot(me, chunk)),
            self.view(self.slot(target, chunk)),
            self.sems,
            (kind,),
            self.device(*target),
        )

    def arrived(self, kind):
        here = self.view(SLOTS - 1)
        twin = self.device(self.level, self.column, 1 - self.core)
        remote(here, here, self.sems, (kind,), twin).wait_recv()

    def up(self, back):
        chunk = (self.level - back, self.column, self.core)
        target = ((self.level + 1) % LEVELS, self.column, self.core)
        if back == 2:
            chunk, target = (self.level - 1, 1, 1), ((self.level + 2) % LEVELS, 0, 0)
        return self.copy(back, chunk, target)

    def over(self, back):
        chunk = (self.level - back, self.column, self.core)
        return self.copy(3 + back, chunk, (self.level, 1 - self.column, self.core))

    def twin(self, back):
        chunk = (self.level - back, self.column, self.core)
        return self.copy(6 + back, chunk, (self.level, self.column, 1 - self.core))

    def pass_on(self, back):
        chunk = (self.level - back, 1 - self.column, self.core)
        return self.copy(9 + back, chunk, (self.level, self.column, 1 - self.core))

    def sends_up(self, back):
        if back == 2:
            return (self.level == LEVELS - 3) & (self.column == 0) & (self.core == 1)
        return (self.level >= back) & (self.level < LEVELS - 1)

    def gets_up(self, back):
        if back == 2:
            return (self.level == LEVELS - 1) & (self.column + self.core == 0)
        return self.level >= back + 1

    def sends_over(self, back):
        if back == 0:
            return self.column == 0
        if back == 1:
            return self.level >= 1
        return (self.level >= 2) & (self.column + self.core >= 1)

    def gets_over(self, back):
        if back == 0:
            return self.column == 1
        if back == 1:
            return self.level >= 1
        return (self.level >= 2) & (1 - self.column + self.core >= 1)

    def sends_twin(self, back):
        return self.core == 0 if back == 0 else self.level >= back

    def gets_twin(self, back):
        return self.core == 1 if back == 0 else self.level >= back

    def gets_pass(self, back):
        if back < 2:
            return self.gets_over(back)
        return (self.level >= 2) & (2 - self.column - self.core >= 1)

    def start_own(self, wide=True):
        pl.when(self.sends_up(0))(lambda: self.up(0).start())
        pl.when(self.sends_twin(0))(lambda: self.twin(0).start())
        self.start_over(0, wide)

    def start_over(self, back, wide=True):
        pl.when(self.sends_over(back) & wide)(lambda: self.over(back).start())

    def after_up(self, back, wide=True):
        @pl.when(self.gets_up(back))
        def _():
            self.arrived(back)

        if back == 0:
            pl.when(self.sends_up(1))(lambda: self.up(1).start())
        self.start_over(back + 1, wide)
        pl.when(self.sends_twin(back + 1))(lambda: self.twin(back + 1).start())

    def after_over(self, back):
        @pl.when(self.gets_over(back))
        def _():
            self.arrived(3 + back)
            self.pass_on(back).start()

        if back == 1:
            pl.when(self.sends_up(2))(lambda: self.up(2).start())

    def after_twins(self):
        for back in range(3):
            pl.when(self.gets_twin(back))(lambda: self.arrived(6 + back))
            pl.when(self.gets_pass(back))(lambda: self.arrived(9 + back))
        pl.when(self.gets_up(2))(lambda: self.arrived(2))

    def finish(self):
        for back in range(3):
            pl.when(self.sends_up(back))(lambda: self.up(back).wait_send())
            pl.when(self.sends_over(back))(lambda: self.over(back).wait_send())
            pl.when(self.sends_twin(back))(lambda: self.twin(back).wait_send())
            pl.when(self.gets_over(back))(lambda: self.pass_on(back).wait_send())


def spot_of(place):
    return (place // 4, (place // 2) % 2, place % 2)


def neighbours(side, spot):
    level, column, core = spot
    return (
        device_at(1 - side, level, column, core),
        device_at(side, level, column, 1 - core),
        device_at(side, level, 1 - column, core),
        device_at(side, (level + 1) % LEVELS, column, core),
        device_at(side, (level + LEVELS - 1) % LEVELS, column, core),
    )


def rows_of(ref):
    return lambda slot: ref.at[:, tile(CHUNK * slot, CHUNK, CHUNK), :]


def row_of(ref, row):
    return lambda slot: ref.at[row, tile(CHUNK * slot, CHUNK, CHUNK), :]


def far_corners(side, spot):
    level, column, core = spot
    return (device_at(side, (level + 2) % LEVELS, column, 1 - core),)


def front_kernel(
    tok_ref,
    cot_ref,
    ids_ref,
    small_ref,
    wk_ref,
    wv_ref,
    wq_ref,
    wup_ref,
    w_out_ref,
    kwin_out,
    vwin_out,
    qwin_out,
    k_own,
    v_own,
    q_own,
    ln_out,
    tok_other,
    cot_other,
    ids_other,
    small_all,
    w_other_out,
    wup_other,
    attn_ref,
    lse_ref,
    mixed_ref,
    ids_all,
    kwin,
    vwin,
    qwin,
    w_other,
    w_own,
    ln_all,
    sent,
    came,
    own_sem,
    y_sems,
    w_sems,
    flow_sems,
    mix_sems,
    out_sem,
):
    side = lax.axis_index("grp")
    spot = spot_of(lax.axis_index("rep"))
    level, column, core = spot
    across, twin, over, above, below = neighbours(side, spot)
    near = device_at(side, level + 1 - 2 * (level % 2), column, core)
    f32, bf16 = jnp.float32, jnp.bfloat16
    half = w_own.shape[1]
    for win in (kwin, vwin, qwin):
        win[...] = jnp.zeros_like(win)
    greet((across, twin, over, above, below) + far_corners(side, spot))

    weights = (wk_ref, wv_ref, wq_ref)
    quarter = half // 4

    def part(owner):
        return tile(quarter * owner, quarter)

    mine = 2 * (level % 2) + core
    own_cols, other_cols = tile(half * side, half, 128), tile(half * (1 - side), half, 128)
    y_small = remote(small_ref, small_all.at[:, own_cols], y_sems, (0,), across)
    y_ids = remote(ids_ref, ids_other, y_sems, (1,), across)
    y_tok = remote(tok_ref, tok_other, y_sems, (2,), across)
    y_cot = remote(cot_ref, cot_other, y_sems, (3,), across)
    ff_half = wup_other.shape[1]

    def w_part(m, owner):
        return wup_other.at[part(owner)] if m == 3 else w_other.at[m, part(owner)]

    def w_across(m):
        if m == 3:
            source = wup_ref.at[part(mine), tile(ff_half * (1 - side), ff_half, 128)]
        else:
            source = weights[m].at[part(mine), other_cols]
        return remote(source, w_part(m, mine), w_sems, (0, m), across)

    def w_over(m):
        here = w_part(m, mine)
        return remote(here, here, w_sems, (1, m), near)

    def w_twin(m):
        here = w_part(m, mine)
        return remote(here, here, w_sems, (2, m), twin)

    def w_pass(m):
        here = w_part(m, 2 * (1 - level % 2) + core)
        return remote(here, here, w_sems, (3, m), twin)

    def w_load(m):
        return pltpu.make_async_copy(weights[m].at[:, own_cols], w_own.at[m], own_sem.at[m])

    y_small.start()
    w_across(0).start()
    w_across(1).start()
    for m in range(3):
        w_load(m).start()

    small_all[:, own_cols] = small_ref[...]

    def norm_into(rows, ref):
        x = ref[...].astype(f32)
        center = x - jnp.mean(x, axis=-1, keepdims=True)
        inverse = lax.rsqrt(jnp.mean(center * center, axis=-1, keepdims=True) + EPSILON)
        gain, beta = small_all[2:3, :].astype(f32), small_all[3:4, :].astype(f32)
        ln_all[rows, :] = (center * inverse * gain + beta).astype(bf16)
        ln_out[rows, :half] = ln_all[rows, own_cols]
        ln_out[rows, half:] = ln_all[rows, other_cols]

    def w_forward(m):
        w_across(m).wait_recv()
        w_over(m).start()
        w_twin(m).start()

    def w_second(m):
        w_over(m).wait_recv()
        w_pass(m).start()

    wins, biases = (kwin, vwin, qwin), (None, 7, 6)

    def project(m, row):
        rows = pl.ds(CHUNK * row, CHUNK)
        value = matmul(ln_out[rows, :half], w_own[m]) + matmul(ln_out[rows, half:], w_other[m])
        if biases[m] is not None:
            value = value + small_ref[biases[m] : biases[m] + 1, :].astype(f32)
        wins[m][row, pl.ds((SLOTS - 1) * CHUNK, CHUNK), :] = value.astype(bf16)
        (k_own, v_own, q_own)[m][rows, :] = value.astype(bf16)

    def win_out(m, row):
        target = (kwin_out, vwin_out, qwin_out)[m]
        return pltpu.make_async_copy(wins[m].at[row], target.at[row], out_sem.at[m, row])

    w_out_copy = pltpu.make_async_copy(w_other, w_other_out, out_sem.at[3, 0])

    def w_ready(m):
        w_load(m).wait()
        w_twin(m).wait_recv()
        w_pass(m).wait_recv()

    flows = [
        [
            Stream(side, spot, m == 2, row_of(wins[m], row), flow_sems.at[3 * row + m])
            for m in range(3)
        ]
        for row in range(2)
    ]
    pairs_of = [flow[:2] for flow in flows]
    queries = [flow[2] for flow in flows]

    def each(streams, event, *args):
        for stream in streams:
            getattr(stream, event)(*args)

    w_forward(0)
    y_ids.start()
    y_small.wait()
    y_tok.start()
    norm_into(pl.ds(0, CHUNK), tok_ref)
    w_forward(1)
    w_across(2).start()
    w_second(0)
    w_ready(0)
    project(0, 0)
    flows[0][0].start_own()
    w_second(1)
    w_ready(1)
    project(1, 0)
    flows[0][1].start_own()
    y_tok.wait_recv()
    norm_into(pl.ds(CHUNK, CHUNK), tok_other)
    project(0, 1)
    flows[1][0].start_own()
    project(1, 1)
    flows[1][1].start_own()
    each(pairs_of[0], "after_up", 0)
    w_forward(2)
    w_across(3).start()
    y_cot.start()
    each(pairs_of[1], "after_up", 0)
    each(pairs_of[0], "after_over", 0)
    w_second(2)
    w_ready(2)
    project(2, 0)
    project(2, 1)
    light = level < 2
    each(queries, "start_own", light)
    w_out_copy.start()
    each(pairs_of[0], "after_up", 1)
    each(pairs_of[1], "after_over", 0)
    each(pairs_of[1], "after_up", 1)
    each(pairs_of[0], "after_over", 1)
    each(queries, "after_up", 0, light)
    w_forward(3)
    each(queries, "after_up", 1, light)
    each(pairs_of[0], "after_over", 2)
    each(pairs_of[1], "after_over", 1)
    for back in range(3):
        each(queries, "start_over", back, jnp.logical_not(light))
    y_ids.wait()
    place = lax.axis_index("rep")
    ids_all[:, : REACH * CHUNK] = jnp.full((8, REACH * CHUNK), -1, jnp.int32)
    row_end = REACH * CHUNK + ids_ref.shape[1]
    ids_all[:, row_end:] = jnp.full((8, REACH * CHUNK), -2, jnp.int32)
    ids_all[:, REACH * CHUNK : row_end] = jnp.zeros((8, ids_ref.shape[1]), jnp.int32)
    ids_all[0:1, REACH * CHUNK : row_end] = ids_ref[...]
    ids_all[1:2, REACH * CHUNK : row_end] = ids_other[...]
    each(pairs_of[0], "after_twins")
    win_out(0, 0).start()
    win_out(1, 0).start()
    pairs = half // CHUNK
    window = pl.ds((SLOTS - 1 - REACH) * CHUNK, WINDOW)
    own_slot = pl.ds((SLOTS - 1) * CHUNK, CHUNK)
    upper, lower = pl.ds(0, CHUNK), pl.ds(CHUNK, CHUNK)
    mix_copy = (
        remote(sent.at[upper], came.at[lower], mix_sems, (0,), across),
        remote(sent.at[lower], came.at[upper], mix_sems, (1,), across),
    )

    def mix(row):
        rows = pl.ds(CHUNK * row, CHUNK)
        mixed = matmul(attn_ref[rows, :].astype(bf16), w_out_ref[...])
        mixed_ref[rows, :] = mixed
        sent[rows, :] = mixed.astype(bf16)
        mix_copy[row].start()

    def unit(i, unused):
        row, block = i // pairs, i % pairs
        rows, lanes = tile(CHUNK * row, CHUNK, CHUNK), tile(CHUNK * block, CHUNK, CHUNK)
        query = qwin[row, own_slot, lanes] * jnp.bfloat16(HEAD_DIM**-0.5)
        key_block, value_block = kwin[row, window, lanes], vwin[row, window, lanes]
        key_ids = ids_all[:2, tile(CHUNK * place, WINDOW, CHUNK)].astype(f32)
        key_ids = jnp.where(row == 0, key_ids[0:1], key_ids[1:2])
        query_ids = jnp.broadcast_to(key_ids[:, -CHUNK:], (CHUNK, CHUNK)).T[:, :1]
        allowed = (query_ids == key_ids) & (
            iota((CHUNK, WINDOW), 1) <= iota((CHUNK, WINDOW), 0) + REACH * CHUNK
        )
        outs, lses = [], []
        for which in range(2):
            scores = jnp.where(allowed, matmul_nt(head_half(query, which), key_block), NEGATIVE)
            top = jnp.max(scores, axis=-1, keepdims=True)
            probs = jnp.exp(scores - top)
            total = jnp.sum(probs, axis=-1, keepdims=True)
            outs.append(matmul((probs * (1.0 / total)).astype(bf16), value_block))
            lses.append(jnp.broadcast_to(top + jnp.log(total), (CHUNK, CHUNK)))
        attn_ref[rows, lanes] = join_halves(*outs)
        lse_ref[rows, lanes] = join_halves(*lses)
        pl.when(i == 2)(lambda: each(pairs_of[1], "after_over", 2))
        return unused

    lax.fori_loop(0, pairs, unit, 0)
    mix(0)
    each(pairs_of[1], "after_twins")
    win_out(0, 1).start()
    win_out(1, 1).start()
    lax.fori_loop(pairs, 2 * pairs, unit, 0)
    mix(1)
    for back in range(3):
        each(queries, "after_over", back)
    w_second(3)
    each(queries, "after_twins")
    for flow in flows:
        each(flow, "finish")
    for row in range(2):
        win_out(2, row).start()
    for copy in mix_copy:
        copy.wait()
    mixed_ref[...] += came[...].astype(f32)
    w_twin(3).wait_recv()
    w_pass(3).wait_recv()
    for m in range(4):
        w_across(m).wait_send()
        w_over(m).wait_send()
        w_twin(m).wait_send()
        w_pass(m).wait_send()
    y_tok.wait_send()
    for row in range(2):
        for m in range(3):
            win_out(m, row).wait()
    w_out_copy.wait()
    y_cot.wait()


def front(tokens, cotangent, doc_ids, small, w_key, w_value, w_query, w_up, w_out, number):
    dma = pltpu.SemaphoreType.DMA
    bf16 = jnp.bfloat16
    chunk, width = tokens.shape
    half, ff = w_up.shape
    hbm, vmem = pl.BlockSpec(memory_space=pl.ANY), pl.BlockSpec(memory_space=pltpu.VMEM)
    window = jax.ShapeDtypeStruct((2, SLOTS * CHUNK, half), bf16)
    return pl.pallas_call(
        front_kernel,
        out_shape=[
            window,
            window,
            window,
            *[jax.ShapeDtypeStruct((2 * chunk, half), bf16)] * 3,
            jax.ShapeDtypeStruct((2 * chunk, width), bf16),
            jax.ShapeDtypeStruct((chunk, width), bf16),
            jax.ShapeDtypeStruct((chunk, width), bf16),
            jax.ShapeDtypeStruct(doc_ids.shape, jnp.int32),
            jax.ShapeDtypeStruct((small.shape[0], width), bf16),
            jax.ShapeDtypeStruct((3, half, half), bf16),
            jax.ShapeDtypeStruct((half, ff // 2), bf16),
            jax.ShapeDtypeStruct((2 * chunk, half), jnp.float32),
            jax.ShapeDtypeStruct((2 * chunk, half), jnp.float32),
            jax.ShapeDtypeStruct((2 * chunk, width), jnp.float32),
            jax.ShapeDtypeStruct((8, 2 * REACH * CHUNK + doc_ids.shape[1]), jnp.int32),
        ],
        in_specs=[vmem, hbm, vmem, vmem, hbm, hbm, hbm, hbm, vmem],
        out_specs=[hbm] * 3 + [vmem] * 5 + [hbm] + [vmem] * 2 + [hbm] * 2 + [vmem] * 4,
        scratch_shapes=[
            *[pltpu.VMEM(window.shape, bf16)] * 3,
            pltpu.VMEM((3, half, half), bf16),
            pltpu.VMEM((3, half, half), bf16),
            pltpu.VMEM((2 * chunk, width), bf16),
            pltpu.VMEM((2 * chunk, width), bf16),
            pltpu.VMEM((2 * chunk, width), bf16),
            dma((3,)),
            dma((2, 4)),
            dma((2, 4, 4)),
            dma((6, 2, 12)),
            dma((2, 2)),
            dma((4, 2)),
        ],
        compiler_params=pltpu.CompilerParams(
            collective_id=number, has_side_effects=True, vmem_limit_bytes=56 * 2**20
        ),
    )(tokens, cotangent, doc_ids, small, w_key, w_value, w_query, w_up, w_out)


MESH_ID = pl.DeviceIdType.MESH
RING = 8
VEC_ROWS = 16
CHAINS = (
    (0, 160, 640, False),
    (1, 160, 640, False),
    (0, 80, 1280, True),
    (1, 80, 1280, True),
    (0, 80, 640, True),
    (0, 80, 640, True),
    (1, 80, 640, True),
    (1, 80, 640, False),
)
EARLY, LATE = (0, 1, 2, 3), (4, 5, 6, 7)


def device_at(side, level, column, core):
    return (side, (level * 2 + column) * 2 + core)


def ring_device(side, spot, core):
    level = jnp.where(spot < 4, spot, 7 - spot)
    return device_at(side, level, spot // 4, core)


def greet(partners):
    barrier = pltpu.get_barrier_semaphore()
    for partner in partners:
        pl.semaphore_signal(barrier, inc=1, device_id=partner, device_id_type=MESH_ID)
    pl.semaphore_wait(barrier, len(partners))


def tile(first, size, step=16):
    return pl.ds(first if isinstance(first, int) else pl.multiple_of(first, step), size)


def remote(source, target, sems, where, device):
    return pltpu.make_async_remote_copy(
        source,
        target,
        sems.at[(0,) + where],
        sems.at[(1,) + where],
        device_id=device,
        device_id_type=MESH_ID,
    )


class Rings:
    def __init__(self, side, spot_on_ring, core, devices, source_of, result_of, buffers, sems):
        self.side, self.spot, self.core = side, spot_on_ring, core
        self.sibling, self.across, ahead, behind = devices
        self.targets = (ahead, behind)
        self.source_of, self.result_of = source_of, result_of
        self.mine, self.theirs, self.landed, self.swapped = buffers
        (
            self.load_sem,
            self.core_sems,
            self.ring_sems,
            self.back_sems,
            self.share_sems,
            self.swap_sems,
            self.keep_sem,
        ) = sems

    def shard_at(self, chain, offset):
        return (self.spot + RING + (1 - 2 * CHAINS[chain][0]) * offset) % RING

    def load(self, chain, step):
        return pltpu.make_async_copy(
            self.source_of(chain, self.core, self.shard_at(chain, RING - 1 - step)),
            self.mine[chain].at[step % 3],
            self.load_sem.at[chain, step % 3],
        )

    def cross(self, chain, step):
        return remote(
            self.source_of(chain, 1 - self.core, self.shard_at(chain, RING - 1 - step)),
            self.theirs[chain].at[step],
            self.core_sems,
            (chain, step),
            self.sibling,
        )

    def start_inputs(self, chains, step):
        for chain in chains:
            self.load(chain, step).start()
            self.cross(chain, step).start()

    def ring_copy(self, chain, step):
        return remote(
            self.mine[chain].at[step % 3],
            self.landed[chain].at[step],
            self.ring_sems,
            (chain, step),
            self.targets[CHAINS[chain][0]],
        )

    def add(self, chain, step, first=False):
        self.load(chain, step).wait()
        self.cross(chain, step).wait()
        f32 = jnp.float32
        value = self.mine[chain][step % 3].astype(f32) + self.theirs[chain][step].astype(f32)
        if not first:
            value = value + self.landed[chain][step - 1].astype(f32)
        self.mine[chain][step % 3] = value.astype(jnp.bfloat16)

    def begin(self, chains):
        for chain in chains:
            self.add(chain, 0, True)
            self.ring_copy(chain, 0).start()
        self.start_inputs(chains, 2)

    def middle(self, chains, step):
        for chain in chains:
            self.ring_copy(chain, step - 1).wait()

            @pl.when(step < RING - 2)
            def _():
                self.load(chain, step + 2).start()
                self.cross(chain, step + 2).start()

            self.add(chain, step)
            self.ring_copy(chain, step).start()

    def back_copy(self, chain, step, own=False):
        shard = self.shard_at(chain, RING - step)
        return remote(
            self.mine[chain].at[(RING - 1) % 3] if own else self.result_of(chain, shard),
            self.result_of(chain, shard),
            self.back_sems,
            (chain, step),
            self.targets[CHAINS[chain][0]],
        )

    def share(self, chain, step, own=False):
        shard = self.shard_at(chain, RING - step)
        return remote(
            self.mine[chain].at[(RING - 1) % 3] if own else self.result_of(chain, shard),
            self.result_of(chain, shard),
            self.share_sems,
            (chain, step),
            self.sibling,
        )

    def keep(self, chain):
        return pltpu.make_async_copy(
            self.mine[chain].at[(RING - 1) % 3],
            self.result_of(chain, self.spot),
            self.keep_sem.at[chain],
        )

    def publish(self, chain):
        self.back_copy(chain, 0, True).start()
        self.share(chain, 0, True).start()
        self.keep(chain).start()

    def trade(self, chain):
        return remote(
            self.mine[chain].at[(RING - 1) % 3],
            self.swapped[chain],
            self.swap_sems,
            (chain,),
            self.across,
        )

    def last(self, chains):
        for chain in chains:
            self.ring_copy(chain, RING - 2).wait()
            self.add(chain, RING - 1)
            if CHAINS[chain][3]:

                @pl.when(self.core == 1)
                def _():
                    self.trade(chain).start()

                @pl.when(self.core == 0)
                def _():
                    self.publish(chain)

            else:
                self.publish(chain)

    def traded(self, chains):
        for chain in chains:
            if CHAINS[chain][3]:

                @pl.when(self.core == 1)
                def _():
                    self.trade(chain).wait()
                    self.mine[chain][(RING - 1) % 3] = self.swapped[chain][...]
                    self.publish(chain)

    def back_begin(self, chains):
        for chain in chains:
            self.back_copy(chain, 0, True).wait()
            self.back_copy(chain, 1).start()
            self.share(chain, 1).start()

    def back_middle(self, chains, step):
        for chain in chains:
            self.back_copy(chain, step).wait()

            @pl.when(step < RING - 2)
            def _():
                self.back_copy(chain, step + 1).start()

            self.share(chain, step + 1).start()

    def end(self, chains):
        for chain in chains:
            self.keep(chain).wait()
            self.share(chain, 0, True).wait()

        def rest(step, unused):
            for chain in chains:
                self.share(chain, step).wait()
            return unused

        lax.fori_loop(1, RING, rest, 0)


def tail_kernel(
    gdown_ref,
    gup_ref,
    part_two_ref,
    hidden_ref,
    small_ref,
    cot_ref,
    w_out_ref,
    attn_ref,
    lse_ref,
    q_ref,
    k_ref,
    v_ref,
    kwin_ref,
    vwin_ref,
    qwin_ref,
    ids_ref,
    ln_ref,
    wk_ref,
    wv_ref,
    wq_ref,
    w_other_ref,
    x_ref,
    bias_up_ref,
    down_ref,
    sum_down,
    sum_out,
    sum_up,
    sum_query,
    sum_key,
    sum_value,
    vec_out_ref,
    grad_input_ref,
    output_ref,
    *refs,
):
    count = len(CHAINS)
    buffers = [refs[i * count : (i + 1) * count] for i in range(4)]
    (
        dowin,
        statwin,
        sent,
        came,
        grad_hidden,
        grad_mix,
        grad_heads,
        gout,
        gqkv,
        grad_three,
        w_own,
        w_other,
        first_buf,
        second_buf,
        grad_one,
        sums,
        sent_down,
        came_down,
        query_ids,
        key_ids,
        later_ids,
        vec_steps,
        vec_landed,
        block_sem,
        weight_sem,
        y_sems,
        do_sems,
        stat_sems,
        vec_sems,
        *ring_sems,
    ) = refs[4 * count :]
    f32, bf16 = jnp.float32, jnp.bfloat16
    side = lax.axis_index("grp")
    spot = spot_of(lax.axis_index("rep"))
    level, column, core = spot
    on_ring = jnp.where(column == 0, level, 7 - level)
    near_by = neighbours(side, spot)
    across, sibling, over = near_by[:3]
    ahead = ring_device(side, (on_ring + 1) % RING, core)
    behind = ring_device(side, (on_ring + RING - 1) % RING, core)
    near = device_at(side, level + 1 - 2 * (level % 2), column, core)
    far = device_at(side, (level + 2) % 4, column, core)
    vec_partners = (sibling, over, near, far)
    block = side + core - 2 * side * core
    half = w_own.shape[1]
    pairs = half // CHUNK
    own_cols = tile(half * side, half, 128)

    def source_of(chain, which, shard):
        if chain < 2:
            return gdown_ref.at[tile(320 * shard + 160 * chain, 160), tile(640 * which, 640, 128)]
        rows = tile(640 * which + 80 * shard, 80)
        if chain < 4:
            return gup_ref.at[rows, pl.ds(1280 * (chain - 2), 1280)]
        if chain < 7:
            return gqkv.at[rows, pl.ds(640 * (chain - 4), 640)]
        return gout.at[tile(80 * shard, 80), tile(640 * which, 640, 128)]

    def result_of(chain, shard):
        if chain < 2:
            return sum_down.at[tile(320 * shard + 160 * chain, 160), tile(640 * core, 640, 128)]
        rows = tile(80 * shard, 80)
        if chain < 4:
            return sum_up.at[rows, tile(2560 * block + 1280 * (chain - 2), 1280, 128)]
        if chain < 7:
            return (sum_query, sum_key, sum_value)[chain - 4].at[rows, tile(640 * block, 640, 128)]
        return sum_out.at[rows, tile(640 * core, 640, 128)]

    rings = Rings(
        side,
        on_ring,
        core,
        (sibling, across, ahead, behind),
        source_of,
        result_of,
        buffers,
        ring_sems,
    )
    stats = Stream(
        side, spot, True, lambda slot: statwin.at[:, tile(CHUNK * slot, CHUNK, CHUNK)], stat_sems
    )
    grads = Stream(side, spot, True, rows_of(dowin), do_sems)
    streams = (stats, grads)
    own_slot = pl.ds((SLOTS - 1) * CHUNK, CHUNK)
    upper, lower = pl.ds(0, CHUNK), pl.ds(CHUNK, CHUNK)

    def exchange(which):
        return (
            remote(sent.at[lower], came.at[which, upper], y_sems, (which, 0), across),
            remote(sent.at[upper], came.at[which, lower], y_sems, (which, 1), across),
        )

    down_copy = remote(sent_down, came_down, y_sems, (2, 0), across)
    dowin[...] = jnp.zeros_like(dowin)
    statwin[...] = jnp.zeros_like(statwin)
    sent[...] = part_two_ref[...].astype(bf16)
    greet(near_by + far_corners(side, spot) + (far, ahead, behind))
    rings.start_inputs(EARLY, 0)
    for copy in exchange(0):
        copy.start()
    rings.start_inputs(EARLY, 1)
    weights = (wq_ref, wk_ref, wv_ref)
    weight_loads = [
        pltpu.make_async_copy(weights[m].at[:, own_cols], w_own.at[m], weight_sem.at[m])
        for m in range(3)
    ] + [
        pltpu.make_async_copy(w_other_ref.at[(m + 2) % 3], w_other.at[m], weight_sem.at[3 + m])
        for m in range(3)
    ]
    for copy in weight_loads:
        copy.start()
    rings.begin(EARLY)
    sent_down[...] = down_ref[CHUNK:, :].astype(bf16)
    down_copy.start()

    for row in range(2):
        line = slice(row, row + 1)
        first = REACH * CHUNK
        own = ids_ref[line, tile(first + CHUNK * lax.axis_index("rep"), CHUNK, CHUNK)].astype(f32)
        query_ids[row] = jnp.broadcast_to(own, (CHUNK, CHUNK)).T
        key_ids[row] = ids_ref[line, tile(CHUNK * lax.axis_index("rep"), WINDOW, CHUNK)].astype(f32)
        for k in range(REACH + 1):
            at = tile(first + CHUNK * (lax.axis_index("rep") + k), CHUNK, CHUNK)
            later_ids[row, :, (REACH - k) * CHUNK : (REACH + 1 - k) * CHUNK] = ids_ref[
                line, at
            ].astype(f32)

    def back_through_norm(which, part_ref, input_ref, gain_line, base, finish):
        zero = jnp.zeros((8, part_ref.shape[1]), f32)

        def some_rows(i, carry):
            rows = tile(32 * i, 32, 32)
            grad = part_ref[rows, :] + came[which, rows, :].astype(f32)
            inputs = input_ref[rows, :].astype(f32)
            center = inputs - jnp.mean(inputs, axis=-1, keepdims=True)
            inverse = lax.rsqrt(jnp.mean(center * center, axis=-1, keepdims=True) + EPSILON)
            normed = center * inverse
            scaled = grad * small_ref[gain_line : gain_line + 1, :].astype(f32)
            value = inverse * (
                scaled
                - jnp.mean(scaled, axis=-1, keepdims=True)
                - normed * jnp.mean(scaled * normed, axis=-1, keepdims=True)
            )
            extra = finish(rows, value)
            parts = [grad * normed, grad] + extra
            return tuple(
                c + jnp.sum(p.reshape(4, 8, -1), axis=0) for c, p in zip(carry, parts)
            )

        totals = lax.fori_loop(0, 8, some_rows, (zero,) * (3 if base == 0 else 2))
        for k, total in enumerate(totals):
            sums[base + k : base + k + 1, :] = jnp.sum(total, axis=0, keepdims=True)

    def finish_two(rows, value):
        hidden = cot_ref[rows, :].astype(f32) + value
        low = hidden.astype(bf16)
        grad_hidden[rows, :] = hidden
        grad_mix[rows, :] = low
        return [low.astype(f32)]

    rings.middle(EARLY, 1)
    for copy in exchange(0):
        copy.wait()
    back_through_norm(0, part_two_ref, hidden_ref, 4, 0, finish_two)
    grad_heads[...] = matmul_nt(grad_mix[...], w_out_ref[...]).astype(bf16)

    def own_stats(i, unused):
        row, pair = i // pairs, i % pairs
        rows, lanes = tile(CHUNK * row, CHUNK, CHUNK), tile(CHUNK * pair, CHUNK, CHUNK)
        weighed = (grad_heads[rows, lanes].astype(f32) * attn_ref[rows, lanes]).T
        level_of = lse_ref[rows, lanes].T
        zero = jnp.zeros((4, CHUNK), f32)
        statwin[tile(8 * i, 8, 8), own_slot] = jnp.concatenate(
            [
                level_of[:1],
                level_of[HALF_LANES : HALF_LANES + 1],
                jnp.sum(weighed[:HALF_LANES], axis=0, keepdims=True),
                jnp.sum(weighed[HALF_LANES:], axis=0, keepdims=True),
                zero,
            ],
            axis=0,
        )
        return unused

    lax.fori_loop(0, 2 * pairs, own_stats, 0)
    dowin[0, own_slot, :] = grad_heads[:CHUNK, :]
    dowin[1, own_slot, :] = grad_heads[CHUNK:, :]
    for stream in streams:
        stream.start_own()

    window = pl.ds((SLOTS - 1 - REACH) * CHUNK, WINDOW)

    def block_loads(refs_bufs, i):
        row, pair = i // pairs, i % pairs
        lanes = tile(CHUNK * pair, CHUNK, CHUNK)
        return [
            pltpu.make_async_copy(
                ref.at[row, window, lanes], buf.at[i % 2], block_sem.at[k, i % 2]
            )
            for k, (ref, buf) in enumerate(refs_bufs)
        ]

    kv_blocks = ((kwin_ref, first_buf), (vwin_ref, second_buf))
    q_blocks = ((qwin_ref, first_buf),)

    def start_blocks(refs_bufs, i):
        for copy in block_loads(refs_bufs, i):
            copy.start()

    def use_blocks(refs_bufs, i):
        for copy in block_loads(refs_bufs, i):
            copy.wait()
        pl.when(i + 1 < 2 * pairs)(lambda: start_blocks(refs_bufs, i + 1))

    scale = HEAD_DIM**-0.5
    start_blocks(kv_blocks, 0)
    attn_low = attn_ref[...].astype(bf16)
    gout[...] = matmul_tn(attn_low, grad_mix[...]).astype(bf16)

    def query_unit(i, unused):
        row, pair = i // pairs, i % pairs
        rows, lanes = tile(CHUNK * row, CHUNK, CHUNK), tile(CHUNK * pair, CHUNK, CHUNK)
        use_blocks(kv_blocks, i)
        query = q_ref[rows, lanes] * jnp.bfloat16(scale)
        keys, values = first_buf[i % 2], second_buf[i % 2]
        grad = grad_heads[rows, lanes]
        allowed = (query_ids[row][:, :1] == key_ids[row]) & (
            iota((CHUNK, WINDOW), 1) <= iota((CHUNK, WINDOW), 0) + REACH * CHUNK
        )
        weighed = grad.astype(f32) * attn_ref[rows, lanes]
        lse_pair = lse_ref[rows, lanes]
        parts = []
        for which in range(2):
            lse = lse_pair[:, which * HALF_LANES : which * HALF_LANES + 1]
            delta = jnp.sum(head_half(weighed, which), axis=-1, keepdims=True)
            scores = jnp.where(allowed, matmul_nt(head_half(query, which), keys), NEGATIVE)
            probs = jnp.exp(scores - lse)
            grad_probs = matmul_nt(head_half(grad, which), values)
            grad_scores = (probs * (grad_probs - delta)).astype(bf16)
            parts.append(matmul(grad_scores, keys))
        grad_three[0, rows, lanes] = (join_halves(*parts) * scale).astype(bf16)
        events = {
            1: (lambda s: s.after_up(0),),
            5: (lambda s: s.after_over(0), lambda s: s.after_up(1)),
            9: (lambda s: s.after_over(1),),
        }
        for at, what in events.items():

            @pl.when(i == at)
            def _():
                rings.middle(EARLY, 2 + at // 4)
                for event in what:
                    for stream in streams:
                        event(stream)

        return unused

    lax.fori_loop(0, 2 * pairs, query_unit, 0)
    start_blocks(q_blocks, 0)
    rings.middle(EARLY, 5)
    for stream in streams:
        stream.after_over(2)
    for stream in streams:
        stream.after_twins()

    def key_unit(i, unused):
        row, pair = i // pairs, i % pairs
        rows, lanes = tile(CHUNK * row, CHUNK, CHUNK), tile(CHUNK * pair, CHUNK, CHUNK)
        use_blocks(q_blocks, i)
        keys = k_ref[rows, lanes] * jnp.bfloat16(scale)
        values = v_ref[rows, lanes]
        queries = first_buf[i % 2]
        after = dowin[row, window, lanes]
        lane = iota((CHUNK, WINDOW), 1)
        ahead_by = (REACH - lane // CHUNK) * CHUNK + lane % CHUNK
        allowed = (query_ids[row][:, :1] == later_ids[row]) & (ahead_by >= iota((CHUNK, WINDOW), 0))
        lines = statwin[tile(8 * i, 8, 8), window]
        key_parts, value_parts = [], []
        for which in range(2):
            lse, delta = lines[which : which + 1], lines[2 + which : 3 + which]
            scores = jnp.where(allowed, matmul_nt(head_half(keys, which), queries), NEGATIVE)
            probs = jnp.exp(scores - lse)
            value_parts.append(matmul(probs.astype(bf16), after))
            grad_probs = matmul_nt(head_half(values, which), after)
            grad_scores = (probs * (grad_probs - delta)).astype(bf16)
            key_parts.append(matmul(grad_scores, queries))
        grad_three[1, rows, lanes] = (join_halves(*key_parts) * scale).astype(bf16)
        grad_three[2, rows, lanes] = join_halves(*value_parts).astype(bf16)
        pl.when(i == 3)(lambda: rings.middle(EARLY, 6))
        pl.when(i == 8)(lambda: rings.last(EARLY))
        return unused

    lax.fori_loop(0, 2 * pairs, key_unit, 0)
    rings.traded(EARLY)
    for stream in streams:
        stream.finish()

    for copy in weight_loads:
        copy.wait()
    rings.back_begin(EARLY)
    for m in range(3):

        def weight_rows(i, unused):
            lanes = tile(256 * i, 256, 256)
            gqkv[lanes, m * half : (m + 1) * half] = matmul_tn(
                ln_ref[:, lanes], grad_three[m]
            ).astype(bf16)
            return unused

        lax.fori_loop(0, 2 * half // 256, weight_rows, 0)
    rings.start_inputs(LATE, 0)
    rings.start_inputs(LATE, 1)
    rings.begin(LATE)

    own_part, other_part = 0.0, 0.0
    for m in range(3):
        own_part = own_part + matmul_nt(grad_three[m], w_own[m])
        other_part = other_part + matmul_nt(grad_three[m], w_other[m])
    grad_one[:, own_cols] = own_part
    grad_one[:, tile(half * (1 - side), half, 128)] = other_part
    sent[...] = grad_one[...].astype(bf16)
    for copy in exchange(1):
        copy.start()
    for k, m in ((0, 0), (1, 2)):
        sums[6 + k : 7 + k, :half] = jnp.sum(grad_three[m].astype(f32), axis=0, keepdims=True)

    def both_rings(step, unused):
        rings.back_middle(EARLY, step)
        rings.middle(LATE, step)
        return unused

    both_rings(jnp.int32(1), 0)
    for copy in exchange(1):
        copy.wait()

    def finish_one(rows, value):
        grad_hidden[rows, :] = grad_hidden[rows, :] + value
        return []

    back_through_norm(1, grad_one, x_ref, 2, 3, finish_one)
    grad_input_ref[...] = grad_hidden[:CHUNK, :]
    sums[5:6, :] = jnp.sum(cot_ref[...].astype(f32), axis=0, keepdims=True)
    vec_steps[0] = jnp.zeros(vec_steps.shape[1:], f32)
    for k in range(4):
        vec_steps[0, 3 + k : 4 + k, :] = bias_up_ref[:1, k * half : (k + 1) * half]
    for row, (line, cols) in {
        0: (6, pl.ds(0, half)),
        1: (7, pl.ds(0, half)),
        2: (2, own_cols),
        7: (5, own_cols),
        8: (3, own_cols),
        9: (4, own_cols),
        10: (0, own_cols),
        11: (1, own_cols),
    }.items():
        vec_steps[0, row : row + 1, :] = sums[line : line + 1, cols]
    vec_copy = [
        remote(vec_steps.at[k], vec_landed.at[k], vec_sems, (k,), vec_partners[k])
        for k in range(4)
    ]
    vec_copy[0].start()
    for k in range(4):
        both_rings(jnp.int32(2 + k), 0)
        vec_copy[k].wait()
        vec_steps[k + 1] = vec_steps[k] + vec_landed[k]
        if k < 3:
            vec_copy[k + 1].start()
    vec_out_ref[...] = vec_steps[4]
    both_rings(jnp.int32(6), 0)
    rings.last(LATE)
    rings.end(EARLY)
    down_copy.wait()
    output_ref[...] = (
        hidden_ref[:CHUNK, :]
        + down_ref[:CHUNK, :]
        + came_down[...].astype(f32)
        + small_ref[1:2, :].astype(f32)
    ).astype(bf16)
    rings.traded(LATE)
    rings.back_begin(LATE)

    def late_back(step, unused):
        rings.back_middle(LATE, step)
        return unused

    lax.fori_loop(1, RING - 1, late_back, 0)
    rings.end(LATE)


def tail(operands, width, half, ff, number):
    dma = pltpu.SemaphoreType.DMA
    f32, bf16 = jnp.float32, jnp.bfloat16
    count = len(CHAINS)
    rows = operands[3].shape[0]
    hbm, vmem = pl.BlockSpec(memory_space=pl.ANY), pl.BlockSpec(memory_space=pltpu.VMEM)
    in_hbm = (0, 1, 12, 13, 14, 17, 18, 19, 20)
    square = jax.ShapeDtypeStruct((half, width), bf16)

    def room(depth):
        return [pltpu.VMEM(depth + (tall, wide), bf16) for _, tall, wide, _ in CHAINS]

    return pl.pallas_call(
        tail_kernel,
        out_shape=[
            jax.ShapeDtypeStruct((ff, width), bf16),
            square,
            jax.ShapeDtypeStruct((half, 2 * ff), bf16),
            square,
            square,
            square,
            jax.ShapeDtypeStruct((VEC_ROWS, half), f32),
            jax.ShapeDtypeStruct((CHUNK, width), f32),
            jax.ShapeDtypeStruct((CHUNK, width), bf16),
        ],
        in_specs=[hbm if i in in_hbm else vmem for i in range(len(operands))],
        out_specs=[hbm] * 6 + [vmem] * 3,
        scratch_shapes=[
            *room((3,)),
            *room((RING,)),
            *room((RING - 1,)),
            *room(()),
            pltpu.VMEM((2, SLOTS * CHUNK, half), bf16),
            pltpu.VMEM((16 * half // CHUNK, SLOTS * CHUNK), f32),
            pltpu.VMEM((rows, width), bf16),
            pltpu.VMEM((2, rows, width), bf16),
            pltpu.VMEM((rows, width), f32),
            pltpu.VMEM((rows, width), bf16),
            pltpu.VMEM((rows, half), bf16),
            pltpu.VMEM((half, width), bf16),
            pltpu.VMEM((width, 3 * half), bf16),
            pltpu.VMEM((3, rows, half), bf16),
            pltpu.VMEM((3, half, half), bf16),
            pltpu.VMEM((3, half, half), bf16),
            pltpu.VMEM((2, WINDOW, CHUNK), bf16),
            pltpu.VMEM((2, WINDOW, CHUNK), bf16),
            pltpu.VMEM((rows, width), f32),
            pltpu.VMEM((8, width), f32),
            pltpu.VMEM((CHUNK, width), bf16),
            pltpu.VMEM((CHUNK, width), bf16),
            pltpu.VMEM((2, CHUNK, CHUNK), f32),
            pltpu.VMEM((2, 1, WINDOW), f32),
            pltpu.VMEM((2, 1, WINDOW), f32),
            pltpu.VMEM((5, VEC_ROWS, half), f32),
            pltpu.VMEM((4, VEC_ROWS, half), f32),
            dma((2, 2)),
            dma((6,)),
            dma((2, 3, 2)),
            dma((2, 12)),
            dma((2, 12)),
            dma((2, 4)),
            dma((count, 3)),
            dma((2, count, RING)),
            dma((2, count, RING - 1)),
            dma((2, count, RING - 1)),
            dma((2, count, RING)),
            dma((2, count)),
            dma((count,)),
        ],
        compiler_params=pltpu.CompilerParams(
            collective_id=number, has_side_effects=True, vmem_limit_bytes=60 * 2**20
        ),
    )(*operands)


FF_BLOCK = 512


def ff_kernel(
    side_ref,
    tok_ref,
    tok_other_ref,
    mixed_ref,
    small_ref,
    cot_ref,
    cot_other_ref,
    up_own_ref,
    up_other_ref,
    down_ref,
    bias_ref,
    hidden_ref,
    x_ref,
    cot_all_ref,
    result_ref,
    back_ref,
    grad_up_ref,
    grad_down_ref,
    grad_bias_ref,
    ln_ref,
    own_first,
    turned,
):
    f32, bf16 = jnp.float32, jnp.bfloat16
    side = side_ref[0]
    step = pl.program_id(0)
    chunk, width = tok_ref.shape
    half = width // 2
    own_cols, other_cols = tile(half * side, half, 128), tile(half * (1 - side), half, 128)

    @pl.when(step == 0)
    def _():
        x_ref[:chunk, :] = tok_ref[...]
        x_ref[chunk:, :] = tok_other_ref[...]
        cot_all_ref[:chunk, :] = cot_ref[...]
        cot_all_ref[chunk:, :] = cot_other_ref[...]

        def some_rows(i, unused):
            rows = tile(32 * i, 32, 32)
            hidden = x_ref[rows, :].astype(f32) + mixed_ref[rows, :] + small_ref[:1, :].astype(f32)
            hidden_ref[rows, :] = hidden
            normed, _ = norm_rows(hidden)
            ln_ref[rows, :] = (
                normed * small_ref[4:5, :].astype(f32) + small_ref[5:6, :].astype(f32)
            ).astype(bf16)
            return unused

        lax.fori_loop(0, 2 * chunk // 32, some_rows, 0)
        own_first[:, :half] = ln_ref[:, own_cols]
        own_first[:, half:] = ln_ref[:, other_cols]
        turned[...] = own_first[...].T
        result_ref[...] = jnp.zeros_like(result_ref)
        back_ref[...] = jnp.zeros_like(back_ref)

    pre_act = (
        matmul(own_first[:, :half], up_own_ref[...])
        + matmul(own_first[:, half:], up_other_ref[...])
        + bias_ref[...].astype(f32)
    )
    value, slope = gelu_pair(pre_act)
    act = value.astype(bf16)
    cot = cot_all_ref[...]
    result_ref[...] += matmul(act, down_ref[...])
    grad_pre = (matmul_nt(cot, down_ref[...]) * slope).astype(bf16)
    grad_bias_ref[...] = jnp.sum(grad_pre.astype(f32), axis=0, keepdims=True)
    grad_down_ref[...] = matmul_tn(act, cot).astype(bf16)
    grad_up_ref[...] = matmul(turned[...], grad_pre).astype(bf16)
    back_ref[:, own_cols] += matmul_nt(grad_pre, up_own_ref[...])
    back_ref[:, other_cols] += matmul_nt(grad_pre, up_other_ref[...])


def feed_forward(side, tokens, tok_other, mixed, small, cotangent, cot_other, w_up, up_other, w_down, b_up):
    f32, bf16 = jnp.float32, jnp.bfloat16
    chunk, width = tokens.shape
    half = width // 2
    ff = w_down.shape[0]
    steps = ff // FF_BLOCK

    def whole(shape):
        return pl.BlockSpec(shape, lambda j, s: (0, 0))

    rows = 2 * chunk
    columns = pl.BlockSpec((half, FF_BLOCK), lambda j, s: (0, j))
    return pl.pallas_call(
        ff_kernel,
        grid_spec=pltpu.PrefetchScalarGridSpec(
            num_scalar_prefetch=1,
            grid=(steps,),
            in_specs=[
                whole((chunk, width)),
                whole((chunk, width)),
                whole((rows, width)),
                whole(small.shape),
                whole((chunk, width)),
                whole((chunk, width)),
                pl.BlockSpec((half, FF_BLOCK), lambda j, s: (0, s[0] * steps + j)),
                columns,
                pl.BlockSpec((FF_BLOCK, width), lambda j, s: (j, 0)),
                pl.BlockSpec((1, FF_BLOCK), lambda j, s: (0, j)),
            ],
            out_specs=[
                whole((rows, width)),
                whole((rows, width)),
                whole((rows, width)),
                whole((rows, width)),
                whole((rows, width)),
                pl.BlockSpec((width, FF_BLOCK), lambda j, s: (0, j)),
                pl.BlockSpec((FF_BLOCK, width), lambda j, s: (j, 0)),
                pl.BlockSpec((1, FF_BLOCK), lambda j, s: (0, j)),
            ],
            scratch_shapes=[
                pltpu.VMEM((rows, width), bf16),
                pltpu.VMEM((rows, width), bf16),
                pltpu.VMEM((width, rows), bf16),
            ],
        ),
        out_shape=[
            jax.ShapeDtypeStruct((rows, width), f32),
            jax.ShapeDtypeStruct((rows, width), bf16),
            jax.ShapeDtypeStruct((rows, width), bf16),
            jax.ShapeDtypeStruct((rows, width), f32),
            jax.ShapeDtypeStruct((rows, width), f32),
            jax.ShapeDtypeStruct((width, ff), bf16),
            jax.ShapeDtypeStruct((ff, width), bf16),
            jax.ShapeDtypeStruct((1, ff), f32),
        ],
        compiler_params=pltpu.CompilerParams(vmem_limit_bytes=56 * 2**20),
    )(
        side.reshape(1).astype(jnp.int32),
        tokens,
        tok_other,
        mixed,
        small,
        cotangent,
        cot_other,
        w_up,
        up_other,
        w_down,
        b_up.reshape(1, -1),
    )


def widen_kernel(*refs):
    count = len(refs) // 2
    for source, target in zip(refs[:count], refs[count:]):
        target[...] = source[...].astype(jnp.float32)


def widen(arrays):
    steps = 4
    specs = [
        pl.BlockSpec((a.shape[0] // steps, a.shape[1]), lambda j: (j, 0)) for a in arrays
    ]
    return pl.pallas_call(
        widen_kernel,
        grid=(steps,),
        in_specs=specs,
        out_specs=specs,
        out_shape=[jax.ShapeDtypeStruct(a.shape, jnp.float32) for a in arrays],
        compiler_params=pltpu.CompilerParams(vmem_limit_bytes=56 * 2**20),
    )(*arrays)


def pair_shards(
    tokens,
    doc_ids,
    w_query,
    w_key,
    w_value,
    w_out,
    w_up,
    w_down,
    b_query,
    b_value,
    b_out,
    b_up,
    b_down,
    attn_gain,
    attn_beta,
    ffn_gain,
    ffn_beta,
    cotangent,
):
    f32, bf16 = jnp.float32, jnp.bfloat16
    chunk, width = tokens.shape
    half = width // 2
    side = lax.axis_index("grp")
    row_of_small = lax.broadcasted_iota(jnp.int32, (16, half), 0)
    small = jnp.zeros((16, half), bf16)
    for line, vector in enumerate(
        (b_out, b_down, attn_gain, attn_beta, ffn_gain, ffn_beta, b_query, b_value)
    ):
        small = jnp.where(row_of_small == line, vector[None, :], small)
    (
        k_win,
        v_win,
        q_win,
        k_own,
        v_own,
        q_own,
        ln_one,
        tok_other,
        cot_other,
        ids_other,
        small,
        w_other,
        w_up_other,
        attn,
        lse,
        mixed,
        ids,
    ) = front(tokens, cotangent, doc_ids, small, w_key, w_value, w_query, w_up, w_out, 2)
    hidden, x_all, cot_all, down, back_two, grad_w_up, grad_w_down, grad_b_up = feed_forward(
        side, tokens, tok_other, mixed, small, cotangent, cot_other, w_up, w_up_other, w_down, b_up
    )
    *sums, vec_sum, grad_input, output = tail(
        (
            grad_w_down,
            grad_w_up,
            back_two,
            hidden,
            small,
            cot_all,
            w_out,
            attn,
            lse,
            q_own,
            k_own,
            v_own,
            k_win,
            v_win,
            q_win,
            ids,
            ln_one,
            w_key,
            w_value,
            w_query,
            w_other,
            x_all,
            grad_b_up,
            down,
        ),
        width,
        half,
        w_down.shape[0],
        1,
    )
    sum_down, sum_out, sum_up, sum_query, sum_key, sum_value = widen(sums)
    cuts = [
        vec_sum[at : at + size].reshape(-1)
        for at, size in ((0, 1), (1, 1), (2, 1), (3, 4), (7, 1), (8, 1), (9, 1), (10, 1), (11, 1))
    ]
    return (
        output,
        grad_input,
        sum_query,
        sum_key,
        sum_value,
        sum_out,
        sum_up,
        sum_down,
        *cuts,
    )


def solution(mesh):
    in_specs = (
        P(("grp", "rep"), None),
        P("grp", None),
        P("grp", None),
        P("grp", None),
        P("grp", None),
        P("grp", None),
        P("grp", None),
        P("grp", None),
        P("grp"),
        P("grp"),
        P("grp"),
        P("grp"),
        P("grp"),
        P("grp"),
        P("grp"),
        P("grp"),
        P("grp"),
        P(("grp", "rep"), None),
    )
    out_specs = (
        P(("grp", "rep"), None),
        P(("grp", "rep"), None),
        P("grp", None),
        P("grp", None),
        P("grp", None),
        P("grp", None),
        P("grp", None),
        P("grp", None),
        P("grp"),
        P("grp"),
        P("grp"),
        P("grp"),
        P("grp"),
        P("grp"),
        P("grp"),
        P("grp"),
        P("grp"),
    )
    plan = pair_shards if fits_pair(mesh) else shards
    return jax.shard_map(plan, mesh=mesh, in_specs=in_specs, out_specs=out_specs, check_vma=False)
```

```python
import jax
import jax.numpy as jnp
from jax import lax
from jax.experimental import pallas as pl
from jax.experimental.pallas import tpu as pltpu
from jax.sharding import PartitionSpec as P

HEADS = 20
HEAD_DIM = 64
PAIRS = 4


EPSILON = 1e-05
NEGATIVE = -1e30
GELU_SCALE = 0.7978845608028654
GELU_CUBIC = 0.044715


def from_behind(array, axis, by):
    length = lax.axis_size(axis)
    pairs = [(i, i + by) for i in range(length) if 0 <= i + by < length]
    return lax.ppermute(array, axis, pairs)


def passed_along(block, axis, distance):
    devices = range(lax.axis_size(axis))
    route = [((i - distance) % len(devices), i) for i in devices]
    return lax.ppermute(block, axis, route)


def norm_rows(values):
    center = values - jnp.mean(values, axis=-1, keepdims=True)
    inverse = lax.rsqrt(jnp.mean(center * center, axis=-1, keepdims=True) + EPSILON)
    return (center * inverse, inverse)


def norm_grad(grad_norm, normed, inverse, gain):
    scaled = grad_norm * gain
    return inverse * (
        scaled
        - jnp.mean(scaled, axis=-1, keepdims=True)
        - normed * jnp.mean(scaled * normed, axis=-1, keepdims=True)
    )


def gelu_pair(inputs):
    inner = jnp.tanh(GELU_SCALE * (inputs + GELU_CUBIC * inputs * inputs * inputs))
    value = 0.5 * inputs * (1.0 + inner)
    slope = 0.5 * (1.0 + inner) + 0.5 * inputs * (1.0 - inner * inner) * GELU_SCALE * (
        1.0 + 3.0 * GELU_CUBIC * inputs * inputs
    )
    return (value, slope)


def matmul(left, right):
    return jnp.dot(left, right, preferred_element_type=jnp.float32)


def matmul_tn(left, right):
    return lax.dot_general(
        left, right, (((0,), (0,)), ((), ())), preferred_element_type=jnp.float32
    )


def matmul_nt(left, right):
    return lax.dot_general(
        left, right, (((1,), (1,)), ((), ())), preferred_element_type=jnp.float32
    )


def shards(
    tokens,
    doc_ids,
    w_query,
    w_key,
    w_value,
    w_out,
    w_up,
    w_down,
    b_query,
    b_value,
    b_out,
    b_up,
    b_down,
    attn_gain,
    attn_beta,
    ffn_gain,
    ffn_beta,
    cotangent,
):
    tok_dev = tokens.shape[0]
    width = tokens.shape[1]
    scale = HEAD_DIM ** (-0.5)
    (
        full_query,
        full_key,
        full_value,
        full_out,
        full_up,
        full_down,
        bias_query,
        bias_value,
        bias_out,
        bias_up,
        bias_down,
        gain_attn,
        beta_attn,
        gain_ffn,
        beta_ffn,
    ) = (
        lax.all_gather(w_query, "grp", axis=0, tiled=True),
        lax.all_gather(w_key, "grp", axis=0, tiled=True),
        lax.all_gather(w_value, "grp", axis=0, tiled=True),
        lax.all_gather(w_out, "grp", axis=0, tiled=True),
        lax.all_gather(w_up, "grp", axis=0, tiled=True),
        lax.all_gather(w_down, "grp", axis=0, tiled=True),
        lax.all_gather(b_query, "grp", axis=0, tiled=True),
        lax.all_gather(b_value, "grp", axis=0, tiled=True),
        lax.all_gather(b_out, "grp", axis=0, tiled=True),
        lax.all_gather(b_up, "grp", axis=0, tiled=True),
        lax.all_gather(b_down, "grp", axis=0, tiled=True),
        lax.all_gather(attn_gain, "grp", axis=0, tiled=True),
        lax.all_gather(attn_beta, "grp", axis=0, tiled=True),
        lax.all_gather(ffn_gain, "grp", axis=0, tiled=True),
        lax.all_gather(ffn_beta, "grp", axis=0, tiled=True),
    )
    rep_index = lax.axis_index("rep")
    pad_front = (2 * PAIRS + 1) * tok_dev
    row_ids = doc_ids[0]
    padded_ids = jnp.concatenate([jnp.full((pad_front,), -1, jnp.int32), row_ids])
    query_pos = rep_index * tok_dev + jnp.arange(tok_dev, dtype=jnp.int32)
    query_doc = lax.dynamic_slice_in_dim(row_ids, rep_index * tok_dev, tok_dev)

    def block_mask(block_index):
        first = (rep_index - 2 * block_index - 1) * tok_dev
        key_pos = first + jnp.arange(2 * tok_dev, dtype=jnp.int32)
        key_doc = lax.dynamic_slice_in_dim(padded_ids, first + pad_front, 2 * tok_dev)
        return (key_doc[None, :] == query_doc[:, None]) & (key_pos[None, :] <= query_pos[:, None])

    xfull = tokens.astype(jnp.float32)
    normed_one, inverse_one = norm_rows(xfull)
    ln_one = (normed_one * gain_attn.astype(jnp.float32) + beta_attn.astype(jnp.float32)).astype(
        jnp.bfloat16
    )
    query = (matmul(ln_one, full_query) + bias_query.astype(jnp.float32)).astype(jnp.bfloat16)
    keys = matmul(ln_one, full_key).astype(jnp.bfloat16)
    values = (matmul(ln_one, full_value) + bias_value.astype(jnp.float32)).astype(jnp.bfloat16)
    query_heads = query.reshape(tok_dev, HEADS, HEAD_DIM)
    earlier = from_behind((keys, values), "rep", 1)
    first_block = (
        jnp.concatenate([earlier[0], keys], axis=0),
        jnp.concatenate([earlier[1], values], axis=0),
    )

    def fetch_pair(block, unused):
        moved = from_behind((block[0], block[1]), "rep", 2)
        return (moved, moved)

    unused_end, following = lax.scan(fetch_pair, first_block, None, length=PAIRS)
    key_blocks = jnp.concatenate([first_block[0][None], following[0]], axis=0)
    value_blocks = jnp.concatenate([first_block[1][None], following[1]], axis=0)
    block_numbers = jnp.arange(PAIRS + 1, dtype=jnp.int32)

    def scores_of(block_keys, block_index):
        raw = (
            jnp.einsum(
                "qhd,khd->hqk",
                query_heads,
                block_keys.reshape(-1, HEADS, HEAD_DIM),
                preferred_element_type=jnp.float32,
            )
            * scale
        )
        return jnp.where(block_mask(block_index)[None], raw, NEGATIVE)

    def max_step(state, inputs):
        run_max, run_sum = state
        block_keys, block_index = inputs
        scores = scores_of(block_keys, block_index)
        new_max = jnp.maximum(run_max, jnp.max(scores, axis=-1))
        run_sum = run_sum * jnp.exp(run_max - new_max) + jnp.sum(
            jnp.exp(scores - new_max[..., None]), axis=-1
        )
        return ((new_max, run_sum), None)

    start_state = (
        jnp.full((HEADS, tok_dev), NEGATIVE, jnp.float32),
        jnp.zeros((HEADS, tok_dev), jnp.float32),
    )
    (top_score, total_exp), unused_max = lax.scan(
        max_step, start_state, (key_blocks, block_numbers)
    )
    log_total = top_score + jnp.log(total_exp)

    def value_step(total, inputs):
        block_keys, block_values, block_index = inputs
        probs = jnp.exp(scores_of(block_keys, block_index) - log_total[..., None]).astype(
            jnp.bfloat16
        )
        return (
            total
            + jnp.einsum(
                "hqk,khd->qhd",
                probs,
                block_values.reshape(-1, HEADS, HEAD_DIM),
                preferred_element_type=jnp.float32,
            ),
            None,
        )

    attn, unused_value = lax.scan(
        value_step,
        jnp.zeros((tok_dev, HEADS, HEAD_DIM), jnp.float32),
        (key_blocks, value_blocks, block_numbers),
    )
    attn_low = attn.reshape(tok_dev, width).astype(jnp.bfloat16)
    hidden = xfull + matmul(attn_low, full_out) + bias_out.astype(jnp.float32)
    normed_two, inverse_two = norm_rows(hidden)
    ln_two = (normed_two * gain_ffn.astype(jnp.float32) + beta_ffn.astype(jnp.float32)).astype(
        jnp.bfloat16
    )
    pre_act = matmul(ln_two, full_up) + bias_up.astype(jnp.float32)
    act_value, act_slope = gelu_pair(pre_act)
    act_low = act_value.astype(jnp.bfloat16)
    result = hidden + matmul(act_low, full_down) + bias_down.astype(jnp.float32)
    output = result.astype(jnp.bfloat16)
    (
        back_query,
        back_key,
        back_value,
        back_out,
        back_up,
        back_down,
        back_gain_attn,
        back_gain_ffn,
    ) = (
        lax.all_gather(w_query, "grp", axis=0, tiled=True),
        lax.all_gather(w_key, "grp", axis=0, tiled=True),
        lax.all_gather(w_value, "grp", axis=0, tiled=True),
        lax.all_gather(w_out, "grp", axis=0, tiled=True),
        lax.all_gather(w_up, "grp", axis=0, tiled=True),
        lax.all_gather(w_down, "grp", axis=0, tiled=True),
        lax.all_gather(attn_gain, "grp", axis=0, tiled=True),
        lax.all_gather(ffn_gain, "grp", axis=0, tiled=True),
    )
    grad_res = cotangent.astype(jnp.float32)
    grad_w_down = matmul_tn(act_low, cotangent)
    grad_b_down = jnp.sum(grad_res, axis=0)
    grad_pre = (matmul_nt(cotangent, back_down) * act_slope).astype(jnp.bfloat16)
    grad_w_up = matmul_tn(ln_two, grad_pre)
    grad_b_up = jnp.sum(grad_pre.astype(jnp.float32), axis=0)
    grad_ln_two = matmul_nt(grad_pre, back_up)
    grad_ffn_gain = jnp.sum(grad_ln_two * normed_two, axis=0)
    grad_ffn_beta = jnp.sum(grad_ln_two, axis=0)
    grad_hidden = grad_res + norm_grad(
        grad_ln_two, normed_two, inverse_two, back_gain_ffn.astype(jnp.float32)
    )
    grad_mix = grad_hidden.astype(jnp.bfloat16)
    grad_w_out = matmul_tn(attn_low, grad_mix)
    grad_b_out = jnp.sum(grad_mix.astype(jnp.float32), axis=0)
    grad_heads = (
        matmul_nt(grad_mix, back_out).astype(jnp.bfloat16).reshape(tok_dev, HEADS, HEAD_DIM)
    )
    delta = jnp.sum(grad_heads.astype(jnp.float32) * attn, axis=-1).T

    def block_grads(block_keys, block_values, block_index):
        probs = jnp.exp(scores_of(block_keys, block_index) - log_total[..., None])
        key_heads = block_keys.reshape(-1, HEADS, HEAD_DIM)
        value_heads = block_values.reshape(-1, HEADS, HEAD_DIM)
        grad_probs = jnp.einsum(
            "qhd,khd->hqk", grad_heads, value_heads, preferred_element_type=jnp.float32
        )
        grad_scores = (probs * (grad_probs - delta[..., None])).astype(jnp.bfloat16)
        part_query = (
            jnp.einsum("hqk,khd->qhd", grad_scores, key_heads, preferred_element_type=jnp.float32)
            * scale
        )
        part_key = (
            jnp.einsum("hqk,qhd->khd", grad_scores, query_heads, preferred_element_type=jnp.float32)
            * scale
        )
        part_value = jnp.einsum(
            "hqk,qhd->khd",
            probs.astype(jnp.bfloat16),
            grad_heads,
            preferred_element_type=jnp.float32,
        )
        return (part_query, part_key, part_value)

    again = from_behind((keys, values), "rep", 1)
    back_block = (
        jnp.concatenate([again[0], keys], axis=0),
        jnp.concatenate([again[1], values], axis=0),
    )
    query_sum, key_acc, value_acc = block_grads(back_block[0], back_block[1], 0)

    def travel_step(carry, inputs):
        query_total, key_total, value_total, block_keys, block_values = carry
        block_index, kept_keys, kept_values = inputs
        block_keys, block_values = from_behind((block_keys, block_values), "rep", 2)
        key_total, value_total = (
            passed_along(key_total.astype(jnp.bfloat16), "rep", 2).astype(key_total.dtype),
            passed_along(value_total.astype(jnp.bfloat16), "rep", 2).astype(value_total.dtype),
        )
        part_query, part_key, part_value = block_grads(block_keys, block_values, block_index)
        return (
            (
                query_total + part_query,
                key_total + part_key,
                value_total + part_value,
                block_keys,
                block_values,
            ),
            None,
        )

    carry_end, unused_travel = lax.scan(
        travel_step,
        (query_sum, key_acc, value_acc, back_block[0], back_block[1]),
        (block_numbers[1:], key_blocks[1:], value_blocks[1:]),
    )
    query_sum, key_acc, value_acc = (carry_end[0], carry_end[1], carry_end[2])
    from_next = (
        passed_along(key_acc[:tok_dev].astype(jnp.bfloat16), "rep", -1).astype(jnp.float32),
        passed_along(value_acc[:tok_dev].astype(jnp.bfloat16), "rep", -1).astype(jnp.float32),
    )
    joined_key = key_acc[tok_dev:] + from_next[0]
    joined_value = value_acc[tok_dev:] + from_next[1]
    returned = (
        passed_along(joined_key.astype(jnp.bfloat16), "rep", -2 * PAIRS).astype(joined_key.dtype),
        passed_along(joined_value.astype(jnp.bfloat16), "rep", -2 * PAIRS).astype(
            joined_value.dtype
        ),
    )
    grad_query_low = query_sum.reshape(tok_dev, width).astype(jnp.bfloat16)
    grad_key_low = returned[0].reshape(tok_dev, width).astype(jnp.bfloat16)
    grad_value_low = returned[1].reshape(tok_dev, width).astype(jnp.bfloat16)
    grad_w_query = matmul_tn(ln_one, grad_query_low)
    grad_b_query = jnp.sum(grad_query_low.astype(jnp.float32), axis=0)
    grad_w_key = matmul_tn(ln_one, grad_key_low)
    grad_w_value = matmul_tn(ln_one, grad_value_low)
    grad_b_value = jnp.sum(grad_value_low.astype(jnp.float32), axis=0)
    grad_ln_one = (
        matmul_nt(grad_query_low, back_query)
        + matmul_nt(grad_key_low, back_key)
        + matmul_nt(grad_value_low, back_value)
    )
    grad_attn_gain = jnp.sum(grad_ln_one * normed_one, axis=0)
    grad_attn_beta = jnp.sum(grad_ln_one, axis=0)
    grad_input = grad_hidden + norm_grad(
        grad_ln_one, normed_one, inverse_one, back_gain_attn.astype(jnp.float32)
    )
    shares = (
        lax.psum_scatter(
            grad_w_query.astype(jnp.bfloat16), "grp", scatter_dimension=0, tiled=True
        ).astype(jnp.float32),
        lax.psum_scatter(
            grad_w_key.astype(jnp.bfloat16), "grp", scatter_dimension=0, tiled=True
        ).astype(jnp.float32),
        lax.psum_scatter(
            grad_w_value.astype(jnp.bfloat16), "grp", scatter_dimension=0, tiled=True
        ).astype(jnp.float32),
        lax.psum_scatter(
            grad_w_out.astype(jnp.bfloat16), "grp", scatter_dimension=0, tiled=True
        ).astype(jnp.float32),
        lax.psum_scatter(
            grad_w_up.astype(jnp.bfloat16), "grp", scatter_dimension=0, tiled=True
        ).astype(jnp.float32),
        lax.psum_scatter(
            grad_w_down.astype(jnp.bfloat16), "grp", scatter_dimension=0, tiled=True
        ).astype(jnp.float32),
        lax.psum_scatter(
            grad_b_query.astype(jnp.bfloat16), "grp", scatter_dimension=0, tiled=True
        ).astype(jnp.float32),
        lax.psum_scatter(
            grad_b_value.astype(jnp.bfloat16), "grp", scatter_dimension=0, tiled=True
        ).astype(jnp.float32),
        lax.psum_scatter(
            grad_b_out.astype(jnp.bfloat16), "grp", scatter_dimension=0, tiled=True
        ).astype(jnp.float32),
        lax.psum_scatter(
            grad_b_up.astype(jnp.bfloat16), "grp", scatter_dimension=0, tiled=True
        ).astype(jnp.float32),
        lax.psum_scatter(
            grad_b_down.astype(jnp.bfloat16), "grp", scatter_dimension=0, tiled=True
        ).astype(jnp.float32),
        lax.psum_scatter(
            grad_attn_gain.astype(jnp.bfloat16), "grp", scatter_dimension=0, tiled=True
        ).astype(jnp.float32),
        lax.psum_scatter(
            grad_attn_beta.astype(jnp.bfloat16), "grp", scatter_dimension=0, tiled=True
        ).astype(jnp.float32),
        lax.psum_scatter(
            grad_ffn_gain.astype(jnp.bfloat16), "grp", scatter_dimension=0, tiled=True
        ).astype(jnp.float32),
        lax.psum_scatter(
            grad_ffn_beta.astype(jnp.bfloat16), "grp", scatter_dimension=0, tiled=True
        ).astype(jnp.float32),
    )
    totals = (
        lax.psum(shares[0].astype(jnp.bfloat16), "rep").astype(jnp.float32),
        lax.psum(shares[1].astype(jnp.bfloat16), "rep").astype(jnp.float32),
        lax.psum(shares[2].astype(jnp.bfloat16), "rep").astype(jnp.float32),
        lax.psum(shares[3].astype(jnp.bfloat16), "rep").astype(jnp.float32),
        lax.psum(shares[4].astype(jnp.bfloat16), "rep").astype(jnp.float32),
        lax.psum(shares[5].astype(jnp.bfloat16), "rep").astype(jnp.float32),
        lax.psum(shares[6].astype(jnp.bfloat16), "rep").astype(jnp.float32),
        lax.psum(shares[7].astype(jnp.bfloat16), "rep").astype(jnp.float32),
        lax.psum(shares[8].astype(jnp.bfloat16), "rep").astype(jnp.float32),
        lax.psum(shares[9].astype(jnp.bfloat16), "rep").astype(jnp.float32),
        lax.psum(shares[10].astype(jnp.bfloat16), "rep").astype(jnp.float32),
        lax.psum(shares[11].astype(jnp.bfloat16), "rep").astype(jnp.float32),
        lax.psum(shares[12].astype(jnp.bfloat16), "rep").astype(jnp.float32),
        lax.psum(shares[13].astype(jnp.bfloat16), "rep").astype(jnp.float32),
        lax.psum(shares[14].astype(jnp.bfloat16), "rep").astype(jnp.float32),
    )
    return (
        output,
        grad_input,
        totals[0],
        totals[1],
        totals[2],
        totals[3],
        totals[4],
        totals[5],
        totals[6],
        totals[7],
        totals[8],
        totals[9],
        totals[10],
        totals[11],
        totals[12],
        totals[13],
        totals[14],
    )


def fits_pair(mesh):
    return mesh.shape["grp"] == 2 and mesh.shape["rep"] == 16


REACH = 9
CHUNK = 128
WINDOW = (REACH + 1) * CHUNK
HALF_LANES = 64


def iota(shape, dim):
    return lax.broadcasted_iota(jnp.int32, shape, dim)


def head_half(block, which):
    first = iota(block.shape, 1) < HALF_LANES
    return jnp.where(first if which == 0 else jnp.logical_not(first), block, jnp.zeros_like(block))


def join_halves(first, second):
    return jnp.where(iota(first.shape, 1) < HALF_LANES, first, second)


SLOTS = 12
LEVELS = 4


class Stream:
    def __init__(self, side, spot, mirrored, view, sems):
        self.side, self.mirrored, self.view, self.sems = side, mirrored, view, sems
        level, column, core = spot
        if mirrored:
            level, column, core = LEVELS - 1 - level, 1 - column, 1 - core
        self.level, self.column, self.core = level, column, core

    def device(self, level, column, core):
        if self.mirrored:
            level, column, core = LEVELS - 1 - level, 1 - column, 1 - core
        return device_at(self.side, level, column, core)

    def slot(self, holder, chunk):
        gaps = [c - h for c, h in zip(chunk, holder)]
        return SLOTS - 1 + 4 * gaps[0] + 2 * gaps[1] + gaps[2]

    def copy(self, kind, chunk, target):
        me = (self.level, self.column, self.core)
        return remote(
            self.view(self.slot(me, chunk)),
            self.view(self.slot(target, chunk)),
            self.sems,
            (kind,),
            self.device(*target),
        )

    def arrived(self, kind):
        here = self.view(SLOTS - 1)
        twin = self.device(self.level, self.column, 1 - self.core)
        remote(here, here, self.sems, (kind,), twin).wait_recv()

    def up(self, back):
        chunk = (self.level - back, self.column, self.core)
        target = ((self.level + 1) % LEVELS, self.column, self.core)
        if back == 2:
            chunk, target = (self.level - 1, 1, 1), ((self.level + 2) % LEVELS, 0, 0)
        return self.copy(back, chunk, target)

    def over(self, back):
        chunk = (self.level - back, self.column, self.core)
        return self.copy(3 + back, chunk, (self.level, 1 - self.column, self.core))

    def twin(self, back):
        chunk = (self.level - back, self.column, self.core)
        return self.copy(6 + back, chunk, (self.level, self.column, 1 - self.core))

    def pass_on(self, back):
        chunk = (self.level - back, 1 - self.column, self.core)
        return self.copy(9 + back, chunk, (self.level, self.column, 1 - self.core))

    def sends_up(self, back):
        if back == 2:
            return (self.level == LEVELS - 3) & (self.column == 0) & (self.core == 1)
        return (self.level >= back) & (self.level < LEVELS - 1)

    def gets_up(self, back):
        if back == 2:
            return (self.level == LEVELS - 1) & (self.column + self.core == 0)
        return self.level >= back + 1

    def sends_over(self, back):
        if back == 0:
            return self.column == 0
        if back == 1:
            return self.level >= 1
        return (self.level >= 2) & (self.column + self.core >= 1)

    def gets_over(self, back):
        if back == 0:
            return self.column == 1
        if back == 1:
            return self.level >= 1
        return (self.level >= 2) & (1 - self.column + self.core >= 1)

    def sends_twin(self, back):
        return self.core == 0 if back == 0 else self.level >= back

    def gets_twin(self, back):
        return self.core == 1 if back == 0 else self.level >= back

    def gets_pass(self, back):
        if back < 2:
            return self.gets_over(back)
        return (self.level >= 2) & (2 - self.column - self.core >= 1)

    def start_own(self, wide=True):
        pl.when(self.sends_up(0))(lambda: self.up(0).start())
        pl.when(self.sends_twin(0))(lambda: self.twin(0).start())
        self.start_over(0, wide)

    def start_over(self, back, wide=True):
        pl.when(self.sends_over(back) & wide)(lambda: self.over(back).start())

    def after_up(self, back, wide=True):
        @pl.when(self.gets_up(back))
        def _():
            self.arrived(back)

        if back == 0:
            pl.when(self.sends_up(1))(lambda: self.up(1).start())
        self.start_over(back + 1, wide)
        pl.when(self.sends_twin(back + 1))(lambda: self.twin(back + 1).start())

    def after_over(self, back):
        @pl.when(self.gets_over(back))
        def _():
            self.arrived(3 + back)
            self.pass_on(back).start()

        if back == 1:
            pl.when(self.sends_up(2))(lambda: self.up(2).start())

    def after_twins(self):
        for back in range(3):
            pl.when(self.gets_twin(back))(lambda: self.arrived(6 + back))
            pl.when(self.gets_pass(back))(lambda: self.arrived(9 + back))
        pl.when(self.gets_up(2))(lambda: self.arrived(2))

    def finish(self):
        for back in range(3):
            pl.when(self.sends_up(back))(lambda: self.up(back).wait_send())
            pl.when(self.sends_over(back))(lambda: self.over(back).wait_send())
            pl.when(self.sends_twin(back))(lambda: self.twin(back).wait_send())
            pl.when(self.gets_over(back))(lambda: self.pass_on(back).wait_send())


def spot_of(place):
    return (place // 4, (place // 2) % 2, place % 2)


def neighbours(side, spot):
    level, column, core = spot
    return (
        device_at(1 - side, level, column, core),
        device_at(side, level, column, 1 - core),
        device_at(side, level, 1 - column, core),
        device_at(side, (level + 1) % LEVELS, column, core),
        device_at(side, (level + LEVELS - 1) % LEVELS, column, core),
    )


def rows_of(ref):
    return lambda slot: ref.at[:, tile(CHUNK * slot, CHUNK, CHUNK), :]


def row_of(ref, row):
    return lambda slot: ref.at[row, tile(CHUNK * slot, CHUNK, CHUNK), :]


def far_corners(side, spot):
    level, column, core = spot
    return (device_at(side, (level + 2) % LEVELS, column, 1 - core),)


def front_kernel(
    tok_ref,
    cot_ref,
    ids_ref,
    small_ref,
    wk_ref,
    wv_ref,
    wq_ref,
    wup_ref,
    w_out_ref,
    kwin_out,
    vwin_out,
    qwin_out,
    k_own,
    v_own,
    q_own,
    ln_out,
    tok_other,
    cot_other,
    ids_other,
    small_all,
    w_other_out,
    wup_other,
    attn_ref,
    lse_ref,
    mixed_ref,
    ids_all,
    kwin,
    vwin,
    qwin,
    w_other,
    w_own,
    ln_all,
    sent,
    came,
    own_sem,
    y_sems,
    w_sems,
    flow_sems,
    mix_sems,
    out_sem,
):
    side = lax.axis_index("grp")
    spot = spot_of(lax.axis_index("rep"))
    level, column, core = spot
    across, twin, over, above, below = neighbours(side, spot)
    near = device_at(side, level + 1 - 2 * (level % 2), column, core)
    f32, bf16 = jnp.float32, jnp.bfloat16
    half = w_own.shape[1]
    for win in (kwin, vwin, qwin):
        win[...] = jnp.zeros_like(win)
    greet((across, twin, over, above, below) + far_corners(side, spot))

    weights = (wk_ref, wv_ref, wq_ref)
    quarter = half // 4

    def part(owner):
        return tile(quarter * owner, quarter)

    mine = 2 * (level % 2) + core
    own_cols, other_cols = tile(half * side, half, 128), tile(half * (1 - side), half, 128)
    y_small = remote(small_ref, small_all.at[:, own_cols], y_sems, (0,), across)
    y_ids = remote(ids_ref, ids_other, y_sems, (1,), across)
    y_tok = remote(tok_ref, tok_other, y_sems, (2,), across)
    y_cot = remote(cot_ref, cot_other, y_sems, (3,), across)
    ff_half = wup_other.shape[1]

    def w_part(m, owner):
        return wup_other.at[part(owner)] if m == 3 else w_other.at[m, part(owner)]

    def w_across(m):
        if m == 3:
            source = wup_ref.at[part(mine), tile(ff_half * (1 - side), ff_half, 128)]
        else:
            source = weights[m].at[part(mine), other_cols]
        return remote(source, w_part(m, mine), w_sems, (0, m), across)

    def w_over(m):
        here = w_part(m, mine)
        return remote(here, here, w_sems, (1, m), near)

    def w_twin(m):
        here = w_part(m, mine)
        return remote(here, here, w_sems, (2, m), twin)

    def w_pass(m):
        here = w_part(m, 2 * (1 - level % 2) + core)
        return remote(here, here, w_sems, (3, m), twin)

    def w_load(m):
        return pltpu.make_async_copy(weights[m].at[:, own_cols], w_own.at[m], own_sem.at[m])

    y_small.start()
    w_across(0).start()
    w_across(1).start()
    for m in range(3):
        w_load(m).start()

    small_all[:, own_cols] = small_ref[...]

    def norm_into(rows, ref):
        x = ref[...].astype(f32)
        center = x - jnp.mean(x, axis=-1, keepdims=True)
        inverse = lax.rsqrt(jnp.mean(center * center, axis=-1, keepdims=True) + EPSILON)
        gain, beta = small_all[2:3, :].astype(f32), small_all[3:4, :].astype(f32)
        ln_all[rows, :] = (center * inverse * gain + beta).astype(bf16)
        ln_out[rows, :half] = ln_all[rows, own_cols]
        ln_out[rows, half:] = ln_all[rows, other_cols]

    def w_forward(m):
        w_across(m).wait_recv()
        w_over(m).start()
        w_twin(m).start()

    def w_second(m):
        w_over(m).wait_recv()
        w_pass(m).start()

    wins, biases = (kwin, vwin, qwin), (None, 7, 6)

    def project(m, row):
        rows = pl.ds(CHUNK * row, CHUNK)
        value = matmul(ln_out[rows, :half], w_own[m]) + matmul(ln_out[rows, half:], w_other[m])
        if biases[m] is not None:
            value = value + small_ref[biases[m] : biases[m] + 1, :].astype(f32)
        wins[m][row, pl.ds((SLOTS - 1) * CHUNK, CHUNK), :] = value.astype(bf16)
        (k_own, v_own, q_own)[m][rows, :] = value.astype(bf16)

    def win_out(m, row):
        target = (kwin_out, vwin_out, qwin_out)[m]
        return pltpu.make_async_copy(wins[m].at[row], target.at[row], out_sem.at[m, row])

    w_out_copy = pltpu.make_async_copy(w_other, w_other_out, out_sem.at[3, 0])

    def w_ready(m):
        w_load(m).wait()
        w_twin(m).wait_recv()
        w_pass(m).wait_recv()

    flows = [
        [
            Stream(side, spot, m == 2, row_of(wins[m], row), flow_sems.at[3 * row + m])
            for m in range(3)
        ]
        for row in range(2)
    ]
    pairs_of = [flow[:2] for flow in flows]
    queries = [flow[2] for flow in flows]

    def each(streams, event, *args):
        for stream in streams:
            getattr(stream, event)(*args)

    w_forward(0)
    y_ids.start()
    y_small.wait()
    y_tok.start()
    norm_into(pl.ds(0, CHUNK), tok_ref)
    w_forward(1)
    w_across(2).start()
    w_second(0)
    w_ready(0)
    project(0, 0)
    flows[0][0].start_own()
    w_second(1)
    w_ready(1)
    project(1, 0)
    flows[0][1].start_own()
    y_tok.wait_recv()
    norm_into(pl.ds(CHUNK, CHUNK), tok_other)
    project(0, 1)
    flows[1][0].start_own()
    project(1, 1)
    flows[1][1].start_own()
    each(pairs_of[0], "after_up", 0)
    w_forward(2)
    w_across(3).start()
    y_cot.start()
    each(pairs_of[1], "after_up", 0)
    each(pairs_of[0], "after_over", 0)
    w_second(2)
    w_ready(2)
    project(2, 0)
    project(2, 1)
    light = level < 2
    each(queries, "start_own", light)
    w_out_copy.start()
    each(pairs_of[0], "after_up", 1)
    each(pairs_of[1], "after_over", 0)
    each(pairs_of[1], "after_up", 1)
    each(pairs_of[0], "after_over", 1)
    each(queries, "after_up", 0, light)
    w_forward(3)
    each(queries, "after_up", 1, light)
    each(pairs_of[0], "after_over", 2)
    each(pairs_of[1], "after_over", 1)
    for back in range(3):
        each(queries, "start_over", back, jnp.logical_not(light))
    y_ids.wait()
    place = lax.axis_index("rep")
    ids_all[:, : REACH * CHUNK] = jnp.full((8, REACH * CHUNK), -1, jnp.int32)
    row_end = REACH * CHUNK + ids_ref.shape[1]
    ids_all[:, row_end:] = jnp.full((8, REACH * CHUNK), -2, jnp.int32)
    ids_all[:, REACH * CHUNK : row_end] = jnp.zeros((8, ids_ref.shape[1]), jnp.int32)
    ids_all[0:1, REACH * CHUNK : row_end] = ids_ref[...]
    ids_all[1:2, REACH * CHUNK : row_end] = ids_other[...]
    each(pairs_of[0], "after_twins")
    win_out(0, 0).start()
    win_out(1, 0).start()
    pairs = half // CHUNK
    window = pl.ds((SLOTS - 1 - REACH) * CHUNK, WINDOW)
    own_slot = pl.ds((SLOTS - 1) * CHUNK, CHUNK)
    upper, lower = pl.ds(0, CHUNK), pl.ds(CHUNK, CHUNK)
    mix_copy = (
        remote(sent.at[upper], came.at[lower], mix_sems, (0,), across),
        remote(sent.at[lower], came.at[upper], mix_sems, (1,), across),
    )

    def mix(row):
        rows = pl.ds(CHUNK * row, CHUNK)
        mixed = matmul(attn_ref[rows, :].astype(bf16), w_out_ref[...])
        mixed_ref[rows, :] = mixed
        sent[rows, :] = mixed.astype(bf16)
        mix_copy[row].start()

    def unit(i, unused):
        row, block = i // pairs, i % pairs
        rows, lanes = tile(CHUNK * row, CHUNK, CHUNK), tile(CHUNK * block, CHUNK, CHUNK)
        query = qwin[row, own_slot, lanes] * jnp.bfloat16(HEAD_DIM**-0.5)
        key_block, value_block = kwin[row, window, lanes], vwin[row, window, lanes]
        key_ids = ids_all[:2, tile(CHUNK * place, WINDOW, CHUNK)].astype(f32)
        key_ids = jnp.where(row == 0, key_ids[0:1], key_ids[1:2])
        query_ids = jnp.broadcast_to(key_ids[:, -CHUNK:], (CHUNK, CHUNK)).T[:, :1]
        allowed = (query_ids == key_ids) & (
            iota((CHUNK, WINDOW), 1) <= iota((CHUNK, WINDOW), 0) + REACH * CHUNK
        )
        outs, lses = [], []
        for which in range(2):
            scores = jnp.where(allowed, matmul_nt(head_half(query, which), key_block), NEGATIVE)
            top = jnp.max(scores, axis=-1, keepdims=True)
            probs = jnp.exp(scores - top)
            total = jnp.sum(probs, axis=-1, keepdims=True)
            outs.append(matmul((probs * (1.0 / total)).astype(bf16), value_block))
            lses.append(jnp.broadcast_to(top + jnp.log(total), (CHUNK, CHUNK)))
        attn_ref[rows, lanes] = join_halves(*outs)
        lse_ref[rows, lanes] = join_halves(*lses)
        pl.when(i == 2)(lambda: each(pairs_of[1], "after_over", 2))
        return unused

    lax.fori_loop(0, pairs, unit, 0)
    mix(0)
    each(pairs_of[1], "after_twins")
    win_out(0, 1).start()
    win_out(1, 1).start()
    lax.fori_loop(pairs, 2 * pairs, unit, 0)
    mix(1)
    for back in range(3):
        each(queries, "after_over", back)
    w_second(3)
    each(queries, "after_twins")
    for flow in flows:
        each(flow, "finish")
    for row in range(2):
        win_out(2, row).start()
    for copy in mix_copy:
        copy.wait()
    mixed_ref[...] += came[...].astype(f32)
    w_twin(3).wait_recv()
    w_pass(3).wait_recv()
    for m in range(4):
        w_across(m).wait_send()
        w_over(m).wait_send()
        w_twin(m).wait_send()
        w_pass(m).wait_send()
    y_tok.wait_send()
    for row in range(2):
        for m in range(3):
            win_out(m, row).wait()
    w_out_copy.wait()
    y_cot.wait()


def front(tokens, cotangent, doc_ids, small, w_key, w_value, w_query, w_up, w_out, number):
    dma = pltpu.SemaphoreType.DMA
    bf16 = jnp.bfloat16
    chunk, width = tokens.shape
    half, ff = w_up.shape
    hbm, vmem = pl.BlockSpec(memory_space=pl.ANY), pl.BlockSpec(memory_space=pltpu.VMEM)
    window = jax.ShapeDtypeStruct((2, SLOTS * CHUNK, half), bf16)
    return pl.pallas_call(
        front_kernel,
        out_shape=[
            window,
            window,
            window,
            *[jax.ShapeDtypeStruct((2 * chunk, half), bf16)] * 3,
            jax.ShapeDtypeStruct((2 * chunk, width), bf16),
            jax.ShapeDtypeStruct((chunk, width), bf16),
            jax.ShapeDtypeStruct((chunk, width), bf16),
            jax.ShapeDtypeStruct(doc_ids.shape, jnp.int32),
            jax.ShapeDtypeStruct((small.shape[0], width), bf16),
            jax.ShapeDtypeStruct((3, half, half), bf16),
            jax.ShapeDtypeStruct((half, ff // 2), bf16),
            jax.ShapeDtypeStruct((2 * chunk, half), jnp.float32),
            jax.ShapeDtypeStruct((2 * chunk, half), jnp.float32),
            jax.ShapeDtypeStruct((2 * chunk, width), jnp.float32),
            jax.ShapeDtypeStruct((8, 2 * REACH * CHUNK + doc_ids.shape[1]), jnp.int32),
        ],
        in_specs=[vmem, hbm, vmem, vmem, hbm, hbm, hbm, hbm, vmem],
        out_specs=[hbm] * 3 + [vmem] * 5 + [hbm] + [vmem] * 2 + [hbm] * 2 + [vmem] * 4,
        scratch_shapes=[
            *[pltpu.VMEM(window.shape, bf16)] * 3,
            pltpu.VMEM((3, half, half), bf16),
            pltpu.VMEM((3, half, half), bf16),
            pltpu.VMEM((2 * chunk, width), bf16),
            pltpu.VMEM((2 * chunk, width), bf16),
            pltpu.VMEM((2 * chunk, width), bf16),
            dma((3,)),
            dma((2, 4)),
            dma((2, 4, 4)),
            dma((6, 2, 12)),
            dma((2, 2)),
            dma((4, 2)),
        ],
        compiler_params=pltpu.CompilerParams(
            collective_id=number, has_side_effects=True, vmem_limit_bytes=56 * 2**20
        ),
    )(tokens, cotangent, doc_ids, small, w_key, w_value, w_query, w_up, w_out)


MESH_ID = pl.DeviceIdType.MESH
RING = 8
VEC_ROWS = 16
CHAINS = (
    (0, 160, 640, False),
    (1, 160, 640, False),
    (0, 80, 1280, True),
    (1, 80, 1280, True),
    (0, 80, 640, True),
    (0, 80, 640, True),
    (1, 80, 640, True),
    (1, 80, 640, False),
)
EARLY, LATE = (0, 1, 2, 3), (4, 5, 6, 7)


def device_at(side, level, column, core):
    return (side, (level * 2 + column) * 2 + core)


def ring_device(side, spot, core):
    level = jnp.where(spot < 4, spot, 7 - spot)
    return device_at(side, level, spot // 4, core)


def greet(partners):
    barrier = pltpu.get_barrier_semaphore()
    for partner in partners:
        pl.semaphore_signal(barrier, inc=1, device_id=partner, device_id_type=MESH_ID)
    pl.semaphore_wait(barrier, len(partners))


def tile(first, size, step=16):
    return pl.ds(first if isinstance(first, int) else pl.multiple_of(first, step), size)


def remote(source, target, sems, where, device):
    return pltpu.make_async_remote_copy(
        source,
        target,
        sems.at[(0,) + where],
        sems.at[(1,) + where],
        device_id=device,
        device_id_type=MESH_ID,
    )


class Rings:
    def __init__(self, side, spot_on_ring, core, devices, source_of, result_of, buffers, sems):
        self.side, self.spot, self.core = side, spot_on_ring, core
        self.sibling, self.across, ahead, behind = devices
        self.targets = (ahead, behind)
        self.source_of, self.result_of = source_of, result_of
        self.mine, self.theirs, self.landed, self.swapped = buffers
        (
            self.load_sem,
            self.core_sems,
            self.ring_sems,
            self.back_sems,
            self.share_sems,
            self.swap_sems,
            self.keep_sem,
        ) = sems

    def shard_at(self, chain, offset):
        return (self.spot + RING + (1 - 2 * CHAINS[chain][0]) * offset) % RING

    def load(self, chain, step):
        return pltpu.make_async_copy(
            self.source_of(chain, self.core, self.shard_at(chain, RING - 1 - step)),
            self.mine[chain].at[step % 3],
            self.load_sem.at[chain, step % 3],
        )

    def cross(self, chain, step):
        return remote(
            self.source_of(chain, 1 - self.core, self.shard_at(chain, RING - 1 - step)),
            self.theirs[chain].at[step],
            self.core_sems,
            (chain, step),
            self.sibling,
        )

    def start_inputs(self, chains, step):
        for chain in chains:
            self.load(chain, step).start()
            self.cross(chain, step).start()

    def ring_copy(self, chain, step):
        return remote(
            self.mine[chain].at[step % 3],
            self.landed[chain].at[step],
            self.ring_sems,
            (chain, step),
            self.targets[CHAINS[chain][0]],
        )

    def add(self, chain, step, first=False):
        self.load(chain, step).wait()
        self.cross(chain, step).wait()
        f32 = jnp.float32
        value = self.mine[chain][step % 3].astype(f32) + self.theirs[chain][step].astype(f32)
        if not first:
            value = value + self.landed[chain][step - 1].astype(f32)
        self.mine[chain][step % 3] = value.astype(jnp.bfloat16)

    def begin(self, chains):
        for chain in chains:
            self.add(chain, 0, True)
            self.ring_copy(chain, 0).start()
        self.start_inputs(chains, 2)

    def middle(self, chains, step):
        for chain in chains:
            self.ring_copy(chain, step - 1).wait()

            @pl.when(step < RING - 2)
            def _():
                self.load(chain, step + 2).start()
                self.cross(chain, step + 2).start()

            self.add(chain, step)
            self.ring_copy(chain, step).start()

    def back_copy(self, chain, step, own=False):
        shard = self.shard_at(chain, RING - step)
        return remote(
            self.mine[chain].at[(RING - 1) % 3] if own else self.result_of(chain, shard),
            self.result_of(chain, shard),
            self.back_sems,
            (chain, step),
            self.targets[CHAINS[chain][0]],
        )

    def share(self, chain, step, own=False):
        shard = self.shard_at(chain, RING - step)
        return remote(
            self.mine[chain].at[(RING - 1) % 3] if own else self.result_of(chain, shard),
            self.result_of(chain, shard),
            self.share_sems,
            (chain, step),
            self.sibling,
        )

    def keep(self, chain):
        return pltpu.make_async_copy(
            self.mine[chain].at[(RING - 1) % 3],
            self.result_of(chain, self.spot),
            self.keep_sem.at[chain],
        )

    def publish(self, chain):
        self.back_copy(chain, 0, True).start()
        self.share(chain, 0, True).start()
        self.keep(chain).start()

    def trade(self, chain):
        return remote(
            self.mine[chain].at[(RING - 1) % 3],
            self.swapped[chain],
            self.swap_sems,
            (chain,),
            self.across,
        )

    def last(self, chains):
        for chain in chains:
            self.ring_copy(chain, RING - 2).wait()
            self.add(chain, RING - 1)
            if CHAINS[chain][3]:

                @pl.when(self.core == 1)
                def _():
                    self.trade(chain).start()

                @pl.when(self.core == 0)
                def _():
                    self.publish(chain)

            else:
                self.publish(chain)

    def traded(self, chains):
        for chain in chains:
            if CHAINS[chain][3]:

                @pl.when(self.core == 1)
                def _():
                    self.trade(chain).wait()
                    self.mine[chain][(RING - 1) % 3] = self.swapped[chain][...]
                    self.publish(chain)

    def back_begin(self, chains):
        for chain in chains:
            self.back_copy(chain, 0, True).wait()
            self.back_copy(chain, 1).start()
            self.share(chain, 1).start()

    def back_middle(self, chains, step):
        for chain in chains:
            self.back_copy(chain, step).wait()

            @pl.when(step < RING - 2)
            def _():
                self.back_copy(chain, step + 1).start()

            self.share(chain, step + 1).start()

    def end(self, chains):
        for chain in chains:
            self.keep(chain).wait()
            self.share(chain, 0, True).wait()

        def rest(step, unused):
            for chain in chains:
                self.share(chain, step).wait()
            return unused

        lax.fori_loop(1, RING, rest, 0)


def tail_kernel(
    gdown_ref,
    gup_ref,
    part_two_ref,
    hidden_ref,
    small_ref,
    cot_ref,
    w_out_ref,
    attn_ref,
    lse_ref,
    q_ref,
    k_ref,
    v_ref,
    kwin_ref,
    vwin_ref,
    qwin_ref,
    ids_ref,
    ln_ref,
    wk_ref,
    wv_ref,
    wq_ref,
    w_other_ref,
    x_ref,
    bias_up_ref,
    down_ref,
    sum_down,
    sum_out,
    sum_up,
    sum_query,
    sum_key,
    sum_value,
    vec_out_ref,
    grad_input_ref,
    output_ref,
    *refs,
):
    count = len(CHAINS)
    buffers = [refs[i * count : (i + 1) * count] for i in range(4)]
    (
        dowin,
        statwin,
        sent,
        came,
        grad_hidden,
        grad_mix,
        grad_heads,
        gout,
        gqkv,
        grad_three,
        w_own,
        w_other,
        first_buf,
        second_buf,
        grad_one,
        sums,
        sent_down,
        came_down,
        query_ids,
        key_ids,
        later_ids,
        vec_steps,
        vec_landed,
        block_sem,
        weight_sem,
        y_sems,
        do_sems,
        stat_sems,
        vec_sems,
        *ring_sems,
    ) = refs[4 * count :]
    f32, bf16 = jnp.float32, jnp.bfloat16
    side = lax.axis_index("grp")
    spot = spot_of(lax.axis_index("rep"))
    level, column, core = spot
    on_ring = jnp.where(column == 0, level, 7 - level)
    near_by = neighbours(side, spot)
    across, sibling, over = near_by[:3]
    ahead = ring_device(side, (on_ring + 1) % RING, core)
    behind = ring_device(side, (on_ring + RING - 1) % RING, core)
    near = device_at(side, level + 1 - 2 * (level % 2), column, core)
    far = device_at(side, (level + 2) % 4, column, core)
    vec_partners = (sibling, over, near, far)
    block = side + core - 2 * side * core
    half = w_own.shape[1]
    pairs = half // CHUNK
    own_cols = tile(half * side, half, 128)

    def source_of(chain, which, shard):
        if chain < 2:
            return gdown_ref.at[tile(320 * shard + 160 * chain, 160), tile(640 * which, 640, 128)]
        rows = tile(640 * which + 80 * shard, 80)
        if chain < 4:
            return gup_ref.at[rows, pl.ds(1280 * (chain - 2), 1280)]
        if chain < 7:
            return gqkv.at[rows, pl.ds(640 * (chain - 4), 640)]
        return gout.at[tile(80 * shard, 80), tile(640 * which, 640, 128)]

    def result_of(chain, shard):
        if chain < 2:
            return sum_down.at[tile(320 * shard + 160 * chain, 160), tile(640 * core, 640, 128)]
        rows = tile(80 * shard, 80)
        if chain < 4:
            return sum_up.at[rows, tile(2560 * block + 1280 * (chain - 2), 1280, 128)]
        if chain < 7:
            return (sum_query, sum_key, sum_value)[chain - 4].at[rows, tile(640 * block, 640, 128)]
        return sum_out.at[rows, tile(640 * core, 640, 128)]

    rings = Rings(
        side,
        on_ring,
        core,
        (sibling, across, ahead, behind),
        source_of,
        result_of,
        buffers,
        ring_sems,
    )
    stats = Stream(
        side, spot, True, lambda slot: statwin.at[:, tile(CHUNK * slot, CHUNK, CHUNK)], stat_sems
    )
    grads = Stream(side, spot, True, rows_of(dowin), do_sems)
    streams = (stats, grads)
    own_slot = pl.ds((SLOTS - 1) * CHUNK, CHUNK)
    upper, lower = pl.ds(0, CHUNK), pl.ds(CHUNK, CHUNK)

    def exchange(which):
        return (
            remote(sent.at[lower], came.at[which, upper], y_sems, (which, 0), across),
            remote(sent.at[upper], came.at[which, lower], y_sems, (which, 1), across),
        )

    down_copy = remote(sent_down, came_down, y_sems, (2, 0), across)
    dowin[...] = jnp.zeros_like(dowin)
    statwin[...] = jnp.zeros_like(statwin)
    sent[...] = part_two_ref[...].astype(bf16)
    greet(near_by + far_corners(side, spot) + (far, ahead, behind))
    rings.start_inputs(EARLY, 0)
    for copy in exchange(0):
        copy.start()
    rings.start_inputs(EARLY, 1)
    weights = (wq_ref, wk_ref, wv_ref)
    weight_loads = [
        pltpu.make_async_copy(weights[m].at[:, own_cols], w_own.at[m], weight_sem.at[m])
        for m in range(3)
    ] + [
        pltpu.make_async_copy(w_other_ref.at[(m + 2) % 3], w_other.at[m], weight_sem.at[3 + m])
        for m in range(3)
    ]
    for copy in weight_loads:
        copy.start()
    rings.begin(EARLY)
    sent_down[...] = down_ref[CHUNK:, :].astype(bf16)
    down_copy.start()

    for row in range(2):
        line = slice(row, row + 1)
        first = REACH * CHUNK
        own = ids_ref[line, tile(first + CHUNK * lax.axis_index("rep"), CHUNK, CHUNK)].astype(f32)
        query_ids[row] = jnp.broadcast_to(own, (CHUNK, CHUNK)).T
        key_ids[row] = ids_ref[line, tile(CHUNK * lax.axis_index("rep"), WINDOW, CHUNK)].astype(f32)
        for k in range(REACH + 1):
            at = tile(first + CHUNK * (lax.axis_index("rep") + k), CHUNK, CHUNK)
            later_ids[row, :, (REACH - k) * CHUNK : (REACH + 1 - k) * CHUNK] = ids_ref[
                line, at
            ].astype(f32)

    def back_through_norm(which, part_ref, input_ref, gain_line, base, finish):
        zero = jnp.zeros((8, part_ref.shape[1]), f32)

        def some_rows(i, carry):
            rows = tile(32 * i, 32, 32)
            grad = part_ref[rows, :] + came[which, rows, :].astype(f32)
            inputs = input_ref[rows, :].astype(f32)
            center = inputs - jnp.mean(inputs, axis=-1, keepdims=True)
            inverse = lax.rsqrt(jnp.mean(center * center, axis=-1, keepdims=True) + EPSILON)
            normed = center * inverse
            scaled = grad * small_ref[gain_line : gain_line + 1, :].astype(f32)
            value = inverse * (
                scaled
                - jnp.mean(scaled, axis=-1, keepdims=True)
                - normed * jnp.mean(scaled * normed, axis=-1, keepdims=True)
            )
            extra = finish(rows, value)
            parts = [grad * normed, grad] + extra
            return tuple(
                c + jnp.sum(p.reshape(4, 8, -1), axis=0) for c, p in zip(carry, parts)
            )

        totals = lax.fori_loop(0, 8, some_rows, (zero,) * (3 if base == 0 else 2))
        for k, total in enumerate(totals):
            sums[base + k : base + k + 1, :] = jnp.sum(total, axis=0, keepdims=True)

    def finish_two(rows, value):
        hidden = cot_ref[rows, :].astype(f32) + value
        low = hidden.astype(bf16)
        grad_hidden[rows, :] = hidden
        grad_mix[rows, :] = low
        return [low.astype(f32)]

    rings.middle(EARLY, 1)
    for copy in exchange(0):
        copy.wait()
    back_through_norm(0, part_two_ref, hidden_ref, 4, 0, finish_two)
    grad_heads[...] = matmul_nt(grad_mix[...], w_out_ref[...]).astype(bf16)

    def own_stats(i, unused):
        row, pair = i // pairs, i % pairs
        rows, lanes = tile(CHUNK * row, CHUNK, CHUNK), tile(CHUNK * pair, CHUNK, CHUNK)
        weighed = (grad_heads[rows, lanes].astype(f32) * attn_ref[rows, lanes]).T
        level_of = lse_ref[rows, lanes].T
        zero = jnp.zeros((4, CHUNK), f32)
        statwin[tile(8 * i, 8, 8), own_slot] = jnp.concatenate(
            [
                level_of[:1],
                level_of[HALF_LANES : HALF_LANES + 1],
                jnp.sum(weighed[:HALF_LANES], axis=0, keepdims=True),
                jnp.sum(weighed[HALF_LANES:], axis=0, keepdims=True),
                zero,
            ],
            axis=0,
        )
        return unused

    lax.fori_loop(0, 2 * pairs, own_stats, 0)
    dowin[0, own_slot, :] = grad_heads[:CHUNK, :]
    dowin[1, own_slot, :] = grad_heads[CHUNK:, :]
    for stream in streams:
        stream.start_own()

    window = pl.ds((SLOTS - 1 - REACH) * CHUNK, WINDOW)

    def block_loads(refs_bufs, i):
        row, pair = i // pairs, i % pairs
        lanes = tile(CHUNK * pair, CHUNK, CHUNK)
        return [
            pltpu.make_async_copy(
                ref.at[row, window, lanes], buf.at[i % 2], block_sem.at[k, i % 2]
            )
            for k, (ref, buf) in enumerate(refs_bufs)
        ]

    kv_blocks = ((kwin_ref, first_buf), (vwin_ref, second_buf))
    q_blocks = ((qwin_ref, first_buf),)

    def start_blocks(refs_bufs, i):
        for copy in block_loads(refs_bufs, i):
            copy.start()

    def use_blocks(refs_bufs, i):
        for copy in block_loads(refs_bufs, i):
            copy.wait()
        pl.when(i + 1 < 2 * pairs)(lambda: start_blocks(refs_bufs, i + 1))

    scale = HEAD_DIM**-0.5
    start_blocks(kv_blocks, 0)
    attn_low = attn_ref[...].astype(bf16)
    gout[...] = matmul_tn(attn_low, grad_mix[...]).astype(bf16)

    def query_unit(i, unused):
        row, pair = i // pairs, i % pairs
        rows, lanes = tile(CHUNK * row, CHUNK, CHUNK), tile(CHUNK * pair, CHUNK, CHUNK)
        use_blocks(kv_blocks, i)
        query = q_ref[rows, lanes] * jnp.bfloat16(scale)
        keys, values = first_buf[i % 2], second_buf[i % 2]
        grad = grad_heads[rows, lanes]
        allowed = (query_ids[row][:, :1] == key_ids[row]) & (
            iota((CHUNK, WINDOW), 1) <= iota((CHUNK, WINDOW), 0) + REACH * CHUNK
        )
        weighed = grad.astype(f32) * attn_ref[rows, lanes]
        lse_pair = lse_ref[rows, lanes]
        parts = []
        for which in range(2):
            lse = lse_pair[:, which * HALF_LANES : which * HALF_LANES + 1]
            delta = jnp.sum(head_half(weighed, which), axis=-1, keepdims=True)
            scores = jnp.where(allowed, matmul_nt(head_half(query, which), keys), NEGATIVE)
            probs = jnp.exp(scores - lse)
            grad_probs = matmul_nt(head_half(grad, which), values)
            grad_scores = (probs * (grad_probs - delta)).astype(bf16)
            parts.append(matmul(grad_scores, keys))
        grad_three[0, rows, lanes] = (join_halves(*parts) * scale).astype(bf16)
        events = {
            1: (lambda s: s.after_up(0),),
            5: (lambda s: s.after_over(0), lambda s: s.after_up(1)),
            9: (lambda s: s.after_over(1),),
        }
        for at, what in events.items():

            @pl.when(i == at)
            def _():
                rings.middle(EARLY, 2 + at // 4)
                for event in what:
                    for stream in streams:
                        event(stream)

        return unused

    lax.fori_loop(0, 2 * pairs, query_unit, 0)
    start_blocks(q_blocks, 0)
    rings.middle(EARLY, 5)
    for stream in streams:
        stream.after_over(2)
    for stream in streams:
        stream.after_twins()

    def key_unit(i, unused):
        row, pair = i // pairs, i % pairs
        rows, lanes = tile(CHUNK * row, CHUNK, CHUNK), tile(CHUNK * pair, CHUNK, CHUNK)
        use_blocks(q_blocks, i)
        keys = k_ref[rows, lanes] * jnp.bfloat16(scale)
        values = v_ref[rows, lanes]
        queries = first_buf[i % 2]
        after = dowin[row, window, lanes]
        lane = iota((CHUNK, WINDOW), 1)
        ahead_by = (REACH - lane // CHUNK) * CHUNK + lane % CHUNK
        allowed = (query_ids[row][:, :1] == later_ids[row]) & (ahead_by >= iota((CHUNK, WINDOW), 0))
        lines = statwin[tile(8 * i, 8, 8), window]
        key_parts, value_parts = [], []
        for which in range(2):
            lse, delta = lines[which : which + 1], lines[2 + which : 3 + which]
            scores = jnp.where(allowed, matmul_nt(head_half(keys, which), queries), NEGATIVE)
            probs = jnp.exp(scores - lse)
            value_parts.append(matmul(probs.astype(bf16), after))
            grad_probs = matmul_nt(head_half(values, which), after)
            grad_scores = (probs * (grad_probs - delta)).astype(bf16)
            key_parts.append(matmul(grad_scores, queries))
        grad_three[1, rows, lanes] = (join_halves(*key_parts) * scale).astype(bf16)
        grad_three[2, rows, lanes] = join_halves(*value_parts).astype(bf16)
        pl.when(i == 3)(lambda: rings.middle(EARLY, 6))
        pl.when(i == 8)(lambda: rings.last(EARLY))
        return unused

    lax.fori_loop(0, 2 * pairs, key_unit, 0)
    rings.traded(EARLY)
    for stream in streams:
        stream.finish()

    for copy in weight_loads:
        copy.wait()
    rings.back_begin(EARLY)
    for m in range(3):

        def weight_rows(i, unused):
            lanes = tile(256 * i, 256, 256)
            gqkv[lanes, m * half : (m + 1) * half] = matmul_tn(
                ln_ref[:, lanes], grad_three[m]
            ).astype(bf16)
            return unused

        lax.fori_loop(0, 2 * half // 256, weight_rows, 0)
    rings.start_inputs(LATE, 0)
    rings.start_inputs(LATE, 1)
    rings.begin(LATE)

    own_part, other_part = 0.0, 0.0
    for m in range(3):
        own_part = own_part + matmul_nt(grad_three[m], w_own[m])
        other_part = other_part + matmul_nt(grad_three[m], w_other[m])
    grad_one[:, own_cols] = own_part
    grad_one[:, tile(half * (1 - side), half, 128)] = other_part
    sent[...] = grad_one[...].astype(bf16)
    for copy in exchange(1):
        copy.start()
    for k, m in ((0, 0), (1, 2)):
        sums[6 + k : 7 + k, :half] = jnp.sum(grad_three[m].astype(f32), axis=0, keepdims=True)

    def both_rings(step, unused):
        rings.back_middle(EARLY, step)
        rings.middle(LATE, step)
        return unused

    both_rings(jnp.int32(1), 0)
    for copy in exchange(1):
        copy.wait()

    def finish_one(rows, value):
        grad_hidden[rows, :] = grad_hidden[rows, :] + value
        return []

    back_through_norm(1, grad_one, x_ref, 2, 3, finish_one)
    grad_input_ref[...] = grad_hidden[:CHUNK, :]
    sums[5:6, :] = jnp.sum(cot_ref[...].astype(f32), axis=0, keepdims=True)
    vec_steps[0] = jnp.zeros(vec_steps.shape[1:], f32)
    for k in range(4):
        vec_steps[0, 3 + k : 4 + k, :] = bias_up_ref[:1, k * half : (k + 1) * half]
    for row, (line, cols) in {
        0: (6, pl.ds(0, half)),
        1: (7, pl.ds(0, half)),
        2: (2, own_cols),
        7: (5, own_cols),
        8: (3, own_cols),
        9: (4, own_cols),
        10: (0, own_cols),
        11: (1, own_cols),
    }.items():
        vec_steps[0, row : row + 1, :] = sums[line : line + 1, cols]
    vec_copy = [
        remote(vec_steps.at[k], vec_landed.at[k], vec_sems, (k,), vec_partners[k])
        for k in range(4)
    ]
    vec_copy[0].start()
    for k in range(4):
        both_rings(jnp.int32(2 + k), 0)
        vec_copy[k].wait()
        vec_steps[k + 1] = vec_steps[k] + vec_landed[k]
        if k < 3:
            vec_copy[k + 1].start()
    vec_out_ref[...] = vec_steps[4]
    both_rings(jnp.int32(6), 0)
    rings.last(LATE)
    rings.end(EARLY)
    down_copy.wait()
    output_ref[...] = (
        hidden_ref[:CHUNK, :]
        + down_ref[:CHUNK, :]
        + came_down[...].astype(f32)
        + small_ref[1:2, :].astype(f32)
    ).astype(bf16)
    rings.traded(LATE)
    rings.back_begin(LATE)

    def late_back(step, unused):
        rings.back_middle(LATE, step)
        return unused

    lax.fori_loop(1, RING - 1, late_back, 0)
    rings.end(LATE)


def tail(operands, width, half, ff, number):
    dma = pltpu.SemaphoreType.DMA
    f32, bf16 = jnp.float32, jnp.bfloat16
    count = len(CHAINS)
    rows = operands[3].shape[0]
    hbm, vmem = pl.BlockSpec(memory_space=pl.ANY), pl.BlockSpec(memory_space=pltpu.VMEM)
    in_hbm = (0, 1, 12, 13, 14, 17, 18, 19, 20)
    square = jax.ShapeDtypeStruct((half, width), bf16)

    def room(depth):
        return [pltpu.VMEM(depth + (tall, wide), bf16) for _, tall, wide, _ in CHAINS]

    return pl.pallas_call(
        tail_kernel,
        out_shape=[
            jax.ShapeDtypeStruct((ff, width), bf16),
            square,
            jax.ShapeDtypeStruct((half, 2 * ff), bf16),
            square,
            square,
            square,
            jax.ShapeDtypeStruct((VEC_ROWS, half), f32),
            jax.ShapeDtypeStruct((CHUNK, width), f32),
            jax.ShapeDtypeStruct((CHUNK, width), bf16),
        ],
        in_specs=[hbm if i in in_hbm else vmem for i in range(len(operands))],
        out_specs=[hbm] * 6 + [vmem] * 3,
        scratch_shapes=[
            *room((3,)),
            *room((RING,)),
            *room((RING - 1,)),
            *room(()),
            pltpu.VMEM((2, SLOTS * CHUNK, half), bf16),
            pltpu.VMEM((16 * half // CHUNK, SLOTS * CHUNK), f32),
            pltpu.VMEM((rows, width), bf16),
            pltpu.VMEM((2, rows, width), bf16),
            pltpu.VMEM((rows, width), f32),
            pltpu.VMEM((rows, width), bf16),
            pltpu.VMEM((rows, half), bf16),
            pltpu.VMEM((half, width), bf16),
            pltpu.VMEM((width, 3 * half), bf16),
            pltpu.VMEM((3, rows, half), bf16),
            pltpu.VMEM((3, half, half), bf16),
            pltpu.VMEM((3, half, half), bf16),
            pltpu.VMEM((2, WINDOW, CHUNK), bf16),
            pltpu.VMEM((2, WINDOW, CHUNK), bf16),
            pltpu.VMEM((rows, width), f32),
            pltpu.VMEM((8, width), f32),
            pltpu.VMEM((CHUNK, width), bf16),
            pltpu.VMEM((CHUNK, width), bf16),
            pltpu.VMEM((2, CHUNK, CHUNK), f32),
            pltpu.VMEM((2, 1, WINDOW), f32),
            pltpu.VMEM((2, 1, WINDOW), f32),
            pltpu.VMEM((5, VEC_ROWS, half), f32),
            pltpu.VMEM((4, VEC_ROWS, half), f32),
            dma((2, 2)),
            dma((6,)),
            dma((2, 3, 2)),
            dma((2, 12)),
            dma((2, 12)),
            dma((2, 4)),
            dma((count, 3)),
            dma((2, count, RING)),
            dma((2, count, RING - 1)),
            dma((2, count, RING - 1)),
            dma((2, count, RING)),
            dma((2, count)),
            dma((count,)),
        ],
        compiler_params=pltpu.CompilerParams(
            collective_id=number, has_side_effects=True, vmem_limit_bytes=60 * 2**20
        ),
    )(*operands)


FF_BLOCK = 512


def ff_kernel(
    side_ref,
    tok_ref,
    tok_other_ref,
    mixed_ref,
    small_ref,
    cot_ref,
    cot_other_ref,
    up_own_ref,
    up_other_ref,
    down_ref,
    bias_ref,
    hidden_ref,
    x_ref,
    cot_all_ref,
    result_ref,
    back_ref,
    grad_up_ref,
    grad_down_ref,
    grad_bias_ref,
    ln_ref,
    own_first,
):
    f32, bf16 = jnp.float32, jnp.bfloat16
    side = side_ref[0]
    step = pl.program_id(0)
    chunk, width = tok_ref.shape
    half = width // 2
    own_cols, other_cols = tile(half * side, half, 128), tile(half * (1 - side), half, 128)

    @pl.when(step == 0)
    def _():
        x_ref[:chunk, :] = tok_ref[...]
        x_ref[chunk:, :] = tok_other_ref[...]
        cot_all_ref[:chunk, :] = cot_ref[...]
        cot_all_ref[chunk:, :] = cot_other_ref[...]

        def some_rows(i, unused):
            rows = tile(64 * i, 64, 64)
            hidden = x_ref[rows, :].astype(f32) + mixed_ref[rows, :] + small_ref[:1, :].astype(f32)
            hidden_ref[rows, :] = hidden
            normed, _ = norm_rows(hidden)
            ln_ref[rows, :] = (
                normed * small_ref[4:5, :].astype(f32) + small_ref[5:6, :].astype(f32)
            ).astype(bf16)
            return unused

        lax.fori_loop(0, 2 * chunk // 64, some_rows, 0)
        own_first[:, :half] = ln_ref[:, own_cols]
        own_first[:, half:] = ln_ref[:, other_cols]
        result_ref[...] = jnp.zeros_like(result_ref)
        back_ref[...] = jnp.zeros_like(back_ref)

    pre_act = (
        matmul(own_first[:, :half], up_own_ref[...])
        + matmul(own_first[:, half:], up_other_ref[...])
        + bias_ref[...].astype(f32)
    )
    value, slope = gelu_pair(pre_act)
    act = value.astype(bf16)
    cot = cot_all_ref[...]
    result_ref[...] += matmul(act, down_ref[...])
    grad_pre = (matmul_nt(cot, down_ref[...]) * slope).astype(bf16)
    grad_bias_ref[...] = jnp.sum(grad_pre.astype(f32), axis=0, keepdims=True)
    grad_down_ref[...] = matmul_tn(act, cot).astype(bf16)
    grad_up_ref[...] = matmul_tn(own_first[...], grad_pre).astype(bf16)
    back_ref[:, own_cols] += matmul_nt(grad_pre, up_own_ref[...])
    back_ref[:, other_cols] += matmul_nt(grad_pre, up_other_ref[...])


def feed_forward(side, tokens, tok_other, mixed, small, cotangent, cot_other, w_up, up_other, w_down, b_up):
    f32, bf16 = jnp.float32, jnp.bfloat16
    chunk, width = tokens.shape
    half = width // 2
    ff = w_down.shape[0]
    steps = ff // FF_BLOCK

    def whole(shape):
        return pl.BlockSpec(shape, lambda j, s: (0, 0))

    rows = 2 * chunk
    columns = pl.BlockSpec((half, FF_BLOCK), lambda j, s: (0, j))
    return pl.pallas_call(
        ff_kernel,
        grid_spec=pltpu.PrefetchScalarGridSpec(
            num_scalar_prefetch=1,
            grid=(steps,),
            in_specs=[
                whole((chunk, width)),
                whole((chunk, width)),
                whole((rows, width)),
                whole(small.shape),
                whole((chunk, width)),
                whole((chunk, width)),
                pl.BlockSpec((half, FF_BLOCK), lambda j, s: (0, s[0] * steps + j)),
                columns,
                pl.BlockSpec((FF_BLOCK, width), lambda j, s: (j, 0)),
                pl.BlockSpec((1, FF_BLOCK), lambda j, s: (0, j)),
            ],
            out_specs=[
                whole((rows, width)),
                whole((rows, width)),
                whole((rows, width)),
                whole((rows, width)),
                whole((rows, width)),
                pl.BlockSpec((width, FF_BLOCK), lambda j, s: (0, j)),
                pl.BlockSpec((FF_BLOCK, width), lambda j, s: (j, 0)),
                pl.BlockSpec((1, FF_BLOCK), lambda j, s: (0, j)),
            ],
            scratch_shapes=[
                pltpu.VMEM((rows, width), bf16),
                pltpu.VMEM((rows, width), bf16),
            ],
        ),
        out_shape=[
            jax.ShapeDtypeStruct((rows, width), f32),
            jax.ShapeDtypeStruct((rows, width), bf16),
            jax.ShapeDtypeStruct((rows, width), bf16),
            jax.ShapeDtypeStruct((rows, width), f32),
            jax.ShapeDtypeStruct((rows, width), f32),
            jax.ShapeDtypeStruct((width, ff), bf16),
            jax.ShapeDtypeStruct((ff, width), bf16),
            jax.ShapeDtypeStruct((1, ff), f32),
        ],
        compiler_params=pltpu.CompilerParams(vmem_limit_bytes=56 * 2**20),
    )(
        side.reshape(1).astype(jnp.int32),
        tokens,
        tok_other,
        mixed,
        small,
        cotangent,
        cot_other,
        w_up,
        up_other,
        w_down,
        b_up.reshape(1, -1),
    )


def widen_kernel(*refs):
    count = len(refs) // 2
    for source, target in zip(refs[:count], refs[count:]):
        target[...] = source[...].astype(jnp.float32)


def widen(arrays):
    steps = 4
    specs = [
        pl.BlockSpec((a.shape[0] // steps, a.shape[1]), lambda j: (j, 0)) for a in arrays
    ]
    return pl.pallas_call(
        widen_kernel,
        grid=(steps,),
        in_specs=specs,
        out_specs=specs,
        out_shape=[jax.ShapeDtypeStruct(a.shape, jnp.float32) for a in arrays],
        compiler_params=pltpu.CompilerParams(vmem_limit_bytes=56 * 2**20),
    )(*arrays)


def pair_shards(
    tokens,
    doc_ids,
    w_query,
    w_key,
    w_value,
    w_out,
    w_up,
    w_down,
    b_query,
    b_value,
    b_out,
    b_up,
    b_down,
    attn_gain,
    attn_beta,
    ffn_gain,
    ffn_beta,
    cotangent,
):
    f32, bf16 = jnp.float32, jnp.bfloat16
    chunk, width = tokens.shape
    half = width // 2
    side = lax.axis_index("grp")
    row_of_small = lax.broadcasted_iota(jnp.int32, (16, half), 0)
    small = jnp.zeros((16, half), bf16)
    for line, vector in enumerate(
        (b_out, b_down, attn_gain, attn_beta, ffn_gain, ffn_beta, b_query, b_value)
    ):
        small = jnp.where(row_of_small == line, vector[None, :], small)
    (
        k_win,
        v_win,
        q_win,
        k_own,
        v_own,
        q_own,
        ln_one,
        tok_other,
        cot_other,
        ids_other,
        small,
        w_other,
        w_up_other,
        attn,
        lse,
        mixed,
        ids,
    ) = front(tokens, cotangent, doc_ids, small, w_key, w_value, w_query, w_up, w_out, 2)
    hidden, x_all, cot_all, down, back_two, grad_w_up, grad_w_down, grad_b_up = feed_forward(
        side, tokens, tok_other, mixed, small, cotangent, cot_other, w_up, w_up_other, w_down, b_up
    )
    *sums, vec_sum, grad_input, output = tail(
        (
            grad_w_down,
            grad_w_up,
            back_two,
            hidden,
            small,
            cot_all,
            w_out,
            attn,
            lse,
            q_own,
            k_own,
            v_own,
            k_win,
            v_win,
            q_win,
            ids,
            ln_one,
            w_key,
            w_value,
            w_query,
            w_other,
            x_all,
            grad_b_up,
            down,
        ),
        width,
        half,
        w_down.shape[0],
        1,
    )
    sum_down, sum_out, sum_up, sum_query, sum_key, sum_value = widen(sums)
    cuts = [
        vec_sum[at : at + size].reshape(-1)
        for at, size in ((0, 1), (1, 1), (2, 1), (3, 4), (7, 1), (8, 1), (9, 1), (10, 1), (11, 1))
    ]
    return (
        output,
        grad_input,
        sum_query,
        sum_key,
        sum_value,
        sum_out,
        sum_up,
        sum_down,
        *cuts,
    )


def solution(mesh):
    in_specs = (
        P(("grp", "rep"), None),
        P("grp", None),
        P("grp", None),
        P("grp", None),
        P("grp", None),
        P("grp", None),
        P("grp", None),
        P("grp", None),
        P("grp"),
        P("grp"),
        P("grp"),
        P("grp"),
        P("grp"),
        P("grp"),
        P("grp"),
        P("grp"),
        P("grp"),
        P(("grp", "rep"), None),
    )
    out_specs = (
        P(("grp", "rep"), None),
        P(("grp", "rep"), None),
        P("grp", None),
        P("grp", None),
        P("grp", None),
        P("grp", None),
        P("grp", None),
        P("grp", None),
        P("grp"),
        P("grp"),
        P("grp"),
        P("grp"),
        P("grp"),
        P("grp"),
        P("grp"),
        P("grp"),
        P("grp"),
    )
    plan = pair_shards if fits_pair(mesh) else shards
    return jax.shard_map(plan, mesh=mesh, in_specs=in_specs, out_specs=out_specs, check_vma=False)
```
